32 devices in a mesh: energy: 16 (over z, y, x), slab: 2 (over core).
Axes of the slice: x: 2, y: 2, z: 4, core: 2. Of those that a mesh axis runs over, the one named last changes fastest.
Arguments:
- lesser_free: float32 [32, 144, 256], P('energy', None, 'slab'), may hold values from -6 to 6
- greater_free: float32 [32, 144, 256], P('energy', None, 'slab'), may hold values from -6 to 6
- retarded: float32 [32, 144, 256], P('energy', None, 'slab'), may hold values from -1.75 to 1.75
- coupling: float32 [12, 144, 256], P(None, None, 'slab'), may hold values from -0.875 to 0.875
- neighbour_offsets: int32 [12, 256], P(None, 'slab'), may hold values from -32 to 32, as said below
- phonon_shift: int32 [64], replicated, may hold values from 1 to 16, as said below
- phonon_coupling: float32 [64], replicated, may hold values from 0.01 to 0.1
- phonon_occupation: float32 [64], replicated, may hold values from 0.05 to 5
Outputs:
- green_lesser: float32 [32, 144, 256], P('energy', None, 'slab')
- green_greater: float32 [32, 144, 256], P('energy', None, 'slab')
The draws below stay inside these ranges and needn't reach their ends.
Inputs may be any that keep to these rules, and one draw needn't show every extreme that they name: `neighbour_offsets`: each atom's 12 offsets are distinct and nonzero. `phonon_shift`: several frequencies may share a shift.
All inputs are finite; a program needn't handle non-finite values.
Results may differ from the reference program's by a relative error of at most 0.0003.
Values sent between devices are 32-bit elements; how exact they have to be, the bound alone decides.
No kernel may reach another device: no remote copies, remote signals or barrier semaphores. Data moves between devices by JAX's collectives and lax.ppermute only.
A program may use at most 64 MiB of HBM per device.

```python
import math
import jax
import jax.numpy as jnp
from jax import lax

NORB = 12
NB = 12
NW = 64
SMAX = 16
HW = 32
ITERS = 2
NE = 32
ATOMS = 256


def draw_neighbour_offsets(key, part):
    count = 2 * HW
    slots = jnp.arange(count, dtype=jnp.int32)
    candidates = jnp.where(slots < HW, slots - HW, slots - HW + 1)
    scores = jax.random.randint(key, (ATOMS, count), 0, 1 << 20, dtype=jnp.int32) * count + slots[None, :]
    atoms = jnp.arange(ATOMS, dtype=jnp.int32)
    boost = ((atoms[:, None] == 0) & ((slots[None, :] == 0) | (slots[None, :] == count - 1))).astype(jnp.int32) * (1 << 28)
    selected_pick = lax.top_k(scores + boost, NB)[1]
    return jnp.take(candidates, selected_pick).T.astype(jnp.int32)


def draw_phonon_shift(key, part):
    shifts = jax.random.randint(key, (NW,), 1, SMAX + 1, dtype=jnp.int32)
    first = jax.random.randint(jax.random.fold_in(key, 11), (), 0, NW, dtype=jnp.int32)
    second = (first + 1 + jax.random.randint(jax.random.fold_in(key, 12), (), 0, NW - 1, dtype=jnp.int32)) % NW
    slots = jnp.arange(NW, dtype=jnp.int32)
    shifts = jnp.where(slots == first, SMAX, shifts)
    return jnp.where(slots == second, 1, shifts).astype(jnp.int32)


def level_of(stream_key, dims, split, least, high):
    loudness, own = 1.0, jax.random.fold_in(stream_key, 6)
    for axis_at, shards_of in split:
        heights = jnp.exp(jax.random.uniform(jax.random.fold_in(own, axis_at), (shards_of,), jnp.float32, least / len(split), high / len(split)))
        loudness = loudness * jnp.repeat(heights, dims[axis_at] // shards_of).reshape([-1 if axis == axis_at else 1 for axis in range(len(dims))])
    return loudness


def centred(rng, dims, deviation, limit, split=(), kind=jnp.bfloat16):
    gain = level_of(rng, dims, split, -0.22, 0.18) if split else 1.0
    result = jax.random.normal(rng, dims, jnp.float32) * deviation * gain
    return jnp.minimum(jnp.maximum(result, -limit), limit).astype(kind)


def setup_inputs(seed: int = 0) -> dict:
    key_list = jax.random.split(jax.random.key(seed), 9)
    return {
        "lesser_free": centred(key_list[0], (NE, NORB * NORB, ATOMS), 1.0, 6.0, ((0, 16), (2, 2)), jnp.float32),
        "greater_free": centred(key_list[1], (NE, NORB * NORB, ATOMS), 1.0, 6.0, ((0, 16), (2, 2)), jnp.float32),
        "retarded": centred(key_list[2], (NE, NORB * NORB, ATOMS), NORB ** -0.5, 1.75, ((0, 16), (2, 2)), jnp.float32),
        "coupling": centred(key_list[3], (NB, NORB * NORB, ATOMS), (NORB * 4) ** -0.5, 0.875, ((2, 2),), jnp.float32),
        "neighbour_offsets": draw_neighbour_offsets(jax.random.fold_in(key_list[8], 71), 0),
        "phonon_shift": draw_phonon_shift(jax.random.fold_in(key_list[8], 71), 0),
        "phonon_coupling": jnp.clip(jnp.exp(jax.random.uniform(key_list[6], (NW,), jnp.float32, math.log(0.01), math.log(0.1))), 0.01, 0.1),
        "phonon_occupation": jnp.clip(jnp.exp(jax.random.uniform(key_list[7], (NW,), jnp.float32, math.log(0.05), math.log(5.0))), 0.05, 5.0),
    }


TOP_RANK = lax.Precision.HIGHEST


def mixing(upper_weight, downward_weight, shifts):
    places = jnp.arange(NE, dtype=jnp.int32)
    spacing = places[None, :] - places[:, None]

    def add_mode(kernel, mode):
        upper, lower, shift = mode
        kernel = kernel + upper * (spacing == shift).astype(jnp.float32) + lower * (spacing == -shift).astype(jnp.float32)
        return kernel, None

    kernel, _ = lax.scan(add_mode, jnp.zeros((NE, NE), jnp.float32), (upper_weight, downward_weight, shifts))
    return kernel


def couple(green, links, energy_displacements):
    padded = jnp.pad(green, ((0, 0), (0, 0), (0, 0), (HW, HW)))
    atoms = jnp.arange(ATOMS, dtype=jnp.int32)

    def add_neighbour(total, neighbour):
        link, offset = neighbour
        near = jnp.take(padded, atoms + offset + HW, axis=3)
        inner = jnp.einsum('ija,ejla->eila', link, near, precision=TOP_RANK)
        return total + jnp.einsum('eila,kla->eika', inner, link, precision=TOP_RANK), None

    total, _ = lax.scan(add_neighbour, jnp.zeros(green.shape, jnp.float32), (links, energy_displacements))
    return total


def dress(retarded_blocks, sigma):
    inner = jnp.einsum('eija,ejla->eila', retarded_blocks, sigma, precision=TOP_RANK)
    return jnp.einsum('eila,ekla->eika', inner, retarded_blocks, precision=TOP_RANK)


def reference(lesser_free, greater_free, retarded, coupling, neighbour_offsets, phonon_shift, phonon_coupling, phonon_occupation):
    blocks = (NE, NORB, NORB, ATOMS)
    emit = phonon_coupling * (phonon_occupation + 1.0)
    absorb = phonon_coupling * phonon_occupation
    kernel_stack = (mixing(emit, absorb, phonon_shift), mixing(absorb, emit, phonon_shift))
    frees = (lesser_free.reshape(blocks), greater_free.reshape(blocks))
    retarded_blocks = retarded.reshape(blocks)
    links = coupling.reshape(NB, NORB, NORB, ATOMS)
    greens = frees
    for step in range(ITERS):
        updated = []
        for kernel, free, green in zip(kernel_stack, frees, greens):
            coupled = couple(green, links, neighbour_offsets)
            sigma = jnp.dot(kernel, coupled.reshape(NE, -1), precision=TOP_RANK).reshape(blocks)
            updated.append(free + dress(retarded_blocks, sigma))
        greens = tuple(updated)
    target = (NE, NORB * NORB, ATOMS)
    return greens[0].reshape(target), greens[1].reshape(target)
```

```python
import jax
import jax.numpy as jnp
from jax import lax
from jax.sharding import PartitionSpec as P

NORB = 12
NB = 12
HW = 32
ITERS = 2


TOP_RANK = lax.Precision.HIGHEST


def padded_2(block, sides, width):
    for axis, dim in sides:
        count = lax.axis_size(axis)
        forward = [(i, i + 1) for i in range(count - 1)]
        backward = [(target, source) for source, target in forward]
        low = lax.ppermute(
            lax.slice_in_dim(block, block.shape[dim] - width, None, axis=dim), axis, forward
        )
        high = lax.ppermute(lax.slice_in_dim(block, 0, width, axis=dim), axis, backward)
        block = jnp.concatenate([low, block, high], axis=dim)
    return block


def banded(upper_weight, downward_weight, shifts, rows, column_entries, lead):
    length = rows + column_entries - 1
    spacing = jnp.arange(length, dtype=jnp.int32) - (rows - 1) - lead
    hits_upper = (spacing[None, :] == shifts[:, None]).astype(jnp.float32)
    hits_lower = (spacing[None, :] == -shifts[:, None]).astype(jnp.float32)
    coeffs = jnp.dot(upper_weight, hits_upper, precision=TOP_RANK) + jnp.dot(
        downward_weight, hits_lower, precision=TOP_RANK
    )
    tiled = jnp.concatenate([jnp.tile(coeffs, rows), jnp.zeros((rows,), jnp.float32)])
    hankel = tiled.reshape(rows, rows + column_entries)[:, :column_entries]
    return hankel[::-1]


def block_sandwich(left, middle):
    inner = 0.0
    for inner_index in range(left.shape[-2]):
        inner = inner + left[..., :, inner_index, None, :] * middle[..., None, inner_index, :, :]
    outer = 0.0
    for outer_index in range(left.shape[-2]):
        outer = outer + inner[..., :, None, outer_index, :] * left[..., None, :, outer_index, :]
    return outer


def couple(green, links, energy_displacements):
    atoms = green.shape[-1]
    padded = padded_2(green, (("slab", 4),), HW)
    wide = padded.shape[-1]
    padded_rows = padded.reshape(-1, wide)
    positions = jnp.arange(atoms, dtype=jnp.int32)
    sources = jnp.arange(wide, dtype=jnp.int32)

    def add_neighbour(neighbour, total):
        targets = positions + energy_displacements[neighbour] + HW
        selector = (sources[:, None] == targets[None, :]).astype(jnp.float32)
        near = jnp.dot(padded_rows, selector, precision=TOP_RANK).reshape(green.shape)
        return total + block_sandwich(links[neighbour], near)

    return lax.fori_loop(0, NB, add_neighbour, jnp.zeros(green.shape, jnp.float32))


def spread(flat, kernel_stack):
    functions, energies, length = flat.shape
    parts = lax.axis_size("energy")
    share = length // parts
    pieces = flat.reshape(functions * energies, parts, share).swapaxes(0, 1)
    gathered = lax.all_to_all(pieces, "energy", 0, 0)
    gathered = gathered.reshape(parts, functions, energies, share)
    mixed = jnp.einsum(
        "wpeqf,qwfd->pwed",
        kernel_stack.reshape(functions, parts, energies, parts, energies),
        gathered,
        precision=TOP_RANK,
    )
    back = lax.all_to_all(mixed.reshape(parts, functions * energies, share), "energy", 0, 0)
    return back.swapaxes(0, 1).reshape(functions, energies, length)


def body(
    lesser_free,
    greater_free,
    retarded,
    coupling,
    neighbour_offsets,
    phonon_shift,
    phonon_coupling,
    phonon_occupation,
):
    energies, pairs, atoms = lesser_free.shape
    free = jnp.stack([lesser_free, greater_free]).reshape(2, energies, NORB, NORB, atoms)
    retarded_blocks = retarded.reshape(energies, NORB, NORB, atoms)
    links = coupling.reshape(NB, NORB, NORB, atoms)
    emit = phonon_coupling * (phonon_occupation + 1.0)
    absorb = phonon_coupling * phonon_occupation
    total = energies * lax.axis_size("energy")
    kernel_stack = jnp.stack(
        [
            banded(emit, absorb, phonon_shift, total, total, 0),
            banded(absorb, emit, phonon_shift, total, total, 0),
        ]
    )
    green = free
    for step in range(ITERS):
        coupled = couple(green, links, neighbour_offsets)
        sigma = spread(coupled.reshape(2, energies, pairs * atoms), kernel_stack)
        green = free + block_sandwich(
            retarded_blocks, sigma.reshape(2, energies, NORB, NORB, atoms)
        )
    result = green.reshape(2, energies, pairs, atoms)
    return (result[0], result[1])


def solution(mesh):
    placed = (
        P("energy", None, "slab"),
        P("energy", None, "slab"),
        P("energy", None, "slab"),
        P(None, None, "slab"),
        P(None, "slab"),
        P(),
        P(),
        P(),
    )
    return jax.shard_map(
        body,
        mesh=mesh,
        in_specs=placed,
        out_specs=(P("energy", None, "slab"), P("energy", None, "slab")),
        check_vma=False,
    )
```

```python
import functools

import jax
import jax.numpy as jnp
from jax import lax
from jax.experimental import pallas as pl
from jax.experimental.pallas import tpu as pltpu
from jax.sharding import PartitionSpec as P

NORB = 12
NB = 12
HW = 32
ITERS = 2
ROWS = 8
FUSED = 1

TOP_RANK = lax.Precision.HIGHEST
PARAMS = pltpu.CompilerParams(vmem_limit_bytes=24 * 1024 * 1024)


def tiles(count):
    return [(at, min(ROWS, count - at)) for at in range(0, count, ROWS)]


def spread_rows(target, base, row, source, first, count):
    for at, size in tiles(count):
        rows = pl.ds((base + at) * ROWS + row, size, stride=ROWS)
        target[rows, :] = source(first + at, size)


def prep_coupling_kernel(rows, coupling, inside, out):
    group = ROWS // rows
    pairs = coupling.shape[1]
    for n in range(NB):
        valid = inside[n : n + 1, :]
        for row in range(rows):
            spread_rows(
                out,
                (n // group) * pairs,
                (n % group) * rows + row,
                lambda at, size: coupling[n, at : at + size, :] * valid,
                0,
                pairs,
            )


def prep_dressing_kernel(rows, retarded, shifts, coupled, occupied, left, right, mixing):
    energies, pairs, _ = retarded.shape
    total = mixing.shape[1]
    share = pairs * rows // ROWS
    for row in range(ROWS):
        read = lambda at, size: retarded[row % energies, at : at + size, :]
        spread_rows(left, 0, row, read, row // rows * share, share)
        spread_rows(right, 0, row, read, 0, pairs)
    places = lax.broadcasted_iota(jnp.int32, (total, total), 0)
    gap = lax.broadcasted_iota(jnp.int32, (total, total), 1) - places

    def add_mode(mode, kernels):
        lesser, greater = kernels
        shift = shifts[mode]
        absorb = coupled[mode] * occupied[mode]
        emit = coupled[mode] * (occupied[mode] + 1.0)
        ahead = gap == shift
        behind = gap == -shift
        lesser = lesser + jnp.where(ahead, emit, 0.0) + jnp.where(behind, absorb, 0.0)
        greater = greater + jnp.where(ahead, absorb, 0.0) + jnp.where(behind, emit, 0.0)
        return lesser, greater

    empty = jnp.zeros((total, total), jnp.float32)
    lesser, greater = lax.fori_loop(0, shifts.shape[0], add_mode, (empty, empty))
    mixing[0] = lesser
    mixing[1] = greater


def couple_kernel(fused, *refs):
    near, far = refs[:fused], refs[fused : 2 * fused]
    lanes, is_near, links_hbm, out = refs[2 * fused : 2 * fused + 4]
    own, other, gathered_a, gathered_b, total, links, sems = refs[2 * fused + 4 :]
    energies, pairs, atoms = near[0].shape
    rows = fused * energies
    group = ROWS // rows
    groups = NB // group
    copies = [
        pltpu.make_async_copy(links_hbm.at[g], links.at[g], sems.at[g]) for g in range(groups)
    ]
    for copy in copies:
        copy.start()
    for row in range(ROWS):
        function, energy = row % rows // energies, row % energies
        for target, sources in ((own, near), (other, far)):
            source = sources[function]
            spread_rows(
                target, 0, row, lambda at, size: source[energy, at : at + size, :], 0, pairs
            )
    buffers = (gathered_a, gathered_b)

    def gather(g, first, count):
        target = buffers[g % 2]
        lane, mine = lanes[g], is_near[g] != 0
        for at in range(count):
            pair = first + at
            rows_at = pl.ds(pl.multiple_of(pair * ROWS, ROWS), ROWS)
            inner = jnp.take_along_axis(own[rows_at, :], lane, axis=1, mode="promise_in_bounds")
            outer = jnp.take_along_axis(other[rows_at, :], lane, axis=1, mode="promise_in_bounds")
            target[pair] = jnp.where(mine, inner, outer)

    blocked = 2
    steps = NORB // blocked
    chunk = pairs // steps
    lax.fori_loop(0, steps, lambda step, _: gather(0, step * chunk, chunk), None)
    for g in range(groups):
        copies[g].wait()
        source = buffers[g % 2]

        def block_row(step, _):
            first = step * blocked
            inner = [[None] * NORB for _ in range(blocked)]
            for j in range(NORB):
                left = [links[g, (first + b) * NORB + j] for b in range(blocked)]
                for l in range(NORB):
                    value = source[j * NORB + l]
                    for b in range(blocked):
                        term = left[b] * value
                        inner[b][l] = term if j == 0 else inner[b][l] + term
            for k in range(NORB):
                sums = [None] * blocked
                for l in range(NORB):
                    right = links[g, k * NORB + l]
                    for b in range(blocked):
                        term = inner[b][l] * right
                        sums[b] = term if l == 0 else sums[b] + term
                for b in range(blocked):
                    at = (first + b) * NORB + k
                    value = sums[b] if g == 0 else total[at] + sums[b]
                    if g < groups - 1:
                        total[at] = value
                    else:
                        width = ROWS // 2
                        while width >= rows:
                            value = value + pltpu.roll(value, width, 0)
                            width //= 2
                        out[at] = value[:rows]
            if g < groups - 1:
                gather(g + 1, step * chunk, chunk)

        lax.fori_loop(0, steps, block_row, None)
    for at in range(pairs, out.shape[0]):
        out[at] = jnp.zeros((rows, atoms), jnp.float32)


def mix_kernel(fused, mixing, blocks, out, before, after):
    parts, share, rows, atoms = blocks.shape
    energies = rows // fused
    for f in range(fused):
        some = slice(f * energies, (f + 1) * energies)
        for part in range(parts):
            for pair in range(share):
                before[part * energies : (part + 1) * energies, pair * atoms : (pair + 1) * atoms] = (
                    blocks[part, pair, some, :]
                )
        after[...] = jnp.dot(
            mixing[f], before[...], precision=TOP_RANK, preferred_element_type=jnp.float32
        )
        for part in range(parts):
            for pair in range(share):
                out[part, pair, some, :] = after[
                    part * energies : (part + 1) * energies, pair * atoms : (pair + 1) * atoms
                ]


def dress_kernel(fused, *refs):
    sigma, left, right = refs[:3]
    free, out = refs[3 : 3 + fused], refs[3 + fused : 3 + 2 * fused]
    copied, dressed = refs[3 + 2 * fused :]
    energies, pairs, atoms = free[0].shape
    rows = fused * energies
    parts = ROWS // rows
    share = pairs // parts
    for pair in range(pairs):
        value = sigma[pair]
        for part in range(parts):
            copied[pair, part * rows : (part + 1) * rows, :] = value
    for i in range(NORB // parts):
        inner = [None] * NORB
        for j in range(NORB):
            factor = left[i * NORB + j]
            for l in range(NORB):
                term = factor * copied[j * NORB + l]
                inner[l] = term if j == 0 else inner[l] + term
        for k in range(NORB):
            value = inner[0] * right[k * NORB]
            for l in range(1, NORB):
                value = value + inner[l] * right[k * NORB + l]
            at = (i * NORB + k) * ROWS
            dressed[at : at + ROWS, :] = value
    for row in range(ROWS):
        function, energy, part = row % rows // energies, row % energies, row // rows
        for at, size in tiles(share):
            first = part * share + at
            piece = dressed[pl.ds(at * ROWS + row, size, stride=ROWS), :]
            out[function][energy, first : first + size, :] = (
                free[function][energy, first : first + size, :] + piece
            )


def call(kernel, outs, scratch, flops, *operands, spaces=None):
    shapes = [jax.ShapeDtypeStruct(dims, jnp.float32) for dims in outs]
    vmem = pl.BlockSpec(memory_space=pltpu.VMEM)
    moved = sum(x.size for x in operands) + sum(x.size for x in shapes)
    return pl.pallas_call(
        kernel,
        out_shape=shapes,
        in_specs=spaces or [vmem] * len(operands),
        out_specs=[vmem] * len(shapes),
        scratch_shapes=scratch,
        compiler_params=PARAMS,
        cost_estimate=pl.CostEstimate(
            flops=flops, bytes_accessed=4 * moved, transcendentals=0
        ),
    )(*operands)


def beside(block):
    count = lax.axis_size("slab")
    if count == 2:
        return lax.ppermute(block, "slab", [(0, 1), (1, 0)])
    forward = [(i, i + 1) for i in range(count - 1)]
    backward = [(target, source) for source, target in forward]
    axis = block.ndim - 1
    atoms = block.shape[axis]
    low = lax.ppermute(lax.slice_in_dim(block, atoms - HW, atoms, axis=axis), "slab", forward)
    high = lax.ppermute(lax.slice_in_dim(block, 0, HW, axis=axis), "slab", backward)
    gap = jnp.zeros(block.shape[:-1] + (atoms - 2 * HW,), block.dtype)
    return jnp.concatenate([high, gap, low], axis=axis)


def body(
    lesser_free,
    greater_free,
    retarded,
    coupling,
    neighbour_offsets,
    phonon_shift,
    phonon_coupling,
    phonon_occupation,
):
    energies, pairs, atoms = lesser_free.shape
    fused = FUSED
    rows = fused * energies
    group = ROWS // rows
    groups = NB // group
    parts = lax.axis_size("energy")
    share = -(-pairs // parts)
    total = energies * parts
    vmem = pl.BlockSpec(memory_space=pltpu.VMEM)
    smem = pl.BlockSpec(memory_space=pltpu.SMEM)
    away = pl.BlockSpec(memory_space=pl.ANY)

    targets = neighbour_offsets + jnp.arange(atoms, dtype=jnp.int32)[None, :]
    placed = targets + lax.axis_index("slab") * atoms
    inside = (placed >= 0) & (placed < lax.axis_size("slab") * atoms)

    def widened(values):
        return jnp.broadcast_to(values[:, None, :], (NB, rows, atoms)).reshape(groups, ROWS, atoms)

    lanes = widened(jnp.remainder(targets, atoms))
    is_near = widened(((targets >= 0) & (targets < atoms)).astype(jnp.int32))

    free = (lesser_free, greater_free)
    chains = [free[at : at + fused] for at in range(0, 2, fused)]
    greens = list(chains)
    halos = [tuple(beside(g) for g in chain) for chain in greens]

    (links,) = call(
        functools.partial(prep_coupling_kernel, rows),
        [(groups * pairs * ROWS, atoms)],
        [],
        coupling.size * rows,
        coupling,
        inside.astype(jnp.float32),
    )
    links = links.reshape(groups, pairs, ROWS, atoms)
    left, right, mixing = call(
        functools.partial(prep_dressing_kernel, rows),
        [(pairs * rows, atoms), (pairs * ROWS, atoms), (2, total, total)],
        [],
        retarded.size * ROWS,
        retarded,
        phonon_shift,
        phonon_coupling,
        phonon_occupation,
        spaces=[vmem, smem, smem, smem],
    )
    left = left.reshape(pairs * rows // ROWS, ROWS, atoms)
    right = right.reshape(pairs, ROWS, atoms)

    wide = pltpu.VMEM((pairs * ROWS, atoms), jnp.float32)
    deep = pltpu.VMEM((pairs, ROWS, atoms), jnp.float32)
    flat = pltpu.VMEM((total, share * atoms), jnp.float32)
    work = 4 * NORB * rows * pairs * atoms

    for step in range(ITERS):
        coupled = [
            call(
                functools.partial(couple_kernel, fused),
                [(parts * share, rows, atoms)],
                [
                    wide,
                    wide,
                    deep,
                    deep,
                    deep,
                    pltpu.VMEM(links.shape, jnp.float32),
                    pltpu.SemaphoreType.DMA((groups,)),
                ],
                NB * work,
                *green,
                *halo,
                lanes,
                is_near,
                links,
                spaces=[vmem] * (2 * fused + 2) + [away],
            )[0]
            for green, halo in zip(greens, halos)
        ]
        gathered = [
            lax.all_to_all(x.reshape(parts, share, rows, atoms), "energy", 0, 0) for x in coupled
        ]
        mixed = [
            call(
                functools.partial(mix_kernel, fused),
                [x.shape],
                [flat, flat],
                2 * total * x.size,
                mixing[at * fused : (at + 1) * fused],
                x,
            )[0]
            for at, x in enumerate(gathered)
        ]
        sigma = [
            lax.all_to_all(x, "energy", 0, 0).reshape(parts * share, rows, atoms) for x in mixed
        ]
        greens = [
            call(
                functools.partial(dress_kernel, fused),
                [lesser_free.shape] * fused,
                [deep, pltpu.VMEM((pairs * rows, atoms), jnp.float32)],
                work,
                x,
                left,
                right,
                *chain,
            )
            for x, chain in zip(sigma, chains)
        ]
        if step < ITERS - 1:
            halos = [tuple(beside(g) for g in chain) for chain in greens]
    return tuple(g for chain in greens for g in chain)


def solution(mesh):
    placed = (
        P("energy", None, "slab"),
        P("energy", None, "slab"),
        P("energy", None, "slab"),
        P(None, None, "slab"),
        P(None, "slab"),
        P(),
        P(),
        P(),
    )
    return jax.shard_map(
        body,
        mesh=mesh,
        in_specs=placed,
        out_specs=(P("energy", None, "slab"), P("energy", None, "slab")),
        check_vma=False,
    )
```

```python
import functools

import jax
import jax.numpy as jnp
from jax import lax
from jax.experimental import pallas as pl
from jax.experimental.pallas import tpu as pltpu
from jax.sharding import PartitionSpec as P

NORB = 12
NB = 12
HW = 32
ITERS = 2
ROWS = 8
FUSED = 2

TOP_RANK = lax.Precision.HIGHEST
PARAMS = pltpu.CompilerParams(vmem_limit_bytes=24 * 1024 * 1024)


def tiles(count):
    return [(at, min(ROWS, count - at)) for at in range(0, count, ROWS)]


def spread_rows(target, base, row, source, first, count):
    for at, size in tiles(count):
        rows = pl.ds((base + at) * ROWS + row, size, stride=ROWS)
        target[rows, :] = source(first + at, size)


def prep_coupling_kernel(rows, coupling, inside, out):
    group = ROWS // rows
    pairs = coupling.shape[1]
    for n in range(NB):
        valid = inside[n : n + 1, :]
        for row in range(rows):
            spread_rows(
                out,
                (n // group) * pairs,
                (n % group) * rows + row,
                lambda at, size: coupling[n, at : at + size, :] * valid,
                0,
                pairs,
            )


def prep_dressing_kernel(rows, retarded, shifts, coupled, occupied, left, right, mixing):
    energies, pairs, _ = retarded.shape
    total = mixing.shape[1]
    share = pairs * rows // ROWS
    for row in range(ROWS):
        read = lambda at, size: retarded[row % energies, at : at + size, :]
        spread_rows(left, 0, row, read, row // rows * share, share)
        spread_rows(right, 0, row, read, 0, pairs)
    places = lax.broadcasted_iota(jnp.int32, (total, total), 0)
    gap = lax.broadcasted_iota(jnp.int32, (total, total), 1) - places

    def add_mode(mode, kernels):
        lesser, greater = kernels
        shift = shifts[mode]
        absorb = coupled[mode] * occupied[mode]
        emit = coupled[mode] * (occupied[mode] + 1.0)
        ahead = gap == shift
        behind = gap == -shift
        lesser = lesser + jnp.where(ahead, emit, 0.0) + jnp.where(behind, absorb, 0.0)
        greater = greater + jnp.where(ahead, absorb, 0.0) + jnp.where(behind, emit, 0.0)
        return lesser, greater

    empty = jnp.zeros((total, total), jnp.float32)
    lesser, greater = lax.fori_loop(0, shifts.shape[0], add_mode, (empty, empty))
    mixing[0] = lesser
    mixing[1] = greater


def couple_kernel(fused, *refs):
    near, far = refs[:fused], refs[fused : 2 * fused]
    lanes, is_near, links_hbm, out = refs[2 * fused : 2 * fused + 4]
    own, other, gathered_a, gathered_b, total, links, sems = refs[2 * fused + 4 :]
    energies, pairs, atoms = near[0].shape
    rows = fused * energies
    group = ROWS // rows
    groups = NB // group
    copies = [
        pltpu.make_async_copy(links_hbm.at[g], links.at[g], sems.at[g]) for g in range(groups)
    ]
    for copy in copies:
        copy.start()
    for row in range(ROWS):
        function, energy = row % rows // energies, row % energies
        for target, sources in ((own, near), (other, far)):
            source = sources[function]
            spread_rows(
                target, 0, row, lambda at, size: source[energy, at : at + size, :], 0, pairs
            )
    buffers = (gathered_a, gathered_b)

    def gather(g, first, count):
        target = buffers[g % 2]
        lane, mine = lanes[g], is_near[g] != 0
        for at in range(count):
            pair = first + at
            rows_at = pl.ds(pl.multiple_of(pair * ROWS, ROWS), ROWS)
            inner = jnp.take_along_axis(own[rows_at, :], lane, axis=1, mode="promise_in_bounds")
            outer = jnp.take_along_axis(other[rows_at, :], lane, axis=1, mode="promise_in_bounds")
            target[pair] = jnp.where(mine, inner, outer)

    blocked = 2
    steps = NORB // blocked
    chunk = pairs // steps
    lax.fori_loop(0, steps, lambda step, _: gather(0, step * chunk, chunk), None)
    for g in range(groups):
        copies[g].wait()
        source = buffers[g % 2]

        def block_row(step, _):
            first = step * blocked
            inner = [[None] * NORB for _ in range(blocked)]
            for j in range(NORB):
                left = [links[g, (first + b) * NORB + j] for b in range(blocked)]
                for l in range(NORB):
                    value = source[j * NORB + l]
                    for b in range(blocked):
                        term = left[b] * value
                        inner[b][l] = term if j == 0 else inner[b][l] + term
            for k in range(NORB):
                sums = [None] * blocked
                for l in range(NORB):
                    right = links[g, k * NORB + l]
                    for b in range(blocked):
                        term = inner[b][l] * right
                        sums[b] = term if l == 0 else sums[b] + term
                for b in range(blocked):
                    at = (first + b) * NORB + k
                    value = sums[b] if g == 0 else total[at] + sums[b]
                    if g < groups - 1:
                        total[at] = value
                    else:
                        width = ROWS // 2
                        while width >= rows:
                            value = value + pltpu.roll(value, width, 0)
                            width //= 2
                        out[at] = value[:rows]
            if g < groups - 1:
                gather(g + 1, step * chunk, chunk)

        lax.fori_loop(0, steps, block_row, None)
    for at in range(pairs, out.shape[0]):
        out[at] = jnp.zeros((rows, atoms), jnp.float32)


def mix_kernel(fused, mixing, blocks, out, before, after):
    parts, share, rows, atoms = blocks.shape
    energies = rows // fused
    for f in range(fused):
        some = slice(f * energies, (f + 1) * energies)
        for part in range(parts):
            for pair in range(share):
                before[part * energies : (part + 1) * energies, pair * atoms : (pair + 1) * atoms] = (
                    blocks[part, pair, some, :]
                )
        after[...] = jnp.dot(
            mixing[f], before[...], precision=TOP_RANK, preferred_element_type=jnp.float32
        )
        for part in range(parts):
            for pair in range(share):
                out[part, pair, some, :] = after[
                    part * energies : (part + 1) * energies, pair * atoms : (pair + 1) * atoms
                ]


def dress_kernel(fused, *refs):
    sigma, left, right = refs[:3]
    free, out = refs[3 : 3 + fused], refs[3 + fused : 3 + 2 * fused]
    copied, dressed = refs[3 + 2 * fused :]
    energies, pairs, atoms = free[0].shape
    rows = fused * energies
    parts = ROWS // rows
    share = pairs // parts
    for pair in range(pairs):
        value = sigma[pair]
        for part in range(parts):
            copied[pair, part * rows : (part + 1) * rows, :] = value
    for i in range(NORB // parts):
        inner = [None] * NORB
        for j in range(NORB):
            factor = left[i * NORB + j]
            for l in range(NORB):
                term = factor * copied[j * NORB + l]
                inner[l] = term if j == 0 else inner[l] + term
        for k in range(NORB):
            value = inner[0] * right[k * NORB]
            for l in range(1, NORB):
                value = value + inner[l] * right[k * NORB + l]
            at = (i * NORB + k) * ROWS
            dressed[at : at + ROWS, :] = value
    for row in range(ROWS):
        function, energy, part = row % rows // energies, row % energies, row // rows
        for at, size in tiles(share):
            first = part * share + at
            piece = dressed[pl.ds(at * ROWS + row, size, stride=ROWS), :]
            out[function][energy, first : first + size, :] = (
                free[function][energy, first : first + size, :] + piece
            )


def call(kernel, outs, scratch, flops, *operands, spaces=None):
    shapes = [jax.ShapeDtypeStruct(dims, jnp.float32) for dims in outs]
    vmem = pl.BlockSpec(memory_space=pltpu.VMEM)
    moved = sum(x.size for x in operands) + sum(x.size for x in shapes)
    return pl.pallas_call(
        kernel,
        out_shape=shapes,
        in_specs=spaces or [vmem] * len(operands),
        out_specs=[vmem] * len(shapes),
        scratch_shapes=scratch,
        compiler_params=PARAMS,
        cost_estimate=pl.CostEstimate(
            flops=flops, bytes_accessed=4 * moved, transcendentals=0
        ),
    )(*operands)


def beside(block):
    count = lax.axis_size("slab")
    if count == 2:
        return lax.ppermute(block, "slab", [(0, 1), (1, 0)])
    forward = [(i, i + 1) for i in range(count - 1)]
    backward = [(target, source) for source, target in forward]
    axis = block.ndim - 1
    atoms = block.shape[axis]
    low = lax.ppermute(lax.slice_in_dim(block, atoms - HW, atoms, axis=axis), "slab", forward)
    high = lax.ppermute(lax.slice_in_dim(block, 0, HW, axis=axis), "slab", backward)
    gap = jnp.zeros(block.shape[:-1] + (atoms - 2 * HW,), block.dtype)
    return jnp.concatenate([high, gap, low], axis=axis)


def body(
    lesser_free,
    greater_free,
    retarded,
    coupling,
    neighbour_offsets,
    phonon_shift,
    phonon_coupling,
    phonon_occupation,
):
    energies, pairs, atoms = lesser_free.shape
    fused = FUSED
    rows = fused * energies
    group = ROWS // rows
    groups = NB // group
    parts = lax.axis_size("energy")
    share = -(-pairs // parts)
    total = energies * parts
    vmem = pl.BlockSpec(memory_space=pltpu.VMEM)
    smem = pl.BlockSpec(memory_space=pltpu.SMEM)
    away = pl.BlockSpec(memory_space=pl.ANY)

    targets = neighbour_offsets + jnp.arange(atoms, dtype=jnp.int32)[None, :]
    placed = targets + lax.axis_index("slab") * atoms
    inside = (placed >= 0) & (placed < lax.axis_size("slab") * atoms)

    def widened(values):
        return jnp.broadcast_to(values[:, None, :], (NB, rows, atoms)).reshape(groups, ROWS, atoms)

    lanes = widened(jnp.remainder(targets, atoms))
    is_near = widened(((targets >= 0) & (targets < atoms)).astype(jnp.int32))

    free = (lesser_free, greater_free)
    chains = [free[at : at + fused] for at in range(0, 2, fused)]
    greens = list(chains)
    halos = [tuple(beside(g) for g in chain) for chain in greens]

    (links,) = call(
        functools.partial(prep_coupling_kernel, rows),
        [(groups * pairs * ROWS, atoms)],
        [],
        coupling.size * rows,
        coupling,
        inside.astype(jnp.float32),
    )
    links = links.reshape(groups, pairs, ROWS, atoms)
    left, right, mixing = call(
        functools.partial(prep_dressing_kernel, rows),
        [(pairs * rows, atoms), (pairs * ROWS, atoms), (2, total, total)],
        [],
        retarded.size * ROWS,
        retarded,
        phonon_shift,
        phonon_coupling,
        phonon_occupation,
        spaces=[vmem, smem, smem, smem],
    )
    left = left.reshape(pairs * rows // ROWS, ROWS, atoms)
    right = right.reshape(pairs, ROWS, atoms)

    wide = pltpu.VMEM((pairs * ROWS, atoms), jnp.float32)
    deep = pltpu.VMEM((pairs, ROWS, atoms), jnp.float32)
    flat = pltpu.VMEM((total, share * atoms), jnp.float32)
    work = 4 * NORB * rows * pairs * atoms

    for step in range(ITERS):
        coupled = [
            call(
                functools.partial(couple_kernel, fused),
                [(parts * share, rows, atoms)],
                [
                    wide,
                    wide,
                    deep,
                    deep,
                    deep,
                    pltpu.VMEM(links.shape, jnp.float32),
                    pltpu.SemaphoreType.DMA((groups,)),
                ],
                NB * work,
                *green,
                *halo,
                lanes,
                is_near,
                links,
                spaces=[vmem] * (2 * fused + 2) + [away],
            )[0]
            for green, halo in zip(greens, halos)
        ]
        gathered = [
            lax.all_to_all(x.reshape(parts, share, rows, atoms), "energy", 0, 0) for x in coupled
        ]
        mixed = [
            call(
                functools.partial(mix_kernel, fused),
                [x.shape],
                [flat, flat],
                2 * total * x.size,
                mixing[at * fused : (at + 1) * fused],
                x,
            )[0]
            for at, x in enumerate(gathered)
        ]
        sigma = [
            lax.all_to_all(x, "energy", 0, 0).reshape(parts * share, rows, atoms) for x in mixed
        ]
        greens = [
            call(
                functools.partial(dress_kernel, fused),
                [lesser_free.shape] * fused,
                [deep, pltpu.VMEM((pairs * rows, atoms), jnp.float32)],
                work,
                x,
                left,
                right,
                *chain,
            )
            for x, chain in zip(sigma, chains)
        ]
        if step < ITERS - 1:
            halos = [tuple(beside(g) for g in chain) for chain in greens]
    return tuple(g for chain in greens for g in chain)


def solution(mesh):
    placed = (
        P("energy", None, "slab"),
        P("energy", None, "slab"),
        P("energy", None, "slab"),
        P(None, None, "slab"),
        P(None, "slab"),
        P(),
        P(),
        P(),
    )
    return jax.shard_map(
        body,
        mesh=mesh,
        in_specs=placed,
        out_specs=(P("energy", None, "slab"), P("energy", None, "slab")),
        check_vma=False,
    )
```

```python
import functools

import jax
import jax.numpy as jnp
from jax import lax
from jax.experimental import pallas as pl
from jax.experimental.pallas import tpu as pltpu
from jax.sharding import PartitionSpec as P

NORB = 12
NB = 12
HW = 32
ITERS = 2
ROWS = 8
FUSED = 2

TOP_RANK = lax.Precision.HIGHEST
PARAMS = pltpu.CompilerParams(vmem_limit_bytes=24 * 1024 * 1024)


def tiles(count):
    return [(at, min(ROWS, count - at)) for at in range(0, count, ROWS)]


def spread_rows(target, base, row, source, first, count):
    for at, size in tiles(count):
        rows = pl.ds((base + at) * ROWS + row, size, stride=ROWS)
        target[rows, :] = source(first + at, size)


def prep_coupling_kernel(rows, coupling, offsets, out, lanes, is_near):
    group = ROWS // rows
    _, pairs, atoms = coupling.shape
    slab, slabs = lax.axis_index("slab"), lax.axis_size("slab")
    targets = offsets[...] + lax.broadcasted_iota(jnp.int32, (NB, atoms), 1)
    placed = targets + slab * atoms
    inside = ((placed >= 0) & (placed < slabs * atoms)).astype(jnp.float32)
    near = ((targets >= 0) & (targets < atoms)).astype(jnp.int32)
    lane = jnp.where(targets < 0, targets + atoms, targets)
    lane = jnp.where(lane >= atoms, lane - atoms, lane)
    for n in range(NB):
        valid = inside[n : n + 1, :]
        some = slice(n % group * rows, (n % group + 1) * rows)
        lanes[n // group, some, :] = jnp.broadcast_to(lane[n : n + 1, :], (rows, atoms))
        is_near[n // group, some, :] = jnp.broadcast_to(near[n : n + 1, :], (rows, atoms))
        for row in range(rows):
            spread_rows(
                out,
                (n // group) * pairs,
                (n % group) * rows + row,
                lambda at, size: coupling[n, at : at + size, :] * valid,
                0,
                pairs,
            )


def partner(device, slot, parts):
    if parts & (parts - 1) == 0:
        return device ^ slot
    return (device + slot) % parts


def origin(device, slot, parts):
    if parts & (parts - 1) == 0:
        return device ^ slot
    return (device + parts - slot) % parts


def exchanged(shares):
    parts = len(shares)
    received = [shares[0]]
    for slot in range(1, parts):
        route = [(i, partner(i, slot, parts)) for i in range(parts)]
        received.append(lax.ppermute(shares[slot], "energy", route))
    return received


def prep_dressing_kernel(rows, retarded, shifts, coupled, occupied, left, right, mixing):
    energies, pairs, _ = retarded.shape
    total = mixing.shape[1]
    parts = total // energies
    device = lax.axis_index("energy")
    share = pairs * rows // ROWS
    for row in range(ROWS):
        read = lambda at, size: retarded[row % energies, at : at + size, :]
        spread_rows(left, 0, row, read, row // rows * share, share)
        spread_rows(right, 0, row, read, 0, pairs)
    row_at = lax.broadcasted_iota(jnp.int32, (total, total), 0)
    column_at = lax.broadcasted_iota(jnp.int32, (total, total), 1)
    sent = jnp.zeros((total, total), jnp.int32)
    came = jnp.zeros((total, total), jnp.int32)
    for slot in range(parts):
        first = slot * energies
        for at in range(energies):
            sent = jnp.where(row_at == first + at, partner(device, slot, parts) * energies + at, sent)
            came = jnp.where(column_at == first + at, origin(device, slot, parts) * energies + at, came)
    gap = came - sent

    def add_mode(mode, kernels):
        lesser, greater = kernels
        shift = shifts[mode]
        absorb = coupled[mode] * occupied[mode]
        emit = coupled[mode] * (occupied[mode] + 1.0)
        ahead = gap == shift
        behind = gap == -shift
        lesser = lesser + jnp.where(ahead, emit, 0.0) + jnp.where(behind, absorb, 0.0)
        greater = greater + jnp.where(ahead, absorb, 0.0) + jnp.where(behind, emit, 0.0)
        return lesser, greater

    empty = jnp.zeros((total, total), jnp.float32)
    lesser, greater = lax.fori_loop(0, shifts.shape[0], add_mode, (empty, empty))
    mixing[0] = lesser
    mixing[1] = greater


def couple_kernel(fused, *refs):
    near, far = refs[:fused], refs[fused : 2 * fused]
    lanes, is_near, links = refs[2 * fused : 2 * fused + 3]
    outs = refs[2 * fused + 3 : -6]
    own, other, gathered_a, gathered_b, total, staged = refs[-6:]
    energies, pairs, atoms = near[0].shape
    rows = fused * energies
    group = ROWS // rows
    groups = NB // group
    for row in range(ROWS):
        function, energy = row % rows // energies, row % energies
        for target, sources in ((own, near), (other, far)):
            source = sources[function]
            spread_rows(
                target, 0, row, lambda at, size: source[energy, at : at + size, :], 0, pairs
            )
    buffers = (gathered_a, gathered_b)

    def gather(g, first, count):
        target = buffers[g % 2]
        lane, mine = lanes[g], is_near[g] != 0
        for at in range(count):
            pair = first + at
            rows_at = pl.ds(pl.multiple_of(pair * ROWS, ROWS), ROWS)
            inner = jnp.take_along_axis(own[rows_at, :], lane, axis=1, mode="promise_in_bounds")
            outer = jnp.take_along_axis(other[rows_at, :], lane, axis=1, mode="promise_in_bounds")
            target[pair] = jnp.where(mine, inner, outer)

    blocked = 3
    steps = NORB // blocked
    chunk = pairs // steps
    lax.fori_loop(0, steps, lambda step, _: gather(0, step * chunk, chunk), None)
    for g in range(groups):
        source = buffers[g % 2]

        def block_row(step, _):
            first = step * blocked
            inner = [[None] * NORB for _ in range(blocked)]
            for j in range(NORB):
                left = [links[g, (first + b) * NORB + j] for b in range(blocked)]
                for l in range(NORB):
                    value = source[j * NORB + l]
                    for b in range(blocked):
                        term = left[b] * value
                        inner[b][l] = term if j == 0 else inner[b][l] + term
            for k in range(NORB):
                sums = [None] * blocked
                for l in range(NORB):
                    right = links[g, k * NORB + l]
                    for b in range(blocked):
                        term = inner[b][l] * right
                        sums[b] = term if l == 0 else sums[b] + term
                for b in range(blocked):
                    at = (first + b) * NORB + k
                    value = sums[b] if g == 0 else total[at] + sums[b]
                    if g < groups - 1:
                        total[at] = value
                    else:
                        width = ROWS // 2
                        while width >= rows:
                            value = value + pltpu.roll(value, width, 0)
                            width //= 2
                        staged[at] = value[:rows]
            if g < groups - 1:
                gather(g + 1, step * chunk, chunk)

        lax.fori_loop(0, steps, block_row, None)
    for at in range(pairs, staged.shape[0]):
        staged[at] = jnp.zeros((rows, atoms), jnp.float32)
    device = lax.axis_index("energy")
    share = outs[0].shape[0]
    for slot, out in enumerate(outs):
        first = partner(device, slot, len(outs)) * share
        for at in range(share):
            out[at] = staged[first + at]


def mix_kernel(fused, parts, mixing, *refs):
    blocks, outs = refs[:parts], refs[parts : 2 * parts]
    before, after = refs[2 * parts :]
    share, rows, atoms = blocks[0].shape
    energies = rows // fused
    for f in range(fused):
        some = slice(f * energies, (f + 1) * energies)
        for slot in range(parts):
            held = slice(slot * energies, (slot + 1) * energies)
            for pair in range(share):
                before[f, held, pair * atoms : (pair + 1) * atoms] = blocks[slot][pair, some, :]
        after[f] = jnp.dot(
            mixing[f], before[f], precision=TOP_RANK, preferred_element_type=jnp.float32
        )
        for slot in range(parts):
            held = slice(slot * energies, (slot + 1) * energies)
            for pair in range(share):
                outs[slot][pair, some, :] = after[f, held, pair * atoms : (pair + 1) * atoms]


def dress_kernel(fused, slots, *refs):
    sigma, refs = refs[:slots], refs[slots:]
    left, right = refs[:2]
    free, out = refs[2 : 2 + fused], refs[2 + fused : 2 + 2 * fused]
    copied, dressed = refs[2 + 2 * fused :]
    energies, pairs, atoms = free[0].shape
    rows = fused * energies
    parts = ROWS // rows
    share = pairs // parts
    device = lax.axis_index("energy")
    width = sigma[0].shape[0]
    for slot in range(slots):
        first = origin(device, slot, slots) * width
        for at in range(width):
            value = sigma[slot][at]
            for part in range(parts):
                copied[first + at, part * rows : (part + 1) * rows, :] = value
    for i in range(NORB // parts):
        inner = [None] * NORB
        for j in range(NORB):
            factor = left[i * NORB + j]
            for l in range(NORB):
                term = factor * copied[j * NORB + l]
                inner[l] = term if j == 0 else inner[l] + term
        for k in range(NORB):
            value = inner[0] * right[k * NORB]
            for l in range(1, NORB):
                value = value + inner[l] * right[k * NORB + l]
            at = (i * NORB + k) * ROWS
            dressed[at : at + ROWS, :] = value
    for row in range(ROWS):
        function, energy, part = row % rows // energies, row % energies, row // rows
        for at, size in tiles(share):
            first = part * share + at
            piece = dressed[pl.ds(at * ROWS + row, size, stride=ROWS), :]
            out[function][energy, first : first + size, :] = (
                free[function][energy, first : first + size, :] + piece
            )


def call(kernel, outs, scratch, flops, *operands, spaces=None):
    shapes = [
        x if isinstance(x, jax.ShapeDtypeStruct) else jax.ShapeDtypeStruct(x, jnp.float32)
        for x in outs
    ]
    vmem = pl.BlockSpec(memory_space=pltpu.VMEM)
    moved = sum(x.size for x in operands) + sum(x.size for x in shapes)
    return pl.pallas_call(
        kernel,
        out_shape=shapes,
        in_specs=spaces or [vmem] * len(operands),
        out_specs=[vmem] * len(shapes),
        scratch_shapes=scratch,
        compiler_params=PARAMS,
        cost_estimate=pl.CostEstimate(
            flops=flops, bytes_accessed=4 * moved, transcendentals=0
        ),
    )(*operands)


def beside(block):
    count = lax.axis_size("slab")
    if count == 2:
        return lax.ppermute(block, "slab", [(0, 1), (1, 0)])
    forward = [(i, i + 1) for i in range(count - 1)]
    backward = [(target, source) for source, target in forward]
    axis = block.ndim - 1
    atoms = block.shape[axis]
    low = lax.ppermute(lax.slice_in_dim(block, atoms - HW, atoms, axis=axis), "slab", forward)
    high = lax.ppermute(lax.slice_in_dim(block, 0, HW, axis=axis), "slab", backward)
    gap = jnp.zeros(block.shape[:-1] + (atoms - 2 * HW,), block.dtype)
    return jnp.concatenate([high, gap, low], axis=axis)


def body(
    lesser_free,
    greater_free,
    retarded,
    coupling,
    neighbour_offsets,
    phonon_shift,
    phonon_coupling,
    phonon_occupation,
):
    energies, pairs, atoms = lesser_free.shape
    fused = FUSED
    rows = fused * energies
    group = ROWS // rows
    groups = NB // group
    parts = lax.axis_size("energy")
    share = -(-pairs // parts)
    total = energies * parts
    vmem = pl.BlockSpec(memory_space=pltpu.VMEM)
    smem = pl.BlockSpec(memory_space=pltpu.SMEM)
    indices = jax.ShapeDtypeStruct((groups, ROWS, atoms), jnp.int32)

    free = (lesser_free, greater_free)
    chains = [free[at : at + fused] for at in range(0, 2, fused)]
    greens = list(chains)
    halos = [tuple(beside(g) for g in chain) for chain in greens]

    links, lanes, is_near = call(
        functools.partial(prep_coupling_kernel, rows),
        [(groups * pairs * ROWS, atoms), indices, indices],
        [],
        coupling.size * rows,
        coupling,
        neighbour_offsets,
    )
    links = links.reshape(groups, pairs, ROWS, atoms)
    left, right, mixing = call(
        functools.partial(prep_dressing_kernel, rows),
        [(pairs * rows, atoms), (pairs * ROWS, atoms), (2, total, total)],
        [],
        retarded.size * ROWS,
        retarded,
        phonon_shift,
        phonon_coupling,
        phonon_occupation,
        spaces=[vmem, smem, smem, smem],
    )
    left = left.reshape(pairs * rows // ROWS, ROWS, atoms)
    right = right.reshape(pairs, ROWS, atoms)

    wide = pltpu.VMEM((pairs * ROWS, atoms), jnp.float32)
    deep = pltpu.VMEM((pairs, ROWS, atoms), jnp.float32)
    flat = pltpu.VMEM((fused, total, share * atoms), jnp.float32)
    staged = pltpu.VMEM((parts * share, rows, atoms), jnp.float32)
    shares = [(share, rows, atoms)] * parts
    work = 4 * NORB * rows * pairs * atoms

    for step in range(ITERS):
        coupled = [
            call(
                functools.partial(couple_kernel, fused),
                shares,
                [wide, wide, deep, deep, deep, staged],
                NB * work,
                *green,
                *halo,
                lanes,
                is_near,
                links,
            )
            for green, halo in zip(greens, halos)
        ]
        gathered = [exchanged(x) for x in coupled]
        mixed = [
            call(
                functools.partial(mix_kernel, fused, parts),
                shares,
                [flat, flat],
                2 * total * rows * share * parts * atoms,
                mixing[at * fused : (at + 1) * fused],
                *x,
            )
            for at, x in enumerate(gathered)
        ]
        sigma = [exchanged(x) for x in mixed]
        greens = [
            call(
                functools.partial(dress_kernel, fused, parts),
                [lesser_free.shape] * fused,
                [
                    pltpu.VMEM((parts * share, ROWS, atoms), jnp.float32),
                    pltpu.VMEM((pairs * rows, atoms), jnp.float32),
                ],
                work,
                *x,
                left,
                right,
                *chain,
            )
            for x, chain in zip(sigma, chains)
        ]
        if step < ITERS - 1:
            halos = [tuple(beside(g) for g in chain) for chain in greens]
    return tuple(g for chain in greens for g in chain)


def solution(mesh):
    placed = (
        P("energy", None, "slab"),
        P("energy", None, "slab"),
        P("energy", None, "slab"),
        P(None, None, "slab"),
        P(None, "slab"),
        P(),
        P(),
        P(),
    )
    return jax.shard_map(
        body,
        mesh=mesh,
        in_specs=placed,
        out_specs=(P("energy", None, "slab"), P("energy", None, "slab")),
        check_vma=False,
    )
```

```python
import functools

import jax
import jax.numpy as jnp
from jax import lax
from jax.experimental import pallas as pl
from jax.experimental.pallas import tpu as pltpu
from jax.sharding import PartitionSpec as P

NORB = 12
NB = 12
HW = 32
ITERS = 2
ROWS = 8
FUSED = 2

TOP_RANK = lax.Precision.HIGHEST
PARAMS = pltpu.CompilerParams(vmem_limit_bytes=24 * 1024 * 1024)


def tiles(count):
    return [(at, min(ROWS, count - at)) for at in range(0, count, ROWS)]


def spread_rows(target, base, row, source, first, count):
    for at, size in tiles(count):
        rows = pl.ds((base + at) * ROWS + row, size, stride=ROWS)
        target[rows, :] = source(first + at, size)


def prep_kernel(fused, chains, *refs):
    coupling_hbm, retarded_hbm, *free_hbm = refs[: 2 + 2]
    offsets, shifts, coupled, occupied = refs[4:8]
    links, lanes, is_near, left, right, mixing = refs[8:14]
    owns = refs[14 : 14 + chains]
    coupling, retarded, free, sems = refs[14 + chains :]
    energies, pairs, atoms = retarded.shape
    rows = fused * energies
    group = ROWS // rows
    copies = [pltpu.make_async_copy(free_hbm[f], free.at[f], sems.at[f]) for f in range(2)]
    copies.append(pltpu.make_async_copy(retarded_hbm, retarded, sems.at[2]))
    for n in range(NB):
        copies.append(
            pltpu.make_async_copy(coupling_hbm.at[n], coupling.at[n], sems.at[3 + n])
        )
    for copy in copies:
        copy.start()

    total = mixing.shape[1]
    gap = lax.broadcasted_iota(jnp.int32, (total, total), 1) - lax.broadcasted_iota(
        jnp.int32, (total, total), 0
    )
    lesser = jnp.zeros((total, total), jnp.float32)
    greater = jnp.zeros((total, total), jnp.float32)
    for mode in range(shifts.shape[0]):
        shift = shifts[mode]
        absorb = coupled[mode] * occupied[mode]
        emit = coupled[mode] * (occupied[mode] + 1.0)
        ahead = gap == shift
        behind = gap == -shift
        lesser = lesser + jnp.where(ahead, emit, jnp.where(behind, absorb, 0.0))
        greater = greater + jnp.where(ahead, absorb, jnp.where(behind, emit, 0.0))
    mixing[0] = lesser
    mixing[1] = greater

    slab, slabs = lax.axis_index("slab"), lax.axis_size("slab")
    targets = offsets[...] + lax.broadcasted_iota(jnp.int32, (NB, atoms), 1)
    placed = targets + slab * atoms
    inside = ((placed >= 0) & (placed < slabs * atoms)).astype(jnp.float32)
    near = ((targets >= 0) & (targets < atoms)).astype(jnp.int32)
    lane = jnp.where(targets < 0, targets + atoms, targets)
    lane = jnp.where(lane >= atoms, lane - atoms, lane)
    for n in range(NB):
        some = slice(n % group * rows, (n % group + 1) * rows)
        lanes[n // group, some, :] = jnp.broadcast_to(lane[n : n + 1, :], (rows, atoms))
        is_near[n // group, some, :] = jnp.broadcast_to(near[n : n + 1, :], (rows, atoms))

    copies[0].wait()
    copies[1].wait()
    for chain, own in enumerate(owns):
        for row in range(ROWS):
            function, energy = chain * fused + row % rows // energies, row % energies
            spread_rows(
                own, 0, row, lambda at, size: free[function, energy, at : at + size, :], 0, pairs
            )
    copies[2].wait()
    share = pairs * rows // ROWS
    for row in range(ROWS):
        read = lambda at, size: retarded[row % energies, at : at + size, :]
        spread_rows(left, 0, row, read, row // rows * share, share)
        spread_rows(right, 0, row, read, 0, pairs)
    for n in range(NB):
        copies[3 + n].wait()
        valid = inside[n : n + 1, :]
        for row in range(rows):
            spread_rows(
                links,
                (n // group) * pairs,
                (n % group) * rows + row,
                lambda at, size: coupling[n, at : at + size, :] * valid,
                0,
                pairs,
            )


def couple_kernel(fused, energies, own, *refs):
    far, refs = refs[:-8], refs[-8:]
    lanes, is_near, links, out = refs[:4]
    other, gathered_a, gathered_b, total = refs[4:]
    _, pairs, _, atoms = links.shape
    rows = fused * energies
    group = ROWS // rows
    groups = NB // group
    if len(far) == 1:
        for pair in range(pairs):
            value = far[0][pair]
            for at in range(0, ROWS, rows):
                other[pair * ROWS + at : pair * ROWS + at + rows, :] = value
    else:
        for row in range(ROWS):
            source = far[row % rows // energies]
            spread_rows(
                other, 0, row, lambda at, size: source[row % energies, at : at + size, :], 0, pairs
            )
    buffers = (gathered_a, gathered_b)

    def gather(g, first, count):
        target = buffers[g % 2]
        lane, mine = lanes[g], is_near[g] != 0
        for at in range(count):
            pair = first + at
            rows_at = pl.ds(pl.multiple_of(pair * ROWS, ROWS), ROWS)
            inner = jnp.take_along_axis(own[rows_at, :], lane, axis=1, mode="promise_in_bounds")
            outer = jnp.take_along_axis(other[rows_at, :], lane, axis=1, mode="promise_in_bounds")
            target[pair] = jnp.where(mine, inner, outer)

    blocked = 2
    steps = NORB // blocked
    chunk = pairs // steps
    lax.fori_loop(0, steps, lambda step, _: gather(0, step * chunk, chunk), None)
    for g in range(groups):
        source = buffers[g % 2]

        def block_row(step, _):
            first = step * blocked
            inner = [[None] * NORB for _ in range(blocked)]
            for j in range(NORB):
                left = [links[g, (first + b) * NORB + j] for b in range(blocked)]
                for l in range(NORB):
                    value = source[j * NORB + l]
                    for b in range(blocked):
                        term = left[b] * value
                        inner[b][l] = term if j == 0 else inner[b][l] + term
            for k in range(NORB):
                sums = [None] * blocked
                for l in range(NORB):
                    right = links[g, k * NORB + l]
                    for b in range(blocked):
                        term = inner[b][l] * right
                        sums[b] = term if l == 0 else sums[b] + term
                for b in range(blocked):
                    at = (first + b) * NORB + k
                    value = sums[b] if g == 0 else total[at] + sums[b]
                    if g < groups - 1:
                        total[at] = value
                    else:
                        width = ROWS // 2
                        while width >= rows:
                            value = value + pltpu.roll(value, width, 0)
                            width //= 2
                        out[at] = value[:rows]
            if g < groups - 1:
                gather(g + 1, step * chunk, chunk)

        lax.fori_loop(0, steps, block_row, None)
    for at in range(pairs, out.shape[0]):
        out[at] = jnp.zeros((rows, atoms), jnp.float32)


def mix_kernel(fused, mixing, blocks, out, before, after):
    parts, share, rows, atoms = blocks.shape
    energies = rows // fused
    for f in range(fused):
        some = slice(f * energies, (f + 1) * energies)
        for part in range(parts):
            for pair in range(share):
                before[part * energies : (part + 1) * energies, pair * atoms : (pair + 1) * atoms] = (
                    blocks[part, pair, some, :]
                )
        after[...] = jnp.dot(
            mixing[f], before[...], precision=TOP_RANK, preferred_element_type=jnp.float32
        )
        for part in range(parts):
            for pair in range(share):
                out[part, pair, some, :] = after[
                    part * energies : (part + 1) * energies, pair * atoms : (pair + 1) * atoms
                ]


def dress(rows, sigma, left, right, copied, keep):
    parts = ROWS // rows
    for pair in range(NORB * NORB):
        value = sigma[pair]
        for part in range(parts):
            copied[pair, part * rows : (part + 1) * rows, :] = value
    for i in range(NORB // parts):
        inner = [None] * NORB
        for j in range(NORB):
            factor = left[i * NORB + j]
            for l in range(NORB):
                term = factor * copied[j * NORB + l]
                inner[l] = term if j == 0 else inner[l] + term
        for k in range(NORB):
            value = inner[0] * right[k * NORB]
            for l in range(1, NORB):
                value = value + inner[l] * right[k * NORB + l]
            keep(i * NORB + k, value)


def dress_between_kernel(rows, sigma, left, right, free, own, compact, copied):
    pairs, _, atoms = sigma.shape[0], rows, sigma.shape[2]
    share = left.shape[0]
    row_at = lax.broadcasted_iota(jnp.int32, (ROWS, atoms), 0)

    def keep(at, value):
        for part in range(ROWS // rows):
            held = (row_at >= part * rows) & (row_at < (part + 1) * rows)
            piece = jnp.where(held, value, 0.0)
            width = ROWS // 2
            while width >= rows:
                piece = piece + pltpu.roll(piece, width, 0)
                width //= 2
            pair = part * share + at
            piece = piece + free[pair * ROWS : (pair + 1) * ROWS, :]
            own[pair * ROWS : (pair + 1) * ROWS, :] = piece
            compact[pair] = piece[:rows]

    dress(rows, sigma, left, right, copied, keep)


def dress_last_kernel(fused, *refs):
    sigma, left, right = refs[:3]
    free, out = refs[3 : 3 + fused], refs[3 + fused : 3 + 2 * fused]
    copied, dressed = refs[3 + 2 * fused :]
    energies = free[0].shape[0]
    rows = fused * energies
    share = left.shape[0]

    def keep(at, value):
        dressed[at * ROWS : (at + 1) * ROWS, :] = value

    dress(rows, sigma, left, right, copied, keep)
    for row in range(ROWS):
        function, energy, part = row % rows // energies, row % energies, row // rows
        for at, size in tiles(share):
            first = part * share + at
            piece = dressed[pl.ds(at * ROWS + row, size, stride=ROWS), :]
            out[function][energy, first : first + size, :] = (
                free[function][energy, first : first + size, :] + piece
            )


def call(kernel, outs, scratch, flops, *operands, spaces=None):
    shapes = [
        x if isinstance(x, jax.ShapeDtypeStruct) else jax.ShapeDtypeStruct(x, jnp.float32)
        for x in outs
    ]
    vmem = pl.BlockSpec(memory_space=pltpu.VMEM)
    moved = sum(x.size for x in operands) + sum(x.size for x in shapes)
    return pl.pallas_call(
        kernel,
        out_shape=shapes,
        in_specs=spaces or [vmem] * len(operands),
        out_specs=[vmem] * len(shapes),
        scratch_shapes=scratch,
        compiler_params=PARAMS,
        cost_estimate=pl.CostEstimate(
            flops=flops, bytes_accessed=4 * moved, transcendentals=0
        ),
    )(*operands)


def beside(block):
    count = lax.axis_size("slab")
    if count == 2:
        return lax.ppermute(block, "slab", [(0, 1), (1, 0)])
    forward = [(i, i + 1) for i in range(count - 1)]
    backward = [(target, source) for source, target in forward]
    axis = block.ndim - 1
    atoms = block.shape[axis]
    low = lax.ppermute(lax.slice_in_dim(block, atoms - HW, atoms, axis=axis), "slab", forward)
    high = lax.ppermute(lax.slice_in_dim(block, 0, HW, axis=axis), "slab", backward)
    gap = jnp.zeros(block.shape[:-1] + (atoms - 2 * HW,), block.dtype)
    return jnp.concatenate([high, gap, low], axis=axis)


def body(
    lesser_free,
    greater_free,
    retarded,
    coupling,
    neighbour_offsets,
    phonon_shift,
    phonon_coupling,
    phonon_occupation,
):
    energies, pairs, atoms = lesser_free.shape
    fused = FUSED
    rows = fused * energies
    group = ROWS // rows
    groups = NB // group
    parts = lax.axis_size("energy")
    share = -(-pairs // parts)
    total = energies * parts
    vmem = pl.BlockSpec(memory_space=pltpu.VMEM)
    smem = pl.BlockSpec(memory_space=pltpu.SMEM)
    away = pl.BlockSpec(memory_space=pltpu.HBM)
    indices = jax.ShapeDtypeStruct((groups, ROWS, atoms), jnp.int32)
    wide = (pairs * ROWS, atoms)
    deep = (pairs, ROWS, atoms)
    work = 4 * NORB * rows * pairs * atoms

    free = (lesser_free, greater_free)
    chains = [free[at : at + fused] for at in range(0, 2, fused)]
    halos = [tuple(beside(g) for g in chain) for chain in chains]
    links, lanes, is_near, left, right, mixing, *frees = call(
        functools.partial(prep_kernel, fused, len(chains)),
        [
            (groups * pairs * ROWS, atoms),
            indices,
            indices,
            (pairs * rows, atoms),
            wide,
            (2, total, total),
        ]
        + [wide] * len(chains),
        [
            pltpu.VMEM(coupling.shape, jnp.float32),
            pltpu.VMEM(retarded.shape, jnp.float32),
            pltpu.VMEM((2,) + retarded.shape, jnp.float32),
            pltpu.SemaphoreType.DMA((3 + NB,)),
        ],
        coupling.size * rows,
        coupling,
        retarded,
        *free,
        neighbour_offsets,
        phonon_shift,
        phonon_coupling,
        phonon_occupation,
        spaces=[away] * 4 + [vmem] + [smem] * 3,
    )
    links = links.reshape(groups, pairs, ROWS, atoms)
    left = left.reshape(pairs * rows // ROWS, ROWS, atoms)
    right = right.reshape(pairs, ROWS, atoms)
    owns = frees

    for step in range(ITERS):
        coupled = [
            call(
                functools.partial(couple_kernel, fused, energies),
                [(parts * share, rows, atoms)],
                [pltpu.VMEM(wide, jnp.float32)] + [pltpu.VMEM(deep, jnp.float32)] * 3,
                NB * work,
                own,
                *halo,
                lanes,
                is_near,
                links,
            )[0]
            for own, halo in zip(owns, halos)
        ]
        gathered = [
            lax.all_to_all(x.reshape(parts, share, rows, atoms), "energy", 0, 0) for x in coupled
        ]
        mixed = [
            call(
                functools.partial(mix_kernel, fused),
                [x.shape],
                [pltpu.VMEM((total, share * atoms), jnp.float32)] * 2,
                2 * total * x.size,
                mixing if len(chains) == 1 else mixing[at * fused : (at + 1) * fused],
                x,
            )[0]
            for at, x in enumerate(gathered)
        ]
        sigma = [
            lax.all_to_all(x, "energy", 0, 0).reshape(parts * share, rows, atoms) for x in mixed
        ]
        if step < ITERS - 1:
            pieces = [
                call(
                    functools.partial(dress_between_kernel, rows),
                    [wide, (pairs, rows, atoms)],
                    [pltpu.VMEM(deep, jnp.float32)],
                    work,
                    x,
                    left,
                    right,
                    start,
                )
                for x, start in zip(sigma, frees)
            ]
            owns = [own for own, _ in pieces]
            halos = [(beside(compact),) for _, compact in pieces]
    outs = [
        call(
            functools.partial(dress_last_kernel, fused),
            [lesser_free.shape] * fused,
            [pltpu.VMEM(deep, jnp.float32), pltpu.VMEM((pairs * rows, atoms), jnp.float32)],
            work,
            x,
            left,
            right,
            *chain,
        )
        for x, chain in zip(sigma, chains)
    ]
    return tuple(g for chain in outs for g in chain)


def solution(mesh):
    placed = (
        P("energy", None, "slab"),
        P("energy", None, "slab"),
        P("energy", None, "slab"),
        P(None, None, "slab"),
        P(None, "slab"),
        P(),
        P(),
        P(),
    )
    return jax.shard_map(
        body,
        mesh=mesh,
        in_specs=placed,
        out_specs=(P("energy", None, "slab"), P("energy", None, "slab")),
        check_vma=False,
    )
```

```python
import functools

import jax
import jax.numpy as jnp
from jax import lax
from jax.experimental import pallas as pl
from jax.experimental.pallas import tpu as pltpu
from jax.sharding import PartitionSpec as P

NORB = 12
NB = 12
HW = 32
ITERS = 2
ROWS = 8
BLOCKED = 2

TOP_RANK = lax.Precision.HIGHEST
PARAMS = pltpu.CompilerParams(vmem_limit_bytes=24 * 1024 * 1024)
ALONE = pltpu.CompilerParams(vmem_limit_bytes=60 * 1024 * 1024)


def spread_rows(target, base, row, source, first, count):
    for at in range(0, count, ROWS):
        size = min(ROWS, count - at)
        rows = pl.ds((base + at) * ROWS + row, size, stride=ROWS)
        target[rows, :] = source(first + at, size)


def index_neighbours(rows, offsets, lanes, is_near, inside):
    atoms = offsets.shape[1]
    group = ROWS // rows
    slab, slabs = lax.axis_index("slab"), lax.axis_size("slab")
    targets = offsets[...] + lax.broadcasted_iota(jnp.int32, (NB, atoms), 1)
    placed = targets + slab * atoms
    inside[...] = ((placed >= 0) & (placed < slabs * atoms)).astype(jnp.float32)
    near = ((targets >= 0) & (targets < atoms)).astype(jnp.int32)
    lane = jnp.where(targets < 0, targets + atoms, targets)
    lane = jnp.where(lane >= atoms, lane - atoms, lane)
    for n in range(NB):
        some = slice(n % group * rows, (n % group + 1) * rows)
        lanes[n // group, some, :] = jnp.broadcast_to(lane[n : n + 1, :], (rows, atoms))
        is_near[n // group, some, :] = jnp.broadcast_to(near[n : n + 1, :], (rows, atoms))


def couple(rows, own, other, coupling, work, arrived, keep, aside):
    lanes, is_near, inside, links, gathered_a, gathered_b, total = work
    pairs = coupling.shape[1]
    group = ROWS // rows
    groups = NB // group
    steps = NORB // BLOCKED
    chunk = pairs // steps
    buffers = (gathered_a, gathered_b)

    def link(g, pair):
        at = (g * pairs + pair) * ROWS
        if not isinstance(at, int):
            at = pl.multiple_of(at, ROWS)
        return links[pl.ds(at, ROWS), :]

    def build(g, first, count):
        for n in range(g * group, (g + 1) * group):
            valid = inside[n : n + 1, :]
            for row in range(rows):
                spread_rows(
                    links,
                    g * pairs + first,
                    n % group * rows + row,
                    lambda at, size: coupling[n, pl.ds(at, size), :] * valid,
                    first,
                    count,
                )

    def gather(g, first, count):
        target = buffers[g % 2]
        lane, mine = lanes[g], is_near[g] != 0
        for at in range(count):
            pair = first + at
            rows_at = pl.ds(pl.multiple_of(pair * ROWS, ROWS), ROWS)
            inner = jnp.take_along_axis(own[rows_at, :], lane, axis=1, mode="promise_in_bounds")
            outer = jnp.take_along_axis(other[rows_at, :], lane, axis=1, mode="promise_in_bounds")
            target[pair] = jnp.where(mine, inner, outer)

    def ahead(g, step):
        first = pl.multiple_of(step * chunk, ROWS)
        gather(g, first, chunk)
        build(g, first, chunk)

    arrived(0)
    lax.fori_loop(0, steps, lambda step, _: ahead(0, step), None)
    for g in range(groups):
        source = buffers[g % 2]
        if g < groups - 1:
            arrived(g + 1)

        def block_row(step, _):
            first = step * BLOCKED
            inner = [[None] * NORB for _ in range(BLOCKED)]
            for j in range(NORB):
                left = [link(g, (first + b) * NORB + j) for b in range(BLOCKED)]
                for l in range(NORB):
                    value = source[j * NORB + l]
                    for b in range(BLOCKED):
                        term = left[b] * value
                        inner[b][l] = term if j == 0 else inner[b][l] + term
            for k in range(NORB):
                sums = [None] * BLOCKED
                for l in range(NORB):
                    right = link(g, k * NORB + l)
                    for b in range(BLOCKED):
                        term = inner[b][l] * right
                        sums[b] = term if l == 0 else sums[b] + term
                for b in range(BLOCKED):
                    at = (first + b) * NORB + k
                    value = sums[b] if g == 0 else total[at] + sums[b]
                    if g < groups - 1:
                        total[at] = value
                    else:
                        width = ROWS // 2
                        while width >= rows:
                            value = value + pltpu.roll(value, width, 0)
                            width //= 2
                        keep(at, value[:rows])
            if g < groups - 1:
                ahead(g + 1, step)
            else:
                aside(step, steps)

        lax.fori_loop(0, steps, block_row, None)


def first_kernel(*refs):
    far_hbm, free_hbm = refs[0:2], refs[2:4]
    retarded_hbm, coupling_hbm, offsets, shifts, coupled, occupied = refs[4:10]
    out_hbm, start_hbm, left_hbm, right_hbm, mixing_hbm = refs[10:15]
    out, start, left, right, mixing = refs[15:20]
    far, free, retarded, coupling, other = refs[20:25]
    work, (fetched, arriving, leaving, passing) = refs[25:32], refs[32:36]
    energies, pairs, atoms = retarded.shape
    rows = 2 * energies
    group = ROWS // rows
    copies = [pltpu.make_async_copy(free_hbm[f], free.at[f], fetched.at[f]) for f in range(2)]
    copies += [pltpu.make_async_copy(far_hbm[f], far.at[f], fetched.at[2 + f]) for f in range(2)]
    copies.append(pltpu.make_async_copy(retarded_hbm, retarded, fetched.at[4]))
    blocks = [
        pltpu.make_async_copy(coupling_hbm.at[n], coupling.at[n], arriving.at[n])
        for n in range(NB)
    ]
    for copy in copies[:4] + blocks + copies[4:]:
        copy.start()

    index_neighbours(rows, offsets, *work[:3])
    total = mixing.shape[1]
    gap = lax.broadcasted_iota(jnp.int32, (total, total), 1) - lax.broadcasted_iota(
        jnp.int32, (total, total), 0
    )
    lesser = jnp.zeros((total, total), jnp.float32)
    greater = jnp.zeros((total, total), jnp.float32)
    for mode in range(shifts.shape[0]):
        shift = shifts[mode]
        absorb = coupled[mode] * occupied[mode]
        emit = coupled[mode] * (occupied[mode] + 1.0)
        ahead = gap == shift
        behind = gap == -shift
        lesser = lesser + jnp.where(ahead, emit, jnp.where(behind, absorb, 0.0))
        greater = greater + jnp.where(ahead, absorb, jnp.where(behind, emit, 0.0))
    mixing[0] = lesser
    mixing[1] = greater

    for f in range(2):
        copies[f].wait()
        copies[2 + f].wait()
    for row in range(ROWS):
        function, energy = row % rows // energies, row % energies
        for target, sources in ((start, free), (other, far)):
            read = lambda at, size: sources[function, energy, at : at + size, :]
            spread_rows(target, 0, row, read, 0, pairs)
    copies[4].wait()
    share = left.shape[0] // ROWS

    def arrived(g):
        for n in range(g * group, (g + 1) * group):
            blocks[n].wait()

    def keep(at, value):
        out[at] = value

    def aside(step, steps):
        some = pl.ds(step * (pairs // steps), pairs // steps)
        pltpu.make_async_copy(out.at[some], out_hbm.at[some], leaving.at[step]).start()
        for row in range(ROWS):
            for target, count, skipped in (
                (left, share // steps, row // rows * share),
                (right, pairs // steps, 0),
            ):
                first = step * count
                read = lambda at, size: retarded[row % energies, pl.ds(skipped + at, size), :]
                spread_rows(target, first, row, read, first, count)

    couple(rows, start, other, coupling, work, arrived, keep, aside)
    sides = [
        pltpu.make_async_copy(held, target, passing.at[at])
        for at, (held, target) in enumerate(
            ((start, start_hbm), (left, left_hbm), (right, right_hbm), (mixing, mixing_hbm))
        )
    ]
    for side in sides:
        side.start()
    steps = NORB // BLOCKED
    for step in range(steps):
        some = pl.ds(step * (pairs // steps), pairs // steps)
        pltpu.make_async_copy(out.at[some], out_hbm.at[some], leaving.at[step]).wait()
    if out.shape[0] > pairs:
        for at in range(pairs, out.shape[0]):
            out[at] = jnp.zeros(out.shape[1:], jnp.float32)
        some = pl.ds(pairs, out.shape[0] - pairs)
        pltpu.make_async_copy(out.at[some], out_hbm.at[some], leaving.at[0]).start()
        pltpu.make_async_copy(out.at[some], out_hbm.at[some], leaving.at[0]).wait()
    for side in sides:
        side.wait()


def couple_kernel(rows, own, far, coupling, offsets, out, other, *work):
    pairs = coupling.shape[1]
    index_neighbours(rows, offsets, *work[:3])
    for pair in range(pairs):
        value = far[pair]
        for at in range(0, ROWS, rows):
            other[pair * ROWS + at : pair * ROWS + at + rows, :] = value

    def keep(at, value):
        out[at] = value

    couple(rows, own, other, coupling, work, lambda g: None, keep, lambda step, steps: None)
    for at in range(pairs, out.shape[0]):
        out[at] = jnp.zeros(out.shape[1:], jnp.float32)


def mix_kernel(fused, mixing, blocks, out, before, after):
    parts, share, rows, atoms = blocks.shape
    energies = rows // fused
    for f in range(fused):
        some = slice(f * energies, (f + 1) * energies)
        for part in range(parts):
            for pair in range(share):
                before[part * energies : (part + 1) * energies, pair * atoms : (pair + 1) * atoms] = (
                    blocks[part, pair, some, :]
                )
        after[...] = jnp.dot(
            mixing[f], before[...], precision=TOP_RANK, preferred_element_type=jnp.float32
        )
        for part in range(parts):
            for pair in range(share):
                out[part, pair, some, :] = after[
                    part * energies : (part + 1) * energies, pair * atoms : (pair + 1) * atoms
                ]


def dress(rows, sigma, left, right, copied, keep):
    parts = ROWS // rows
    for pair in range(NORB * NORB):
        value = sigma[pair]
        for part in range(parts):
            copied[pair, part * rows : (part + 1) * rows, :] = value
    for i in range(NORB // parts):
        inner = [None] * NORB
        for j in range(NORB):
            factor = left[i * NORB + j]
            for l in range(NORB):
                term = factor * copied[j * NORB + l]
                inner[l] = term if j == 0 else inner[l] + term
        for k in range(NORB):
            value = inner[0] * right[k * NORB]
            for l in range(1, NORB):
                value = value + inner[l] * right[k * NORB + l]
            keep(i * NORB + k, value)


def dress_between_kernel(rows, sigma, left, right, free, own, compact, copied):
    atoms = sigma.shape[2]
    share = left.shape[0]
    row_at = lax.broadcasted_iota(jnp.int32, (ROWS, atoms), 0)

    def keep(at, value):
        for part in range(ROWS // rows):
            held = (row_at >= part * rows) & (row_at < (part + 1) * rows)
            piece = jnp.where(held, value, 0.0)
            width = ROWS // 2
            while width >= rows:
                piece = piece + pltpu.roll(piece, width, 0)
                width //= 2
            pair = part * share + at
            piece = piece + free[pair * ROWS : (pair + 1) * ROWS, :]
            own[pair * ROWS : (pair + 1) * ROWS, :] = piece
            compact[pair] = piece[:rows]

    dress(rows, sigma, left, right, copied, keep)


def dress_last_kernel(*refs):
    sigma, left, right = refs[:3]
    free, out_hbm = refs[3:5], refs[5:7]
    copied, dressed, out, leaving = refs[7:]
    energies, pairs, _ = free[0].shape
    rows = 2 * energies
    parts = ROWS // rows
    share = left.shape[0]
    stage = 2 * NORB
    copies = []

    def keep(at, value):
        dressed[at * ROWS : (at + 1) * ROWS, :] = value
        if (at + 1) % stage and at + 1 < share:
            return
        done = at // stage * stage
        for row in range(ROWS):
            function, energy, part = row % rows // energies, row % energies, row // rows
            for begin in range(done, at + 1, ROWS):
                size = min(ROWS, at + 1 - begin)
                first = part * share + begin
                piece = dressed[pl.ds(begin * ROWS + row, size, stride=ROWS), :]
                out[function, energy, first : first + size, :] = (
                    free[function][energy, first : first + size, :] + piece
                )
        for function in range(2):
            for part in range(parts):
                some = pl.ds(part * share + done, at + 1 - done)
                copies.append(
                    pltpu.make_async_copy(
                        out.at[function, :, some, :],
                        out_hbm[function].at[:, some, :],
                        leaving.at[len(copies)],
                    )
                )
                copies[-1].start()

    dress(rows, sigma, left, right, copied, keep)
    for copy in copies:
        copy.wait()


def call(kernel, outs, scratch, flops, *operands, spaces=None, targets=None, params=PARAMS):
    shapes = [jax.ShapeDtypeStruct(x, jnp.float32) for x in outs]
    vmem = pl.BlockSpec(memory_space=pltpu.VMEM)
    moved = sum(x.size for x in operands) + sum(x.size for x in shapes)
    return pl.pallas_call(
        kernel,
        out_shape=shapes,
        in_specs=spaces or [vmem] * len(operands),
        out_specs=targets or [vmem] * len(shapes),
        scratch_shapes=scratch,
        compiler_params=params,
        cost_estimate=pl.CostEstimate(
            flops=flops, bytes_accessed=4 * moved, transcendentals=0
        ),
    )(*operands)


def beside(block):
    count = lax.axis_size("slab")
    if count == 2:
        return lax.ppermute(block, "slab", [(0, 1), (1, 0)])
    forward = [(i, i + 1) for i in range(count - 1)]
    backward = [(target, source) for source, target in forward]
    axis = block.ndim - 1
    atoms = block.shape[axis]
    low = lax.ppermute(lax.slice_in_dim(block, atoms - HW, atoms, axis=axis), "slab", forward)
    high = lax.ppermute(lax.slice_in_dim(block, 0, HW, axis=axis), "slab", backward)
    gap = jnp.zeros(block.shape[:-1] + (atoms - 2 * HW,), block.dtype)
    return jnp.concatenate([high, gap, low], axis=axis)


def body(
    lesser_free,
    greater_free,
    retarded,
    coupling,
    neighbour_offsets,
    phonon_shift,
    phonon_coupling,
    phonon_occupation,
):
    energies, pairs, atoms = lesser_free.shape
    rows = 2 * energies
    groups = NB * rows // ROWS
    parts = lax.axis_size("energy")
    share = -(-pairs // parts)
    total = energies * parts
    vmem = pl.BlockSpec(memory_space=pltpu.VMEM)
    smem = pl.BlockSpec(memory_space=pltpu.SMEM)
    away = pl.BlockSpec(memory_space=pltpu.HBM)
    held = lambda *dims: pltpu.VMEM(dims, jnp.float32)
    wide = (pairs * ROWS, atoms)
    deep = (pairs, ROWS, atoms)
    thin = (pairs * rows, atoms)
    every = (parts * share, rows, atoms)
    flops = 4 * NORB * rows * pairs * atoms
    index = pltpu.VMEM((groups, ROWS, atoms), jnp.int32)
    work = [index, index, held(NB, atoms), held(groups * pairs * ROWS, atoms)] + [held(*deep)] * 3
    transfer = lambda count: pltpu.SemaphoreType.DMA((count,))

    free = (lesser_free, greater_free)
    coupled, start, left, right, mixing = call(
        first_kernel,
        [every, wide, thin, wide, (2, total, total)],
        [held(*every), held(*wide), held(*thin), held(*wide), held(2, total, total)]
        + [held(2, *retarded.shape), held(2, *retarded.shape), held(*retarded.shape)]
        + [held(*coupling.shape), held(*wide)]
        + work
        + [transfer(5), transfer(NB), transfer(NORB // BLOCKED), transfer(4)],
        NB * flops,
        *(beside(g) for g in free),
        *free,
        retarded,
        coupling,
        neighbour_offsets,
        phonon_shift,
        phonon_coupling,
        phonon_occupation,
        spaces=[away] * 6 + [vmem] + [smem] * 3,
        targets=[away] * 5,
        params=ALONE,
    )
    left = left.reshape(pairs * rows // ROWS, ROWS, atoms)
    right = right.reshape(deep)

    for step in range(ITERS):
        if step > 0:
            own, compact = call(
                functools.partial(dress_between_kernel, rows),
                [wide, (pairs, rows, atoms)],
                [held(*deep)],
                flops,
                sigma,
                left,
                right,
                start,
            )
            (coupled,) = call(
                functools.partial(couple_kernel, rows),
                [every],
                [held(*wide)] + work,
                NB * flops,
                own,
                beside(compact),
                coupling,
                neighbour_offsets,
            )
        gathered = lax.all_to_all(coupled.reshape(parts, share, rows, atoms), "energy", 0, 0)
        (mixed,) = call(
            functools.partial(mix_kernel, 2),
            [gathered.shape],
            [held(total, share * atoms)] * 2,
            2 * total * gathered.size,
            mixing,
            gathered,
        )
        sigma = lax.all_to_all(mixed, "energy", 0, 0).reshape(every)
    stages = -(-thin[0] // (ROWS * 2 * NORB))
    return call(
        dress_last_kernel,
        [lesser_free.shape] * 2,
        [held(*deep), held(*thin), held(2, *lesser_free.shape)]
        + [transfer(stages * 2 * ROWS // rows)],
        flops,
        sigma,
        left,
        right,
        *free,
        targets=[away] * 2,
    )


def solution(mesh):
    placed = (
        P("energy", None, "slab"),
        P("energy", None, "slab"),
        P("energy", None, "slab"),
        P(None, None, "slab"),
        P(None, "slab"),
        P(),
        P(),
        P(),
    )
    return jax.shard_map(
        body,
        mesh=mesh,
        in_specs=placed,
        out_specs=(P("energy", None, "slab"), P("energy", None, "slab")),
        check_vma=False,
    )
```

```python
import functools

import jax
import jax.numpy as jnp
from jax import lax
from jax.experimental import pallas as pl
from jax.experimental.pallas import tpu as pltpu
from jax.sharding import PartitionSpec as P

NORB = 12
NB = 12
HW = 32
ITERS = 2
ROWS = 8
BLOCKED = 2

TOP_RANK = lax.Precision.HIGHEST
PARAMS = pltpu.CompilerParams(vmem_limit_bytes=24 * 1024 * 1024)
ALONE = pltpu.CompilerParams(vmem_limit_bytes=60 * 1024 * 1024)


def spread_rows(target, base, row, source, first, count):
    for at in range(0, count, ROWS):
        size = min(ROWS, count - at)
        rows = pl.ds((base + at) * ROWS + row, size, stride=ROWS)
        target[rows, :] = source(first + at, size)


def index_neighbours(rows, offsets, lanes, is_near, inside):
    atoms = offsets.shape[1]
    group = ROWS // rows
    slab, slabs = lax.axis_index("slab"), lax.axis_size("slab")
    targets = offsets[...] + lax.broadcasted_iota(jnp.int32, (NB, atoms), 1)
    placed = targets + slab * atoms
    inside[...] = ((placed >= 0) & (placed < slabs * atoms)).astype(jnp.float32)
    near = ((targets >= 0) & (targets < atoms)).astype(jnp.int32)
    lane = jnp.where(targets < 0, targets + atoms, targets)
    lane = jnp.where(lane >= atoms, lane - atoms, lane)
    for n in range(NB):
        some = slice(n % group * rows, (n % group + 1) * rows)
        lanes[n // group, some, :] = jnp.broadcast_to(lane[n : n + 1, :], (rows, atoms))
        is_near[n // group, some, :] = jnp.broadcast_to(near[n : n + 1, :], (rows, atoms))


def couple(rows, own, other, coupling, work, arrived, keep, aside):
    lanes, is_near, inside, links_a, links_b, gathered_a, gathered_b, total = work
    pairs = coupling.shape[1]
    group = ROWS // rows
    groups = NB // group
    steps = NORB // BLOCKED
    chunk = pairs // steps
    buffers, links = (gathered_a, gathered_b), (links_a, links_b)

    def link(g, pair):
        at = pair * ROWS
        if not isinstance(at, int):
            at = pl.multiple_of(at, ROWS)
        return links[g % 2][pl.ds(at, ROWS), :]

    def build(g, first, count):
        for n in range(g * group, (g + 1) * group):
            valid = inside[n : n + 1, :]
            for row in range(rows):
                spread_rows(
                    links[g % 2],
                    first,
                    n % group * rows + row,
                    lambda at, size: coupling[n, pl.ds(at, size), :] * valid,
                    first,
                    count,
                )

    def gather(g, first, count):
        target = buffers[g % 2]
        lane, mine = lanes[g], is_near[g] != 0
        for at in range(count):
            pair = first + at
            rows_at = pl.ds(pl.multiple_of(pair * ROWS, ROWS), ROWS)
            inner = jnp.take_along_axis(own[rows_at, :], lane, axis=1, mode="promise_in_bounds")
            outer = jnp.take_along_axis(other[rows_at, :], lane, axis=1, mode="promise_in_bounds")
            target[pair] = jnp.where(mine, inner, outer)

    def ahead(g, step):
        first = pl.multiple_of(step * chunk, ROWS)
        gather(g, first, chunk)
        build(g, first, chunk)

    arrived(0)
    lax.fori_loop(0, steps, lambda step, _: ahead(0, step), None)
    for g in range(groups):
        source = buffers[g % 2]
        if g < groups - 1:
            arrived(g + 1)

        def block_row(step, _):
            first = step * BLOCKED
            inner = [[None] * NORB for _ in range(BLOCKED)]
            for j in range(NORB):
                left = [link(g, (first + b) * NORB + j) for b in range(BLOCKED)]
                for l in range(NORB):
                    value = source[j * NORB + l]
                    for b in range(BLOCKED):
                        term = left[b] * value
                        inner[b][l] = term if j == 0 else inner[b][l] + term
            for k in range(NORB):
                sums = [None] * BLOCKED
                for l in range(NORB):
                    right = link(g, k * NORB + l)
                    for b in range(BLOCKED):
                        term = inner[b][l] * right
                        sums[b] = term if l == 0 else sums[b] + term
                for b in range(BLOCKED):
                    at = (first + b) * NORB + k
                    value = sums[b] if g == 0 else total[at] + sums[b]
                    if g < groups - 1:
                        total[at] = value
                    else:
                        width = ROWS // 2
                        while width >= rows:
                            value = value + pltpu.roll(value, width, 0)
                            width //= 2
                        keep(at, value[:rows])
            if g < groups - 1:
                ahead(g + 1, step)
            else:
                aside(step, steps)

        lax.fori_loop(0, steps, block_row, None)


def prep_kernel(*refs):
    free_hbm, retarded_hbm, shifts, coupled, occupied = refs[0:2], *refs[2:6]
    targets = refs[6:10]
    start, left, right, mixing = refs[10:14]
    free, retarded, fetched, passing = refs[14:18]
    energies, pairs, _ = retarded.shape
    rows = 2 * energies
    share = left.shape[0] // ROWS
    copies = [pltpu.make_async_copy(free_hbm[f], free.at[f], fetched.at[f]) for f in range(2)]
    copies.append(pltpu.make_async_copy(retarded_hbm, retarded, fetched.at[2]))
    for copy in copies:
        copy.start()
    sides = [
        pltpu.make_async_copy(held, target, passing.at[at])
        for at, (held, target) in enumerate(zip((start, left, right, mixing), targets))
    ]

    total = mixing.shape[1]
    gap = lax.broadcasted_iota(jnp.int32, (total, total), 1) - lax.broadcasted_iota(
        jnp.int32, (total, total), 0
    )
    lesser = jnp.zeros((total, total), jnp.float32)
    greater = jnp.zeros((total, total), jnp.float32)
    for mode in range(shifts.shape[0]):
        shift = shifts[mode]
        absorb = coupled[mode] * occupied[mode]
        emit = coupled[mode] * (occupied[mode] + 1.0)
        ahead = gap == shift
        behind = gap == -shift
        lesser = lesser + jnp.where(ahead, emit, jnp.where(behind, absorb, 0.0))
        greater = greater + jnp.where(ahead, absorb, jnp.where(behind, emit, 0.0))
    mixing[0] = lesser
    mixing[1] = greater
    sides[3].start()

    copies[0].wait()
    copies[1].wait()
    for row in range(ROWS):
        function, energy = row % rows // energies, row % energies
        read = lambda at, size: free[function, energy, at : at + size, :]
        spread_rows(start, 0, row, read, 0, pairs)
    sides[0].start()
    copies[2].wait()
    for row in range(ROWS):
        skipped = row // rows * share
        read = lambda at, size: retarded[row % energies, at : at + size, :]
        spread_rows(left, 0, row, read, skipped, share)
        spread_rows(right, 0, row, read, 0, pairs)
    sides[1].start()
    sides[2].start()
    for side in sides:
        side.wait()


def first_kernel(*refs):
    far_hbm, own_hbm, coupling_hbm, offsets, out_hbm = refs[0:2], *refs[2:6]
    out, own, far, coupling, other = refs[6:11]
    work, (fetched, arriving, leaving) = refs[11:19], refs[19:22]
    energies, pairs = far.shape[1:3]
    rows = 2 * energies
    group = ROWS // rows
    copies = [pltpu.make_async_copy(far_hbm[f], far.at[f], fetched.at[f]) for f in range(2)]
    copies.append(pltpu.make_async_copy(own_hbm, own, fetched.at[2]))
    blocks = [
        pltpu.make_async_copy(coupling_hbm.at[n], coupling.at[n], arriving.at[n])
        for n in range(NB)
    ]
    for copy in copies + blocks:
        copy.start()
    index_neighbours(rows, offsets, *work[:3])
    for copy in copies[:2]:
        copy.wait()
    for row in range(ROWS):
        function, energy = row % rows // energies, row % energies
        read = lambda at, size: far[function, energy, at : at + size, :]
        spread_rows(other, 0, row, read, 0, pairs)
    copies[2].wait()

    def arrived(g):
        for n in range(g * group, (g + 1) * group):
            blocks[n].wait()

    def keep(at, value):
        out[at] = value

    def leave(step, steps):
        some = pl.ds(step * (pairs // steps), pairs // steps)
        return pltpu.make_async_copy(out.at[some], out_hbm.at[some], leaving.at[step])

    couple(
        rows, own, other, coupling, work, arrived, keep, lambda step, steps: leave(step, steps).start()
    )
    steps = NORB // BLOCKED
    if out.shape[0] > pairs:
        for at in range(pairs, out.shape[0]):
            out[at] = jnp.zeros(out.shape[1:], jnp.float32)
        some = pl.ds(pairs, out.shape[0] - pairs)
        rest = pltpu.make_async_copy(out.at[some], out_hbm.at[some], leaving.at[steps])
        rest.start()
        rest.wait()
    for step in range(steps):
        leave(step, steps).wait()


def couple_kernel(rows, own, far, coupling, offsets, out, other, *work):
    pairs = coupling.shape[1]
    index_neighbours(rows, offsets, *work[:3])
    for pair in range(pairs):
        value = far[pair]
        for at in range(0, ROWS, rows):
            other[pair * ROWS + at : pair * ROWS + at + rows, :] = value

    def keep(at, value):
        out[at] = value

    couple(rows, own, other, coupling, work, lambda g: None, keep, lambda step, steps: None)
    for at in range(pairs, out.shape[0]):
        out[at] = jnp.zeros(out.shape[1:], jnp.float32)


def mix_kernel(fused, mixing, blocks, out, before, after):
    parts, share, rows, atoms = blocks.shape
    energies = rows // fused
    for f in range(fused):
        some = slice(f * energies, (f + 1) * energies)
        for part in range(parts):
            for pair in range(share):
                before[part * energies : (part + 1) * energies, pair * atoms : (pair + 1) * atoms] = (
                    blocks[part, pair, some, :]
                )
        after[...] = jnp.dot(
            mixing[f], before[...], precision=TOP_RANK, preferred_element_type=jnp.float32
        )
        for part in range(parts):
            for pair in range(share):
                out[part, pair, some, :] = after[
                    part * energies : (part + 1) * energies, pair * atoms : (pair + 1) * atoms
                ]


def dress(rows, sigma, left, right, copied, keep):
    parts = ROWS // rows
    for pair in range(NORB * NORB):
        value = sigma[pair]
        for part in range(parts):
            copied[pair, part * rows : (part + 1) * rows, :] = value
    for i in range(NORB // parts):
        inner = [None] * NORB
        for j in range(NORB):
            factor = left[i * NORB + j]
            for l in range(NORB):
                term = factor * copied[j * NORB + l]
                inner[l] = term if j == 0 else inner[l] + term
        for k in range(NORB):
            value = inner[0] * right[k * NORB]
            for l in range(1, NORB):
                value = value + inner[l] * right[k * NORB + l]
            keep(i * NORB + k, value)


def dress_between_kernel(rows, sigma, left, right, free, own, compact, copied):
    atoms = sigma.shape[2]
    share = left.shape[0]
    row_at = lax.broadcasted_iota(jnp.int32, (ROWS, atoms), 0)

    def keep(at, value):
        for part in range(ROWS // rows):
            held = (row_at >= part * rows) & (row_at < (part + 1) * rows)
            piece = jnp.where(held, value, 0.0)
            width = ROWS // 2
            while width >= rows:
                piece = piece + pltpu.roll(piece, width, 0)
                width //= 2
            pair = part * share + at
            piece = piece + free[pair * ROWS : (pair + 1) * ROWS, :]
            own[pair * ROWS : (pair + 1) * ROWS, :] = piece
            compact[pair] = piece[:rows]

    dress(rows, sigma, left, right, copied, keep)


def dress_last_kernel(*refs):
    sigma, left, right = refs[:3]
    free, out_hbm = refs[3:5], refs[5:7]
    copied, dressed, out, leaving = refs[7:]
    energies, pairs, _ = free[0].shape
    rows = 2 * energies
    parts = ROWS // rows
    share = left.shape[0]
    stage = 2 * NORB
    copies = []

    def keep(at, value):
        dressed[at * ROWS : (at + 1) * ROWS, :] = value
        if (at + 1) % stage and at + 1 < share:
            return
        done = at // stage * stage
        for row in range(ROWS):
            function, energy, part = row % rows // energies, row % energies, row // rows
            for begin in range(done, at + 1, ROWS):
                size = min(ROWS, at + 1 - begin)
                first = part * share + begin
                piece = dressed[pl.ds(begin * ROWS + row, size, stride=ROWS), :]
                out[function, energy, first : first + size, :] = (
                    free[function][energy, first : first + size, :] + piece
                )
        for function in range(2):
            for part in range(parts):
                some = pl.ds(part * share + done, at + 1 - done)
                copies.append(
                    pltpu.make_async_copy(
                        out.at[function, :, some, :],
                        out_hbm[function].at[:, some, :],
                        leaving.at[len(copies)],
                    )
                )
                copies[-1].start()

    dress(rows, sigma, left, right, copied, keep)
    for copy in copies:
        copy.wait()


def call(kernel, outs, scratch, flops, *operands, spaces=None, targets=None, params=PARAMS):
    shapes = [jax.ShapeDtypeStruct(x, jnp.float32) for x in outs]
    vmem = pl.BlockSpec(memory_space=pltpu.VMEM)
    moved = sum(x.size for x in operands) + sum(x.size for x in shapes)
    return pl.pallas_call(
        kernel,
        out_shape=shapes,
        in_specs=spaces or [vmem] * len(operands),
        out_specs=targets or [vmem] * len(shapes),
        scratch_shapes=scratch,
        compiler_params=params,
        cost_estimate=pl.CostEstimate(
            flops=flops, bytes_accessed=4 * moved, transcendentals=0
        ),
    )(*operands)


def beside(block):
    count = lax.axis_size("slab")
    if count == 2:
        return lax.ppermute(block, "slab", [(0, 1), (1, 0)])
    forward = [(i, i + 1) for i in range(count - 1)]
    backward = [(target, source) for source, target in forward]
    axis = block.ndim - 1
    atoms = block.shape[axis]
    low = lax.ppermute(lax.slice_in_dim(block, atoms - HW, atoms, axis=axis), "slab", forward)
    high = lax.ppermute(lax.slice_in_dim(block, 0, HW, axis=axis), "slab", backward)
    gap = jnp.zeros(block.shape[:-1] + (atoms - 2 * HW,), block.dtype)
    return jnp.concatenate([high, gap, low], axis=axis)


def body(
    lesser_free,
    greater_free,
    retarded,
    coupling,
    neighbour_offsets,
    phonon_shift,
    phonon_coupling,
    phonon_occupation,
):
    energies, pairs, atoms = lesser_free.shape
    rows = 2 * energies
    groups = NB * rows // ROWS
    parts = lax.axis_size("energy")
    share = -(-pairs // parts)
    total = energies * parts
    vmem = pl.BlockSpec(memory_space=pltpu.VMEM)
    smem = pl.BlockSpec(memory_space=pltpu.SMEM)
    away = pl.BlockSpec(memory_space=pltpu.HBM)
    held = lambda *dims: pltpu.VMEM(dims, jnp.float32)
    wide = (pairs * ROWS, atoms)
    deep = (pairs, ROWS, atoms)
    thin = (pairs * rows, atoms)
    every = (parts * share, rows, atoms)
    flops = 4 * NORB * rows * pairs * atoms
    index = pltpu.VMEM((groups, ROWS, atoms), jnp.int32)
    work = [index, index, held(NB, atoms)] + [held(*wide)] * 2 + [held(*deep)] * 3
    transfer = lambda count: pltpu.SemaphoreType.DMA((count,))

    free = (lesser_free, greater_free)
    halos = [beside(g) for g in free]
    start, left, right, mixing = call(
        prep_kernel,
        [wide, thin, wide, (2, total, total)],
        [held(*wide), held(*thin), held(*wide), held(2, total, total)]
        + [held(2, *retarded.shape), held(*retarded.shape), transfer(3), transfer(4)],
        4 * ROWS * retarded.size,
        *free,
        retarded,
        phonon_shift,
        phonon_coupling,
        phonon_occupation,
        spaces=[away] * 3 + [smem] * 3,
        targets=[away] * 4,
        params=ALONE,
    )
    (coupled,) = call(
        first_kernel,
        [every],
        [held(*every), held(*wide), held(2, *retarded.shape), held(*coupling.shape), held(*wide)]
        + work
        + [transfer(3), transfer(NB), transfer(NORB // BLOCKED + 1)],
        NB * flops,
        *halos,
        start,
        coupling,
        neighbour_offsets,
        spaces=[pl.BlockSpec(memory_space=pl.ANY)] * 2 + [away] * 2 + [vmem],
        targets=[away],
        params=ALONE,
    )
    left = left.reshape(pairs * rows // ROWS, ROWS, atoms)
    right = right.reshape(deep)

    for step in range(ITERS):
        if step > 0:
            own, compact = call(
                functools.partial(dress_between_kernel, rows),
                [wide, (pairs, rows, atoms)],
                [held(*deep)],
                flops,
                sigma,
                left,
                right,
                start,
            )
            (coupled,) = call(
                functools.partial(couple_kernel, rows),
                [every],
                [held(*wide)] + work,
                NB * flops,
                own,
                beside(compact),
                coupling,
                neighbour_offsets,
            )
        gathered = lax.all_to_all(coupled.reshape(parts, share, rows, atoms), "energy", 0, 0)
        (mixed,) = call(
            functools.partial(mix_kernel, 2),
            [gathered.shape],
            [held(total, share * atoms)] * 2,
            2 * total * gathered.size,
            mixing,
            gathered,
        )
        sigma = lax.all_to_all(mixed, "energy", 0, 0).reshape(every)
    stages = -(-thin[0] // (ROWS * 2 * NORB))
    return call(
        dress_last_kernel,
        [lesser_free.shape] * 2,
        [held(*deep), held(*thin), held(2, *lesser_free.shape)]
        + [transfer(stages * 2 * ROWS // rows)],
        flops,
        sigma,
        left,
        right,
        *free,
        targets=[away] * 2,
    )


def solution(mesh):
    placed = (
        P("energy", None, "slab"),
        P("energy", None, "slab"),
        P("energy", None, "slab"),
        P(None, None, "slab"),
        P(None, "slab"),
        P(),
        P(),
        P(),
    )
    return jax.shard_map(
        body,
        mesh=mesh,
        in_specs=placed,
        out_specs=(P("energy", None, "slab"), P("energy", None, "slab")),
        check_vma=False,
    )
```

```python
import functools

import jax
import jax.numpy as jnp
from jax import lax
from jax.experimental import pallas as pl
from jax.experimental.pallas import tpu as pltpu
from jax.sharding import PartitionSpec as P

NORB = 12
NB = 12
HW = 32
ITERS = 2
ROWS = 8
BLOCKED = 2

TOP_RANK = lax.Precision.HIGHEST
PARAMS = pltpu.CompilerParams(vmem_limit_bytes=24 * 1024 * 1024)


def spread_rows(target, base, row, source, first, count):
    for at in range(0, count, ROWS):
        size = min(ROWS, count - at)
        rows = pl.ds((base + at) * ROWS + row, size, stride=ROWS)
        target[rows, :] = source(first + at, size)


def index_neighbours(rows, offsets, lanes, is_near, inside):
    atoms = offsets.shape[1]
    group = ROWS // rows
    slab, slabs = lax.axis_index("slab"), lax.axis_size("slab")
    targets = offsets[...] + lax.broadcasted_iota(jnp.int32, (NB, atoms), 1)
    placed = targets + slab * atoms
    inside[...] = ((placed >= 0) & (placed < slabs * atoms)).astype(jnp.float32)
    near = ((targets >= 0) & (targets < atoms)).astype(jnp.int32)
    lane = jnp.where(targets < 0, targets + atoms, targets)
    lane = jnp.where(lane >= atoms, lane - atoms, lane)
    for n in range(NB):
        some = slice(n % group * rows, (n % group + 1) * rows)
        lanes[n // group, some, :] = jnp.broadcast_to(lane[n : n + 1, :], (rows, atoms))
        is_near[n // group, some, :] = jnp.broadcast_to(near[n : n + 1, :], (rows, atoms))


def couple(rows, own, other, coupling, work, keep):
    lanes, is_near, inside, links_a, links_b, gathered_a, gathered_b, total = work
    pairs = coupling.shape[1]
    group = ROWS // rows
    groups = NB // group
    steps = NORB // BLOCKED
    chunk = pairs // steps
    buffers, links = (gathered_a, gathered_b), (links_a, links_b)

    def link(g, pair):
        at = pair * ROWS
        if not isinstance(at, int):
            at = pl.multiple_of(at, ROWS)
        return links[g % 2][pl.ds(at, ROWS), :]

    def build(g, first, count):
        for n in range(g * group, (g + 1) * group):
            valid = inside[n : n + 1, :]
            for row in range(rows):
                spread_rows(
                    links[g % 2],
                    first,
                    n % group * rows + row,
                    lambda at, size: coupling[n, pl.ds(at, size), :] * valid,
                    first,
                    count,
                )

    def gather(g, first, count):
        target = buffers[g % 2]
        lane, mine = lanes[g], is_near[g] != 0
        for at in range(count):
            pair = first + at
            rows_at = pl.ds(pl.multiple_of(pair * ROWS, ROWS), ROWS)
            inner = jnp.take_along_axis(own[rows_at, :], lane, axis=1, mode="promise_in_bounds")
            outer = jnp.take_along_axis(other[rows_at, :], lane, axis=1, mode="promise_in_bounds")
            target[pair] = jnp.where(mine, inner, outer)

    def ahead(g, step):
        first = pl.multiple_of(step * chunk, ROWS)
        gather(g, first, chunk)
        build(g, first, chunk)

    lax.fori_loop(0, steps, lambda step, _: ahead(0, step), None)
    for g in range(groups):
        source = buffers[g % 2]

        def block_row(step, _):
            first = step * BLOCKED
            inner = [[None] * NORB for _ in range(BLOCKED)]
            for j in range(NORB):
                left = [link(g, (first + b) * NORB + j) for b in range(BLOCKED)]
                for l in range(NORB):
                    value = source[j * NORB + l]
                    for b in range(BLOCKED):
                        term = left[b] * value
                        inner[b][l] = term if j == 0 else inner[b][l] + term
            for k in range(NORB):
                sums = [None] * BLOCKED
                for l in range(NORB):
                    right = link(g, k * NORB + l)
                    for b in range(BLOCKED):
                        term = inner[b][l] * right
                        sums[b] = term if l == 0 else sums[b] + term
                for b in range(BLOCKED):
                    at = (first + b) * NORB + k
                    value = sums[b] if g == 0 else total[at] + sums[b]
                    if g < groups - 1:
                        total[at] = value
                    else:
                        width = ROWS // 2
                        while width >= rows:
                            value = value + pltpu.roll(value, width, 0)
                            width //= 2
                        keep(at, value[:rows])
            if g < groups - 1:
                ahead(g + 1, step)

        lax.fori_loop(0, steps, block_row, None)


def prep_kernel(*refs):
    free_hbm, retarded_hbm, modes_hbm, coupling_hbm = refs[0:2], refs[2], refs[3:6], refs[6]
    start, left, right, mixing, coupling = refs[7:12]
    free, retarded, shifts, coupled, occupied, sems = refs[12:]
    energies, pairs, _ = retarded.shape
    rows = 2 * energies
    share = left.shape[0] // ROWS
    moves = [(free_hbm[f], free.at[f]) for f in range(2)] + [(retarded_hbm, retarded)]
    moves += list(zip(modes_hbm, (shifts, coupled, occupied))) + [(coupling_hbm, coupling)]
    copies = [
        pltpu.make_async_copy(source, target, sems.at[at])
        for at, (source, target) in enumerate(moves)
    ]
    for copy in copies:
        copy.start()

    copies[0].wait()
    copies[1].wait()
    for row in range(ROWS):
        function, energy = row % rows // energies, row % energies
        read = lambda at, size: free[function, energy, at : at + size, :]
        spread_rows(start, 0, row, read, 0, pairs)
    copies[2].wait()
    for row in range(ROWS):
        skipped = row // rows * share
        read = lambda at, size: retarded[row % energies, at : at + size, :]
        spread_rows(left, 0, row, read, skipped, share)
        spread_rows(right, 0, row, read, 0, pairs)
    for copy in copies[3:6]:
        copy.wait()
    total = mixing.shape[1]
    gap = lax.broadcasted_iota(jnp.int32, (total, total), 1) - lax.broadcasted_iota(
        jnp.int32, (total, total), 0
    )
    lesser = jnp.zeros((total, total), jnp.float32)
    greater = jnp.zeros((total, total), jnp.float32)
    for mode in range(shifts.shape[0]):
        shift = shifts[mode]
        absorb = coupled[mode] * occupied[mode]
        emit = coupled[mode] * (occupied[mode] + 1.0)
        ahead = gap == shift
        behind = gap == -shift
        lesser = lesser + jnp.where(ahead, emit, jnp.where(behind, absorb, 0.0))
        greater = greater + jnp.where(ahead, absorb, jnp.where(behind, emit, 0.0))
    mixing[0] = lesser
    mixing[1] = greater
    copies[6].wait()


def couple_kernel(rows, own, *refs):
    far, (coupling, offsets, out, other, *work) = refs[:-12], refs[-12:]
    pairs = coupling.shape[1]
    index_neighbours(rows, offsets, *work[:3])
    if len(far) == 1:
        for pair in range(pairs):
            value = far[0][pair]
            for at in range(0, ROWS, rows):
                other[pair * ROWS + at : pair * ROWS + at + rows, :] = value
    else:
        energies = rows // len(far)
        for row in range(ROWS):
            source = far[row % rows // energies]
            read = lambda at, size: source[row % energies, at : at + size, :]
            spread_rows(other, 0, row, read, 0, pairs)

    def keep(at, value):
        out[at] = value

    couple(rows, own, other, coupling, work, keep)
    for at in range(pairs, out.shape[0]):
        out[at] = jnp.zeros(out.shape[1:], jnp.float32)


def mix_kernel(fused, mixing, blocks, out, before, after):
    parts, share, rows, atoms = blocks.shape
    energies = rows // fused
    for f in range(fused):
        some = slice(f * energies, (f + 1) * energies)
        for part in range(parts):
            for pair in range(share):
                before[part * energies : (part + 1) * energies, pair * atoms : (pair + 1) * atoms] = (
                    blocks[part, pair, some, :]
                )
        after[...] = jnp.dot(
            mixing[f], before[...], precision=TOP_RANK, preferred_element_type=jnp.float32
        )
        for part in range(parts):
            for pair in range(share):
                out[part, pair, some, :] = after[
                    part * energies : (part + 1) * energies, pair * atoms : (pair + 1) * atoms
                ]


def dress(rows, sigma, left, right, copied, keep):
    parts = ROWS // rows
    for pair in range(NORB * NORB):
        value = sigma[pair]
        for part in range(parts):
            copied[pair, part * rows : (part + 1) * rows, :] = value
    for i in range(NORB // parts):
        inner = [None] * NORB
        for j in range(NORB):
            factor = left[i * NORB + j]
            for l in range(NORB):
                term = factor * copied[j * NORB + l]
                inner[l] = term if j == 0 else inner[l] + term
        for k in range(NORB):
            value = inner[0] * right[k * NORB]
            for l in range(1, NORB):
                value = value + inner[l] * right[k * NORB + l]
            keep(i * NORB + k, value)


def dress_between_kernel(rows, sigma, left, right, free, own, compact, copied):
    atoms = sigma.shape[2]
    share = left.shape[0]
    row_at = lax.broadcasted_iota(jnp.int32, (ROWS, atoms), 0)

    def keep(at, value):
        for part in range(ROWS // rows):
            held = (row_at >= part * rows) & (row_at < (part + 1) * rows)
            piece = jnp.where(held, value, 0.0)
            width = ROWS // 2
            while width >= rows:
                piece = piece + pltpu.roll(piece, width, 0)
                width //= 2
            pair = part * share + at
            piece = piece + free[pair * ROWS : (pair + 1) * ROWS, :]
            own[pair * ROWS : (pair + 1) * ROWS, :] = piece
            compact[pair] = piece[:rows]

    dress(rows, sigma, left, right, copied, keep)


def dress_last_kernel(*refs):
    sigma, left, right = refs[:3]
    free, out_hbm = refs[3:5], refs[5:7]
    copied, dressed, out, leaving = refs[7:]
    energies, pairs, _ = free[0].shape
    rows = 2 * energies
    parts = ROWS // rows
    share = left.shape[0]
    stage = 2 * NORB
    copies = []

    def keep(at, value):
        dressed[at * ROWS : (at + 1) * ROWS, :] = value
        if (at + 1) % stage and at + 1 < share:
            return
        done = at // stage * stage
        for row in range(ROWS):
            function, energy, part = row % rows // energies, row % energies, row // rows
            for begin in range(done, at + 1, ROWS):
                size = min(ROWS, at + 1 - begin)
                first = part * share + begin
                piece = dressed[pl.ds(begin * ROWS + row, size, stride=ROWS), :]
                out[function, energy, first : first + size, :] = (
                    free[function][energy, first : first + size, :] + piece
                )
        for function in range(2):
            for part in range(parts):
                some = pl.ds(part * share + done, at + 1 - done)
                copies.append(
                    pltpu.make_async_copy(
                        out.at[function, :, some, :],
                        out_hbm[function].at[:, some, :],
                        leaving.at[len(copies)],
                    )
                )
                copies[-1].start()

    dress(rows, sigma, left, right, copied, keep)
    for copy in copies:
        copy.wait()


def call(kernel, outs, scratch, flops, *operands, spaces=None, targets=None):
    shapes = [jax.ShapeDtypeStruct(x, jnp.float32) for x in outs]
    vmem = pl.BlockSpec(memory_space=pltpu.VMEM)
    moved = sum(x.size for x in operands) + sum(x.size for x in shapes)
    return pl.pallas_call(
        kernel,
        out_shape=shapes,
        in_specs=spaces or [vmem] * len(operands),
        out_specs=targets or [vmem] * len(shapes),
        scratch_shapes=scratch,
        compiler_params=PARAMS,
        cost_estimate=pl.CostEstimate(
            flops=flops, bytes_accessed=4 * moved, transcendentals=0
        ),
    )(*operands)


def beside(block):
    count = lax.axis_size("slab")
    if count == 2:
        return lax.ppermute(block, "slab", [(0, 1), (1, 0)])
    forward = [(i, i + 1) for i in range(count - 1)]
    backward = [(target, source) for source, target in forward]
    axis = block.ndim - 1
    atoms = block.shape[axis]
    low = lax.ppermute(lax.slice_in_dim(block, atoms - HW, atoms, axis=axis), "slab", forward)
    high = lax.ppermute(lax.slice_in_dim(block, 0, HW, axis=axis), "slab", backward)
    gap = jnp.zeros(block.shape[:-1] + (atoms - 2 * HW,), block.dtype)
    return jnp.concatenate([high, gap, low], axis=axis)


def body(
    lesser_free,
    greater_free,
    retarded,
    coupling,
    neighbour_offsets,
    phonon_shift,
    phonon_coupling,
    phonon_occupation,
):
    energies, pairs, atoms = lesser_free.shape
    rows = 2 * energies
    groups = NB * rows // ROWS
    parts = lax.axis_size("energy")
    share = -(-pairs // parts)
    total = energies * parts
    away = pl.BlockSpec(memory_space=pltpu.HBM)
    held = lambda *dims: pltpu.VMEM(dims, jnp.float32)
    wide = (pairs * ROWS, atoms)
    deep = (pairs, ROWS, atoms)
    thin = (pairs * rows, atoms)
    every = (parts * share, rows, atoms)
    flops = 4 * NORB * rows * pairs * atoms
    index = pltpu.VMEM((groups, ROWS, atoms), jnp.int32)
    work = [index, index, held(NB, atoms)] + [held(*wide)] * 2 + [held(*deep)] * 3
    transfer = lambda count: pltpu.SemaphoreType.DMA((count,))

    free = (lesser_free, greater_free)
    halos = [beside(g) for g in free]
    phonons = (phonon_shift, phonon_coupling, phonon_occupation)
    own, left, right, mixing, links = call(
        prep_kernel,
        [wide, thin, wide, (2, total, total), coupling.shape],
        [held(2, *retarded.shape), held(*retarded.shape)]
        + [pltpu.SMEM(x.shape, x.dtype) for x in phonons]
        + [transfer(7)],
        4 * ROWS * retarded.size,
        *(
            pltpu.with_memory_space_constraint(x, pltpu.HBM)
            for x in (*free, retarded, *phonons, coupling)
        ),
        spaces=[away] * 7,
    )
    start = own
    left = left.reshape(pairs * rows // ROWS, ROWS, atoms)
    right = right.reshape(deep)

    for step in range(ITERS):
        if step > 0:
            own, compact = call(
                functools.partial(dress_between_kernel, rows),
                [wide, (pairs, rows, atoms)],
                [held(*deep)],
                flops,
                sigma,
                left,
                right,
                start,
            )
            halos = [beside(compact)]
        (coupled,) = call(
            functools.partial(couple_kernel, rows),
            [every],
            [held(*wide)] + work,
            NB * flops,
            own,
            *halos,
            links,
            neighbour_offsets,
        )
        gathered = lax.all_to_all(coupled.reshape(parts, share, rows, atoms), "energy", 0, 0)
        (mixed,) = call(
            functools.partial(mix_kernel, 2),
            [gathered.shape],
            [held(total, share * atoms)] * 2,
            2 * total * gathered.size,
            mixing,
            gathered,
        )
        sigma = lax.all_to_all(mixed, "energy", 0, 0).reshape(every)
    stages = -(-thin[0] // (ROWS * 2 * NORB))
    return call(
        dress_last_kernel,
        [lesser_free.shape] * 2,
        [held(*deep), held(*thin), held(2, *lesser_free.shape)]
        + [transfer(stages * 2 * ROWS // rows)],
        flops,
        sigma,
        left,
        right,
        *free,
        targets=[away] * 2,
    )


def solution(mesh):
    placed = (
        P("energy", None, "slab"),
        P("energy", None, "slab"),
        P("energy", None, "slab"),
        P(None, None, "slab"),
        P(None, "slab"),
        P(),
        P(),
        P(),
    )
    return jax.shard_map(
        body,
        mesh=mesh,
        in_specs=placed,
        out_specs=(P("energy", None, "slab"), P("energy", None, "slab")),
        check_vma=False,
    )
```

```python
import functools

import jax
import jax.numpy as jnp
from jax import lax
from jax.experimental import pallas as pl
from jax.experimental.pallas import tpu as pltpu
from jax.sharding import PartitionSpec as P

NORB = 12
NB = 12
HW = 32
ITERS = 2
ROWS = 8
LANES = 128

TOP_RANK = lax.Precision.HIGHEST
PARAMS = pltpu.CompilerParams(vmem_limit_bytes=24 * 1024 * 1024)


def spread_rows(target, base, row, source, first, count):
    for at in range(0, count, ROWS):
        size = min(ROWS, count - at)
        rows = pl.ds((base + at) * ROWS + row, size, stride=ROWS)
        target[rows, :] = source(first + at, size)


def index_neighbours(rows, offsets, lanes, is_near, inside):
    atoms = offsets.shape[1]
    group = ROWS // rows
    slab, slabs = lax.axis_index("slab"), lax.axis_size("slab")
    targets = offsets[...] + lax.broadcasted_iota(jnp.int32, (NB, atoms), 1)
    placed = targets + slab * atoms
    inside[...] = ((placed >= 0) & (placed < slabs * atoms)).astype(jnp.float32)
    near = ((targets >= 0) & (targets < atoms)).astype(jnp.int32)
    lane = jnp.where(targets < 0, targets + atoms, targets)
    lane = jnp.where(lane >= atoms, lane - atoms, lane)
    for n in range(NB):
        some = slice(n % group * rows, (n % group + 1) * rows)
        lanes[n // group, some, :] = jnp.broadcast_to(lane[n : n + 1, :], (rows, atoms))
        is_near[n // group, some, :] = jnp.broadcast_to(near[n : n + 1, :], (rows, atoms))


def couple(rows, blocked, unroll, own, other, lanes, is_near, links, work, keep):
    gathered_a, gathered_b, total = work
    groups = NB * rows // ROWS
    pairs = total.shape[0]
    steps = NORB // blocked
    chunk = pairs // steps
    buffers = (gathered_a, gathered_b)

    def gather(g, first, count):
        target = buffers[g % 2]
        lane, mine = lanes[g], is_near[g] != 0
        for at in range(count):
            pair = first + at
            rows_at = pl.ds(pl.multiple_of(pair * ROWS, ROWS), ROWS)
            inner = jnp.take_along_axis(own[rows_at, :], lane, axis=1, mode="promise_in_bounds")
            outer = jnp.take_along_axis(other[rows_at, :], lane, axis=1, mode="promise_in_bounds")
            target[pair] = jnp.where(mine, inner, outer)

    lax.fori_loop(0, steps, lambda step, _: gather(0, step * chunk, chunk), None)
    for g in range(groups):
        source = buffers[g % 2]

        def block_row(step, _):
            first = step * blocked
            inner = [[None] * NORB for _ in range(blocked)]
            for j in range(NORB):
                left = [links[g, (first + b) * NORB + j] for b in range(blocked)]
                for l in range(NORB):
                    value = source[j * NORB + l]
                    for b in range(blocked):
                        term = left[b] * value
                        inner[b][l] = term if j == 0 else inner[b][l] + term
            for k in range(NORB):
                sums = [None] * blocked
                for l in range(NORB):
                    right = links[g, k * NORB + l]
                    for b in range(blocked):
                        term = inner[b][l] * right
                        sums[b] = term if l == 0 else sums[b] + term
                for b in range(blocked):
                    at = (first + b) * NORB + k
                    value = sums[b] if g == 0 else total[at] + sums[b]
                    if g < groups - 1:
                        total[at] = value
                    else:
                        width = ROWS // 2
                        while width >= rows:
                            value = value + pltpu.roll(value, width, 0)
                            width //= 2
                        keep(at, value[:rows])
            if g < groups - 1:
                gather(g + 1, step * chunk, chunk)

        lax.fori_loop(0, steps, block_row, None, unroll=unroll)


def mix_weights(mixing, shifts, coupled, occupied):
    total = mixing.shape[1]
    lane = lax.broadcasted_iota(jnp.int32, (ROWS, LANES), 1)
    row = lax.broadcasted_iota(jnp.int32, (ROWS, LANES), 0)
    emitted = jnp.zeros((ROWS, LANES), jnp.float32)
    absorbed = jnp.zeros((ROWS, LANES), jnp.float32)
    for mode in range(shifts.shape[0]):
        hit = lane == shifts[mode]
        absorb = coupled[mode] * occupied[mode]
        emit = coupled[mode] * (occupied[mode] + 1.0)
        emitted = emitted + jnp.where(hit, emit, 0.0)
        absorbed = absorbed + jnp.where(hit, absorb, 0.0)
    for at in range(0, total, ROWS):
        for first in range(0, total, LANES):
            width = min(LANES, total - first)
            gap = lane + first - (row + at)
            far = jnp.minimum(jnp.abs(gap), LANES - 1)
            emit = jnp.take_along_axis(emitted, far, axis=1, mode="promise_in_bounds")
            absorb = jnp.take_along_axis(absorbed, far, axis=1, mode="promise_in_bounds")
            some = slice(first, first + width)
            mixing[0, at : at + ROWS, some] = jnp.where(gap > 0, emit, absorb)[:, :width]
            mixing[1, at : at + ROWS, some] = jnp.where(gap > 0, absorb, emit)[:, :width]


def prep_kernel(*refs):
    free_hbm, retarded_hbm, modes_hbm = refs[0:2], refs[2], refs[3:6]
    offsets_hbm, coupling_hbm = refs[6:8]
    start, left, right, mixing, links, lanes, is_near = refs[8:15]
    free, retarded, shifts, coupled, occupied, offsets, coupling, inside, sems = refs[15:]
    energies, pairs, _ = retarded.shape
    rows = 2 * energies
    group = ROWS // rows
    share = left.shape[0] // ROWS
    moves = [(free_hbm[f], free.at[f]) for f in range(2)] + [(retarded_hbm, retarded)]
    moves += list(zip(modes_hbm, (shifts, coupled, occupied))) + [(offsets_hbm, offsets)]
    moves += [(coupling_hbm.at[n], coupling.at[n]) for n in range(NB)]
    copies = [
        pltpu.make_async_copy(source, target, sems.at[at])
        for at, (source, target) in enumerate(moves)
    ]
    for copy in copies:
        copy.start()

    copies[0].wait()
    copies[1].wait()
    for row in range(ROWS):
        function, energy = row % rows // energies, row % energies
        read = lambda at, size: free[function, energy, at : at + size, :]
        spread_rows(start, 0, row, read, 0, pairs)
    copies[2].wait()
    for row in range(ROWS):
        skipped = row // rows * share
        read = lambda at, size: retarded[row % energies, at : at + size, :]
        spread_rows(left, 0, row, read, skipped, share)
        spread_rows(right, 0, row, read, 0, pairs)
    for copy in copies[3:7]:
        copy.wait()
    mix_weights(mixing, shifts, coupled, occupied)
    index_neighbours(rows, offsets, lanes, is_near, inside)
    for n in range(NB):
        copies[7 + n].wait()
        valid = inside[n : n + 1, :]
        for row in range(rows):
            read = lambda at, size: coupling[n, at : at + size, :] * valid
            spread_rows(links, n // group * pairs, n % group * rows + row, read, 0, pairs)


def couple_kernel(rows, blocked, unroll, own, *refs):
    far, (lanes, is_near, links, out, other, *work) = refs[:-8], refs[-8:]
    pairs = links.shape[1]
    if len(far) == 1:
        for pair in range(pairs):
            value = far[0][pair]
            for at in range(0, ROWS, rows):
                other[pair * ROWS + at : pair * ROWS + at + rows, :] = value
    else:
        energies = rows // len(far)
        for row in range(ROWS):
            source = far[row % rows // energies]
            read = lambda at, size: source[row % energies, at : at + size, :]
            spread_rows(other, 0, row, read, 0, pairs)

    def keep(at, value):
        out[at] = value

    couple(rows, blocked, unroll, own, other, lanes, is_near, links, work, keep)
    for at in range(pairs, out.shape[0]):
        out[at] = jnp.zeros(out.shape[1:], jnp.float32)


def mix_kernel(fused, mixing, blocks, out, before, after):
    parts, share, rows, atoms = blocks.shape
    energies = rows // fused
    for f in range(fused):
        some = slice(f * energies, (f + 1) * energies)
        for part in range(parts):
            for pair in range(share):
                before[part * energies : (part + 1) * energies, pair * atoms : (pair + 1) * atoms] = (
                    blocks[part, pair, some, :]
                )
        after[...] = jnp.dot(
            mixing[f], before[...], precision=TOP_RANK, preferred_element_type=jnp.float32
        )
        for part in range(parts):
            for pair in range(share):
                out[part, pair, some, :] = after[
                    part * energies : (part + 1) * energies, pair * atoms : (pair + 1) * atoms
                ]


def dress(rows, sigma, left, right, copied, keep):
    parts = ROWS // rows
    for pair in range(NORB * NORB):
        value = sigma[pair]
        for part in range(parts):
            copied[pair, part * rows : (part + 1) * rows, :] = value
    for i in range(NORB // parts):
        inner = [None] * NORB
        for j in range(NORB):
            factor = left[i * NORB + j]
            for l in range(NORB):
                term = factor * copied[j * NORB + l]
                inner[l] = term if j == 0 else inner[l] + term
        for k in range(NORB):
            value = inner[0] * right[k * NORB]
            for l in range(1, NORB):
                value = value + inner[l] * right[k * NORB + l]
            keep(i * NORB + k, value)


def dress_between_kernel(rows, sigma, left, right, free, own, compact, copied):
    atoms = sigma.shape[2]
    share = left.shape[0]
    row_at = lax.broadcasted_iota(jnp.int32, (ROWS, atoms), 0)

    def keep(at, value):
        for part in range(ROWS // rows):
            held = (row_at >= part * rows) & (row_at < (part + 1) * rows)
            piece = jnp.where(held, value, 0.0)
            width = ROWS // 2
            while width >= rows:
                piece = piece + pltpu.roll(piece, width, 0)
                width //= 2
            pair = part * share + at
            piece = piece + free[pair * ROWS : (pair + 1) * ROWS, :]
            own[pair * ROWS : (pair + 1) * ROWS, :] = piece
            compact[pair] = piece[:rows]

    dress(rows, sigma, left, right, copied, keep)


def dress_last_kernel(*refs):
    sigma, left, right = refs[:3]
    free, out_hbm = refs[3:5], refs[5:7]
    copied, dressed, out, leaving = refs[7:]
    energies, pairs, _ = free[0].shape
    rows = 2 * energies
    parts = ROWS // rows
    share = left.shape[0]
    stage = 2 * NORB
    copies = []

    def keep(at, value):
        dressed[at * ROWS : (at + 1) * ROWS, :] = value
        if (at + 1) % stage and at + 1 < share:
            return
        done = at // stage * stage
        for row in range(ROWS):
            function, energy, part = row % rows // energies, row % energies, row // rows
            for begin in range(done, at + 1, ROWS):
                size = min(ROWS, at + 1 - begin)
                first = part * share + begin
                piece = dressed[pl.ds(begin * ROWS + row, size, stride=ROWS), :]
                out[function, energy, first : first + size, :] = (
                    free[function][energy, first : first + size, :] + piece
                )
        for function in range(2):
            for part in range(parts):
                some = pl.ds(part * share + done, at + 1 - done)
                copies.append(
                    pltpu.make_async_copy(
                        out.at[function, :, some, :],
                        out_hbm[function].at[:, some, :],
                        leaving.at[len(copies)],
                    )
                )
                copies[-1].start()

    dress(rows, sigma, left, right, copied, keep)
    for copy in copies:
        copy.wait()


def call(kernel, outs, scratch, flops, *operands, spaces=None, targets=None):
    shapes = [
        x if isinstance(x, jax.ShapeDtypeStruct) else jax.ShapeDtypeStruct(x, jnp.float32)
        for x in outs
    ]
    vmem = pl.BlockSpec(memory_space=pltpu.VMEM)
    moved = sum(x.size for x in operands) + sum(x.size for x in shapes)
    return pl.pallas_call(
        kernel,
        out_shape=shapes,
        in_specs=spaces or [vmem] * len(operands),
        out_specs=targets or [vmem] * len(shapes),
        scratch_shapes=scratch,
        compiler_params=PARAMS,
        cost_estimate=pl.CostEstimate(
            flops=flops, bytes_accessed=4 * moved, transcendentals=0
        ),
    )(*operands)


def beside(block):
    count = lax.axis_size("slab")
    if count == 2:
        return lax.ppermute(block, "slab", [(0, 1), (1, 0)])
    forward = [(i, i + 1) for i in range(count - 1)]
    backward = [(target, source) for source, target in forward]
    axis = block.ndim - 1
    atoms = block.shape[axis]
    low = lax.ppermute(lax.slice_in_dim(block, atoms - HW, atoms, axis=axis), "slab", forward)
    high = lax.ppermute(lax.slice_in_dim(block, 0, HW, axis=axis), "slab", backward)
    gap = jnp.zeros(block.shape[:-1] + (atoms - 2 * HW,), block.dtype)
    return jnp.concatenate([high, gap, low], axis=axis)


def body(
    lesser_free,
    greater_free,
    retarded,
    coupling,
    neighbour_offsets,
    phonon_shift,
    phonon_coupling,
    phonon_occupation,
):
    energies, pairs, atoms = lesser_free.shape
    rows = 2 * energies
    groups = NB * rows // ROWS
    parts = lax.axis_size("energy")
    share = -(-pairs // parts)
    total = energies * parts
    away = pl.BlockSpec(memory_space=pltpu.HBM)
    held = lambda *dims: pltpu.VMEM(dims, jnp.float32)
    wide = (pairs * ROWS, atoms)
    deep = (pairs, ROWS, atoms)
    thin = (pairs * rows, atoms)
    every = (parts * share, rows, atoms)
    flops = 4 * NORB * rows * pairs * atoms
    index = jax.ShapeDtypeStruct((groups, ROWS, atoms), jnp.int32)
    transfer = lambda count: pltpu.SemaphoreType.DMA((count,))

    free = (lesser_free, greater_free)
    halos = [beside(g) for g in free]
    phonons = (phonon_shift, phonon_coupling, phonon_occupation)
    constants = (retarded, *phonons, neighbour_offsets, coupling)
    own, left, right, mixing, links, lanes, is_near = call(
        prep_kernel,
        [wide, thin, wide, (2, total, total), (groups * wide[0], atoms), index, index],
        [held(2, *retarded.shape), held(*retarded.shape)]
        + [pltpu.SMEM(x.shape, x.dtype) for x in phonons]
        + [pltpu.VMEM(neighbour_offsets.shape, jnp.int32)]
        + [held(*coupling.shape), held(NB, atoms), transfer(7 + NB)],
        rows * coupling.size,
        *(pltpu.with_memory_space_constraint(x, pltpu.HBM) for x in (*free, *constants)),
        spaces=[away] * 8,
    )
    links = links.reshape(groups, pairs, ROWS, atoms)
    start = own
    left = left.reshape(pairs * rows // ROWS, ROWS, atoms)
    right = right.reshape(deep)

    for step in range(ITERS):
        if step > 0:
            own, compact = call(
                functools.partial(dress_between_kernel, rows),
                [wide, (pairs, rows, atoms)],
                [held(*deep)],
                flops,
                sigma,
                left,
                right,
                start,
            )
            halos = [beside(compact)]
        (coupled,) = call(
            functools.partial(couple_kernel, rows, *((3, 1) if step == 0 else (2, 2))),
            [every],
            [held(*wide)] + [held(*deep)] * 3,
            NB * flops,
            own,
            *halos,
            lanes,
            is_near,
            links,
        )
        gathered = lax.all_to_all(coupled.reshape(parts, share, rows, atoms), "energy", 0, 0)
        (mixed,) = call(
            functools.partial(mix_kernel, 2),
            [gathered.shape],
            [held(total, share * atoms)] * 2,
            2 * total * gathered.size,
            mixing,
            gathered,
        )
        sigma = lax.all_to_all(mixed, "energy", 0, 0).reshape(every)
    stages = -(-thin[0] // (ROWS * 2 * NORB))
    return call(
        dress_last_kernel,
        [lesser_free.shape] * 2,
        [held(*deep), held(*thin), held(2, *lesser_free.shape)]
        + [transfer(stages * 2 * ROWS // rows)],
        flops,
        sigma,
        left,
        right,
        *free,
        targets=[away] * 2,
    )


def solution(mesh):
    placed = (
        P("energy", None, "slab"),
        P("energy", None, "slab"),
        P("energy", None, "slab"),
        P(None, None, "slab"),
        P(None, "slab"),
        P(),
        P(),
        P(),
    )
    return jax.shard_map(
        body,
        mesh=mesh,
        in_specs=placed,
        out_specs=(P("energy", None, "slab"), P("energy", None, "slab")),
        check_vma=False,
    )
```

```python
import functools

import jax
import jax.numpy as jnp
from jax import lax
from jax.experimental import pallas as pl
from jax.experimental.pallas import tpu as pltpu
from jax.sharding import PartitionSpec as P

NORB = 12
NB = 12
HW = 32
ITERS = 2
ROWS = 8
LANES = 128
BLOCKED = 2

TOP_RANK = lax.Precision.HIGHEST
PARAMS = pltpu.CompilerParams(vmem_limit_bytes=24 * 1024 * 1024)


def each(count, step):
    lax.fori_loop(0, count, lambda at, _: step(at), None)


def eight(at):
    return pl.ds(pl.multiple_of(at * ROWS, ROWS), ROWS)


def spread_rows(target, base, sources, count):
    def tile(at):
        for row, source in sources:
            rows = pl.ds((base + at * ROWS) * ROWS + row, ROWS, stride=ROWS)
            target[rows, :] = source(pl.multiple_of(at * ROWS, ROWS))

    each(count // ROWS, tile)


def index_neighbours(rows, offsets, lanes, is_near, inside):
    atoms = offsets.shape[1]
    group = ROWS // rows
    slab, slabs = lax.axis_index("slab"), lax.axis_size("slab")
    targets = offsets[...] + lax.broadcasted_iota(jnp.int32, (NB, atoms), 1)
    placed = targets + slab * atoms
    inside[...] = ((placed >= 0) & (placed < slabs * atoms)).astype(jnp.float32)
    near = ((targets >= 0) & (targets < atoms)).astype(jnp.int32)
    lane = jnp.where(targets < 0, targets + atoms, targets)
    lane = jnp.where(lane >= atoms, lane - atoms, lane)
    for n in range(NB):
        some = slice(n % group * rows, (n % group + 1) * rows)
        lanes[n // group, some, :] = jnp.broadcast_to(lane[n : n + 1, :], (rows, atoms))
        is_near[n // group, some, :] = jnp.broadcast_to(near[n : n + 1, :], (rows, atoms))


def couple(own, other, lanes, is_near, links, gathered_a, gathered_b, total):
    groups, pairs = links.shape[:2]
    steps = NORB // BLOCKED
    chunk = pairs // steps

    def gather(target, g, step):
        lane, mine = lanes[g], is_near[g] != 0
        for at in range(chunk):
            pair = step * chunk + at
            inner = jnp.take_along_axis(own[eight(pair), :], lane, axis=1, mode="promise_in_bounds")
            outer = jnp.take_along_axis(other[eight(pair), :], lane, axis=1, mode="promise_in_bounds")
            target[pair] = jnp.where(mine, inner, outer)

    def group_sums(g, source, target):
        following = jnp.minimum(g + 1, groups - 1)

        def block_row(step):
            first = step * BLOCKED
            inner = [[None] * NORB for _ in range(BLOCKED)]
            for j in range(NORB):
                left = [links[g, (first + b) * NORB + j] for b in range(BLOCKED)]
                for l in range(NORB):
                    value = source[j * NORB + l]
                    for b in range(BLOCKED):
                        term = left[b] * value
                        inner[b][l] = term if j == 0 else inner[b][l] + term
            for k in range(NORB):
                at = [(first + b) * NORB + k for b in range(BLOCKED)]
                sums = [total[at[b]] for b in range(BLOCKED)]
                for l in range(NORB):
                    right = links[g, k * NORB + l]
                    for b in range(BLOCKED):
                        sums[b] = sums[b] + inner[b][l] * right
                for b in range(BLOCKED):
                    total[at[b]] = sums[b]
            gather(target, following, step)

        each(steps, block_row)

    def clear(step):
        for at in range(chunk):
            total[step * chunk + at] = jnp.zeros(total.shape[1:], jnp.float32)
        gather(gathered_a, 0, step)

    def two_groups(half):
        group_sums(half * 2, gathered_a, gathered_b)
        group_sums(half * 2 + 1, gathered_b, gathered_a)

    each(steps, clear)
    each(groups // 2, two_groups)
    if groups % 2:
        group_sums(groups - 1, gathered_a, gathered_b)


def couple_kernel(rows, own, *refs):
    far, (lanes, is_near, links, out, other, *work) = refs[:-8], refs[-8:]
    pairs = links.shape[1]
    total = work[-1]
    if len(far) == 1:

        def widen(tile):
            for pair in range(ROWS):
                value = far[0][tile * ROWS + pair]
                for at in range(0, ROWS, rows):
                    some = pl.ds((tile * ROWS + pair) * ROWS + at, rows)
                    other[some, :] = value

        each(pairs // ROWS, widen)
    else:
        energies = rows // len(far)

        def reader(row):
            source, energy = far[row % rows // energies], row % energies
            return row, lambda at: source[energy, pl.ds(at, ROWS), :]

        spread_rows(other, 0, [reader(row) for row in range(ROWS)], pairs)
    couple(own, other, lanes, is_near, links, *work)

    def finish(tile):
        for at in range(ROWS):
            value = total[tile * ROWS + at]
            width = ROWS // 2
            while width >= rows:
                value = value + pltpu.roll(value, width, 0)
                width //= 2
            out[tile * ROWS + at] = value[:rows]

    each(pairs // ROWS, finish)
    for at in range(pairs, out.shape[0]):
        out[at] = jnp.zeros(out.shape[1:], jnp.float32)


def mix_weights(mixing, shifts, coupled, occupied):
    total = mixing.shape[1]
    lane = lax.broadcasted_iota(jnp.int32, (ROWS, LANES), 1)
    row = lax.broadcasted_iota(jnp.int32, (ROWS, LANES), 0)
    emitted = jnp.zeros((ROWS, LANES), jnp.float32)
    absorbed = jnp.zeros((ROWS, LANES), jnp.float32)

    def add_mode(mode, weights):
        emitted, absorbed = weights
        hit = lane == shifts[mode]
        absorb = coupled[mode] * occupied[mode]
        emit = coupled[mode] * (occupied[mode] + 1.0)
        return emitted + jnp.where(hit, emit, 0.0), absorbed + jnp.where(hit, absorb, 0.0)

    emitted, absorbed = lax.fori_loop(
        0, shifts.shape[0], add_mode, (emitted, absorbed), unroll=8
    )
    for at in range(0, total, ROWS):
        for first in range(0, total, LANES):
            width = min(LANES, total - first)
            gap = lane + first - (row + at)
            far = jnp.minimum(jnp.abs(gap), LANES - 1)
            emit = jnp.take_along_axis(emitted, far, axis=1, mode="promise_in_bounds")
            absorb = jnp.take_along_axis(absorbed, far, axis=1, mode="promise_in_bounds")
            some = slice(first, first + width)
            mixing[0, at : at + ROWS, some] = jnp.where(gap > 0, emit, absorb)[:, :width]
            mixing[1, at : at + ROWS, some] = jnp.where(gap > 0, absorb, emit)[:, :width]


def prep_kernel(*refs):
    free_hbm, retarded_hbm, modes_hbm = refs[0:2], refs[2], refs[3:6]
    offsets_hbm, coupling_hbm = refs[6:8]
    start, left, right, mixing, links, lanes, is_near = refs[8:15]
    free, retarded, shifts, coupled, occupied, offsets, coupling, inside, sems = refs[15:]
    energies, pairs, _ = retarded.shape
    rows = 2 * energies
    group = ROWS // rows
    share = left.shape[0] // ROWS
    moves = [(free_hbm[f], free.at[f]) for f in range(2)] + [(retarded_hbm, retarded)]
    moves += list(zip(modes_hbm, (shifts, coupled, occupied))) + [(offsets_hbm, offsets)]
    moves += [(coupling_hbm.at[n], coupling.at[n]) for n in range(NB)]
    copies = [
        pltpu.make_async_copy(source, target, sems.at[at])
        for at, (source, target) in enumerate(moves)
    ]
    for copy in copies:
        copy.start()

    copies[0].wait()
    copies[1].wait()

    def own_reader(row):
        function, energy = row % rows // energies, row % energies
        return row, lambda at: free[function, energy, pl.ds(at, ROWS), :]

    spread_rows(start, 0, [own_reader(row) for row in range(ROWS)], pairs)
    copies[2].wait()

    def factor_reader(row, skipped):
        return row, lambda at: retarded[row % energies, pl.ds(skipped + at, ROWS), :]

    spread_rows(left, 0, [factor_reader(row, row // rows * share) for row in range(ROWS)], share)
    spread_rows(right, 0, [factor_reader(row, 0) for row in range(ROWS)], pairs)
    for copy in copies[3:7]:
        copy.wait()
    mix_weights(mixing, shifts, coupled, occupied)
    index_neighbours(rows, offsets, lanes, is_near, inside)
    for copy in copies[7:]:
        copy.wait()

    def expand(n):
        valid = inside[pl.ds(n, 1), :]
        read = lambda at: coupling[n, pl.ds(at, ROWS), :] * valid
        first = n % group * rows
        spread_rows(
            links, n // group * pairs, [(first + row, read) for row in range(rows)], pairs
        )

    each(NB, expand)


def mix_kernel(fused, mixing, blocks, out, before, after):
    parts, share, rows, atoms = blocks.shape
    energies = rows // fused

    def place(pair):
        lanes = pl.ds(pl.multiple_of(pair * atoms, atoms), atoms)
        for part in range(parts):
            held = slice(part * energies, (part + 1) * energies)
            value = blocks[part, pair]
            for f in range(fused):
                before[f, held, lanes] = value[f * energies : (f + 1) * energies]

    def replace(pair):
        lanes = pl.ds(pl.multiple_of(pair * atoms, atoms), atoms)
        for part in range(parts):
            held = slice(part * energies, (part + 1) * energies)
            for f in range(fused):
                out[part, pair, f * energies : (f + 1) * energies, :] = after[f, held, lanes]

    each(share, place)
    for f in range(fused):
        after[f] = jnp.dot(
            mixing[f], before[f], precision=TOP_RANK, preferred_element_type=jnp.float32
        )
    each(share, replace)


def widen_sigma(rows, sigma, copied):
    def widen(tile):
        for at in range(ROWS):
            pair = tile * ROWS + at
            value = sigma[pair]
            for first in range(0, ROWS, rows):
                copied[pair, first : first + rows, :] = value

    each(copied.shape[0] // ROWS, widen)


def dress_row(i, left, right, copied, keep):
    inner = [None] * NORB
    for j in range(NORB):
        factor = left[i * NORB + j]
        for l in range(NORB):
            term = factor * copied[j * NORB + l]
            inner[l] = term if j == 0 else inner[l] + term
    for k in range(NORB):
        value = inner[0] * right[k * NORB]
        for l in range(1, NORB):
            value = value + inner[l] * right[k * NORB + l]
        keep(i * NORB + k, value)


def dress_between_kernel(rows, sigma, left, right, free, own, compact, copied):
    atoms = sigma.shape[2]
    share = left.shape[0]
    row_at = lax.broadcasted_iota(jnp.int32, (ROWS, atoms), 0)

    def keep(at, value):
        for part in range(ROWS // rows):
            held = (row_at >= part * rows) & (row_at < (part + 1) * rows)
            piece = jnp.where(held, value, 0.0)
            width = ROWS // 2
            while width >= rows:
                piece = piece + pltpu.roll(piece, width, 0)
                width //= 2
            pair = part * share + at
            piece = piece + free[eight(pair), :]
            own[eight(pair), :] = piece
            compact[pair] = piece[:rows]

    widen_sigma(rows, sigma, copied)
    each(share // NORB, lambda i: dress_row(i, left, right, copied, keep))


def dress_last_kernel(*refs):
    sigma, left, right = refs[:3]
    free, out_hbm = refs[3:5], refs[5:7]
    copied, dressed, out, leaving = refs[7:]
    energies, pairs, _ = free[0].shape
    rows = 2 * energies
    parts = ROWS // rows
    share = left.shape[0]
    stage = 2 * NORB
    stages = share // stage

    def keep(at, value):
        dressed[eight(at), :] = value

    def departure(done, function, part):
        some = pl.ds(pl.multiple_of(part * share + done * stage, ROWS), stage)
        return pltpu.make_async_copy(
            out.at[function, :, some, :],
            out_hbm[function].at[:, some, :],
            leaving.at[(done * 2 + function) * parts + part],
        )

    def dress_stage(done):
        for at in range(stage // NORB):
            dress_row(done * (stage // NORB) + at, left, right, copied, keep)
        for row in range(ROWS):
            function, energy, part = row % rows // energies, row % energies, row // rows
            for at in range(0, stage, ROWS):
                begin = done * stage + at
                some = pl.ds(pl.multiple_of(part * share + begin, ROWS), ROWS)
                piece = dressed[pl.ds(begin * ROWS + row, ROWS, stride=ROWS), :]
                out[function, energy, some, :] = free[function][energy, some, :] + piece
        for function in range(2):
            for part in range(parts):
                departure(done, function, part).start()

    def await_stage(done):
        for function in range(2):
            for part in range(parts):
                departure(done, function, part).wait()

    widen_sigma(rows, sigma, copied)
    each(stages, dress_stage)
    each(stages, await_stage)


def call(kernel, outs, scratch, flops, *operands, spaces=None, targets=None):
    shapes = [
        x if isinstance(x, jax.ShapeDtypeStruct) else jax.ShapeDtypeStruct(x, jnp.float32)
        for x in outs
    ]
    vmem = pl.BlockSpec(memory_space=pltpu.VMEM)
    moved = sum(x.size for x in operands) + sum(x.size for x in shapes)
    return pl.pallas_call(
        kernel,
        out_shape=shapes,
        in_specs=spaces or [vmem] * len(operands),
        out_specs=targets or [vmem] * len(shapes),
        scratch_shapes=scratch,
        compiler_params=PARAMS,
        cost_estimate=pl.CostEstimate(
            flops=flops, bytes_accessed=4 * moved, transcendentals=0
        ),
    )(*operands)


def beside(block):
    count = lax.axis_size("slab")
    if count == 2:
        return lax.ppermute(block, "slab", [(0, 1), (1, 0)])
    forward = [(i, i + 1) for i in range(count - 1)]
    backward = [(target, source) for source, target in forward]
    axis = block.ndim - 1
    atoms = block.shape[axis]
    low = lax.ppermute(lax.slice_in_dim(block, atoms - HW, atoms, axis=axis), "slab", forward)
    high = lax.ppermute(lax.slice_in_dim(block, 0, HW, axis=axis), "slab", backward)
    gap = jnp.zeros(block.shape[:-1] + (atoms - 2 * HW,), block.dtype)
    return jnp.concatenate([high, gap, low], axis=axis)


def body(
    lesser_free,
    greater_free,
    retarded,
    coupling,
    neighbour_offsets,
    phonon_shift,
    phonon_coupling,
    phonon_occupation,
):
    energies, pairs, atoms = lesser_free.shape
    rows = 2 * energies
    groups = NB * rows // ROWS
    parts = lax.axis_size("energy")
    share = -(-pairs // parts)
    total = energies * parts
    away = pl.BlockSpec(memory_space=pltpu.HBM)
    held = lambda *dims: pltpu.VMEM(dims, jnp.float32)
    wide = (pairs * ROWS, atoms)
    deep = (pairs, ROWS, atoms)
    thin = (pairs * rows, atoms)
    every = (parts * share, rows, atoms)
    flops = 4 * NORB * rows * pairs * atoms
    index = jax.ShapeDtypeStruct((groups, ROWS, atoms), jnp.int32)
    transfer = lambda count: pltpu.SemaphoreType.DMA((count,))

    free = (lesser_free, greater_free)
    halos = [beside(g) for g in free]
    phonons = (phonon_shift, phonon_coupling, phonon_occupation)
    constants = (retarded, *phonons, neighbour_offsets, coupling)
    own, left, right, mixing, links, lanes, is_near = call(
        prep_kernel,
        [wide, thin, wide, (2, total, total), (groups * wide[0], atoms), index, index],
        [held(2, *retarded.shape), held(*retarded.shape)]
        + [pltpu.SMEM(x.shape, x.dtype) for x in phonons]
        + [pltpu.VMEM(neighbour_offsets.shape, jnp.int32)]
        + [held(*coupling.shape), held(NB, atoms), transfer(7 + NB)],
        rows * coupling.size,
        *(pltpu.with_memory_space_constraint(x, pltpu.HBM) for x in (*free, *constants)),
        spaces=[away] * 8,
    )
    links = links.reshape(groups, pairs, ROWS, atoms)
    start = own
    left = left.reshape(pairs * rows // ROWS, ROWS, atoms)
    right = right.reshape(deep)

    for step in range(ITERS):
        if step > 0:
            own, compact = call(
                functools.partial(dress_between_kernel, rows),
                [wide, (pairs, rows, atoms)],
                [held(*deep)],
                flops,
                sigma,
                left,
                right,
                start,
            )
            halos = [beside(compact)]
        (coupled,) = call(
            functools.partial(couple_kernel, rows),
            [every],
            [held(*wide)] + [held(*deep)] * 3,
            NB * flops,
            own,
            *halos,
            lanes,
            is_near,
            links,
        )
        gathered = lax.all_to_all(coupled.reshape(parts, share, rows, atoms), "energy", 0, 0)
        (mixed,) = call(
            functools.partial(mix_kernel, 2),
            [gathered.shape],
            [held(2, total, share * atoms)] * 2,
            2 * total * gathered.size,
            mixing,
            gathered,
        )
        sigma = lax.all_to_all(mixed, "energy", 0, 0).reshape(every)
    stages = -(-thin[0] // (ROWS * 2 * NORB))
    return call(
        dress_last_kernel,
        [lesser_free.shape] * 2,
        [held(*deep), held(*thin), held(2, *lesser_free.shape)]
        + [transfer(stages * 2 * ROWS // rows)],
        flops,
        sigma,
        left,
        right,
        *free,
        targets=[away] * 2,
    )


def solution(mesh):
    placed = (
        P("energy", None, "slab"),
        P("energy", None, "slab"),
        P("energy", None, "slab"),
        P(None, None, "slab"),
        P(None, "slab"),
        P(),
        P(),
        P(),
    )
    return jax.shard_map(
        body,
        mesh=mesh,
        in_specs=placed,
        out_specs=(P("energy", None, "slab"), P("energy", None, "slab")),
        check_vma=False,
    )
```

```python
import functools

import jax
import jax.numpy as jnp
from jax import lax
from jax.experimental import pallas as pl
from jax.experimental.pallas import tpu as pltpu
from jax.sharding import PartitionSpec as P

NORB = 12
NB = 12
HW = 32
ITERS = 2
ROWS = 8
LANES = 128
BLOCKED = 2

TOP_RANK = lax.Precision.HIGHEST
PARAMS = pltpu.CompilerParams(vmem_limit_bytes=24 * 1024 * 1024)


def each(count, step):
    lax.fori_loop(0, count, lambda at, _: step(at), None)


def eight(at):
    return pl.ds(pl.multiple_of(at * ROWS, ROWS), ROWS)


def spread_rows(target, base, row, source, first, count):
    for at in range(0, count, ROWS):
        size = min(ROWS, count - at)
        rows = pl.ds((base + at) * ROWS + row, size, stride=ROWS)
        target[rows, :] = source(first + at, size)


def exchanged(shares):
    parts, slabs = lax.axis_size("energy"), lax.axis_size("slab")
    groups = [
        [device * slabs + slab for device in range(parts)][:: -1 if slab % 2 else 1]
        for slab in range(slabs)
    ]
    return lax.all_to_all(shares, ("energy", "slab"), 0, 0, axis_index_groups=groups)


def index_neighbours(rows, offsets, lanes, is_near, inside):
    atoms = offsets.shape[1]
    group = ROWS // rows
    slab, slabs = lax.axis_index("slab"), lax.axis_size("slab")
    targets = offsets[...] + lax.broadcasted_iota(jnp.int32, (NB, atoms), 1)
    placed = targets + slab * atoms
    inside[...] = ((placed >= 0) & (placed < slabs * atoms)).astype(jnp.float32)
    near = ((targets >= 0) & (targets < atoms)).astype(jnp.int32)
    lane = jnp.where(targets < 0, targets + atoms, targets)
    lane = jnp.where(lane >= atoms, lane - atoms, lane)
    for n in range(NB):
        some = slice(n % group * rows, (n % group + 1) * rows)
        lanes[n // group, some, :] = jnp.broadcast_to(lane[n : n + 1, :], (rows, atoms))
        is_near[n // group, some, :] = jnp.broadcast_to(near[n : n + 1, :], (rows, atoms))


def couple(own, other, lanes, is_near, links, gathered_a, gathered_b, total):
    groups, pairs = links.shape[:2]
    steps = NORB // BLOCKED
    chunk = pairs // steps

    def gather(target, g, step):
        lane, mine = lanes[g], is_near[g] != 0
        for at in range(chunk):
            pair = step * chunk + at
            inner = jnp.take_along_axis(own[eight(pair), :], lane, axis=1, mode="promise_in_bounds")
            outer = jnp.take_along_axis(other[eight(pair), :], lane, axis=1, mode="promise_in_bounds")
            target[pair] = jnp.where(mine, inner, outer)

    def group_sums(g, source, target):
        following = jnp.minimum(g + 1, groups - 1)

        def block_row(step):
            first = step * BLOCKED
            inner = [[None] * NORB for _ in range(BLOCKED)]
            for j in range(NORB):
                left = [links[g, (first + b) * NORB + j] for b in range(BLOCKED)]
                for l in range(NORB):
                    value = source[j * NORB + l]
                    for b in range(BLOCKED):
                        term = left[b] * value
                        inner[b][l] = term if j == 0 else inner[b][l] + term
            for k in range(NORB):
                at = [(first + b) * NORB + k for b in range(BLOCKED)]
                sums = [total[at[b]] for b in range(BLOCKED)]
                for l in range(NORB):
                    right = links[g, k * NORB + l]
                    for b in range(BLOCKED):
                        sums[b] = sums[b] + inner[b][l] * right
                for b in range(BLOCKED):
                    total[at[b]] = sums[b]
            gather(target, following, step)

        each(steps, block_row)

    def clear(step):
        for at in range(chunk):
            total[step * chunk + at] = jnp.zeros(total.shape[1:], jnp.float32)
        gather(gathered_a, 0, step)

    def two_groups(half):
        group_sums(half * 2, gathered_a, gathered_b)
        group_sums(half * 2 + 1, gathered_b, gathered_a)

    each(steps, clear)
    each(groups // 2, two_groups)
    if groups % 2:
        group_sums(groups - 1, gathered_a, gathered_b)


def mix_weights(mixing, energies, shifts, coupled, occupied):
    total = mixing.shape[1]
    lane = lax.broadcasted_iota(jnp.int32, (ROWS, LANES), 1)
    row = lax.broadcasted_iota(jnp.int32, (ROWS, LANES), 0)
    emitted = jnp.zeros((ROWS, LANES), jnp.float32)
    absorbed = jnp.zeros((ROWS, LANES), jnp.float32)
    for mode in range(shifts.shape[0]):
        hit = lane == shifts[mode]
        absorb = coupled[mode] * occupied[mode]
        emit = coupled[mode] * (occupied[mode] + 1.0)
        emitted = emitted + jnp.where(hit, emit, 0.0)
        absorbed = absorbed + jnp.where(hit, absorb, 0.0)
    for at in range(0, total, ROWS):
        for first in range(0, total, LANES):
            width = min(LANES, total - first)
            apart = (lane + first) // energies - (row + at) // energies
            apart = jnp.where(lax.axis_index("slab") % 2 == 1, -apart, apart)
            gap = apart * energies + (lane + first) % energies - (row + at) % energies
            far = jnp.minimum(jnp.abs(gap), LANES - 1)
            emit = jnp.take_along_axis(emitted, far, axis=1, mode="promise_in_bounds")
            absorb = jnp.take_along_axis(absorbed, far, axis=1, mode="promise_in_bounds")
            some = slice(first, first + width)
            mixing[0, at : at + ROWS, some] = jnp.where(gap > 0, emit, absorb)[:, :width]
            mixing[1, at : at + ROWS, some] = jnp.where(gap > 0, absorb, emit)[:, :width]


def prep_kernel(*refs):
    free_hbm, retarded_hbm, modes_hbm = refs[0:2], refs[2], refs[3:6]
    offsets_hbm, coupling_hbm = refs[6:8]
    start, left, right, mixing, links, lanes, is_near = refs[8:15]
    free, retarded, shifts, coupled, occupied, offsets, coupling, inside, sems = refs[15:]
    energies, pairs, _ = retarded.shape
    rows = 2 * energies
    group = ROWS // rows
    share = left.shape[0] // ROWS
    moves = [(free_hbm[f], free.at[f]) for f in range(2)] + [(retarded_hbm, retarded)]
    moves += list(zip(modes_hbm, (shifts, coupled, occupied))) + [(offsets_hbm, offsets)]
    moves += [(coupling_hbm.at[n], coupling.at[n]) for n in range(NB)]
    copies = [
        pltpu.make_async_copy(source, target, sems.at[at])
        for at, (source, target) in enumerate(moves)
    ]
    for copy in copies:
        copy.start()

    copies[0].wait()
    copies[1].wait()
    for row in range(ROWS):
        function, energy = row % rows // energies, row % energies
        read = lambda at, size: free[function, energy, at : at + size, :]
        spread_rows(start, 0, row, read, 0, pairs)
    copies[2].wait()
    for row in range(ROWS):
        skipped = row // rows * share
        read = lambda at, size: retarded[row % energies, at : at + size, :]
        spread_rows(left, 0, row, read, skipped, share)
        spread_rows(right, 0, row, read, 0, pairs)
    for copy in copies[3:7]:
        copy.wait()
    mix_weights(mixing, energies, shifts, coupled, occupied)
    index_neighbours(rows, offsets, lanes, is_near, inside)
    for n in range(NB):
        copies[7 + n].wait()
        valid = inside[n : n + 1, :]
        for row in range(rows):
            read = lambda at, size: coupling[n, at : at + size, :] * valid
            spread_rows(links, n // group * pairs, n % group * rows + row, read, 0, pairs)


def couple_kernel(rows, own, *refs):
    far, (lanes, is_near, links, out, other, *work) = refs[:-8], refs[-8:]
    pairs = links.shape[1]
    total = work[-1]
    if len(far) == 1:
        for pair in range(pairs):
            value = far[0][pair]
            for at in range(0, ROWS, rows):
                other[pair * ROWS + at : pair * ROWS + at + rows, :] = value
    else:
        energies = rows // len(far)
        for row in range(ROWS):
            source = far[row % rows // energies]
            read = lambda at, size: source[row % energies, at : at + size, :]
            spread_rows(other, 0, row, read, 0, pairs)
    couple(own, other, lanes, is_near, links, *work)
    for pair in range(pairs):
        value = total[pair]
        width = ROWS // 2
        while width >= rows:
            value = value + pltpu.roll(value, width, 0)
            width //= 2
        out[pair] = value[:rows]
    for at in range(pairs, out.shape[0]):
        out[at] = jnp.zeros(out.shape[1:], jnp.float32)


def mix_kernel(fused, mixing, blocks, out, before, after):
    parts, share, rows, atoms = blocks.shape
    energies = rows // fused
    for f in range(fused):
        some = slice(f * energies, (f + 1) * energies)
        for part in range(parts):
            for pair in range(share):
                before[part * energies : (part + 1) * energies, pair * atoms : (pair + 1) * atoms] = (
                    blocks[part, pair, some, :]
                )
        after[...] = jnp.dot(
            mixing[f], before[...], precision=TOP_RANK, preferred_element_type=jnp.float32
        )
        for part in range(parts):
            for pair in range(share):
                out[part, pair, some, :] = after[
                    part * energies : (part + 1) * energies, pair * atoms : (pair + 1) * atoms
                ]


def dress(rows, sigma, left, right, copied, keep):
    parts = ROWS // rows
    for pair in range(NORB * NORB):
        value = sigma[pair]
        for part in range(parts):
            copied[pair, part * rows : (part + 1) * rows, :] = value
    for i in range(NORB // parts):
        inner = [None] * NORB
        for j in range(NORB):
            factor = left[i * NORB + j]
            for l in range(NORB):
                term = factor * copied[j * NORB + l]
                inner[l] = term if j == 0 else inner[l] + term
        for k in range(NORB):
            value = inner[0] * right[k * NORB]
            for l in range(1, NORB):
                value = value + inner[l] * right[k * NORB + l]
            keep(i * NORB + k, value)


def dress_between_kernel(rows, sigma, left, right, free, own, compact, copied):
    atoms = sigma.shape[2]
    share = left.shape[0]
    row_at = lax.broadcasted_iota(jnp.int32, (ROWS, atoms), 0)

    def keep(at, value):
        for part in range(ROWS // rows):
            held = (row_at >= part * rows) & (row_at < (part + 1) * rows)
            piece = jnp.where(held, value, 0.0)
            width = ROWS // 2
            while width >= rows:
                piece = piece + pltpu.roll(piece, width, 0)
                width //= 2
            pair = part * share + at
            piece = piece + free[pair * ROWS : (pair + 1) * ROWS, :]
            own[pair * ROWS : (pair + 1) * ROWS, :] = piece
            compact[pair] = piece[:rows]

    dress(rows, sigma, left, right, copied, keep)


def dress_last_kernel(*refs):
    sigma, left, right = refs[:3]
    free, out_hbm = refs[3:5], refs[5:7]
    copied, dressed, out, leaving = refs[7:]
    energies, pairs, _ = free[0].shape
    rows = 2 * energies
    parts = ROWS // rows
    share = left.shape[0]
    stage = 2 * NORB
    copies = []

    def keep(at, value):
        dressed[at * ROWS : (at + 1) * ROWS, :] = value
        if (at + 1) % stage and at + 1 < share:
            return
        done = at // stage * stage
        for row in range(ROWS):
            function, energy, part = row % rows // energies, row % energies, row // rows
            for begin in range(done, at + 1, ROWS):
                size = min(ROWS, at + 1 - begin)
                first = part * share + begin
                piece = dressed[pl.ds(begin * ROWS + row, size, stride=ROWS), :]
                out[function, energy, first : first + size, :] = (
                    free[function][energy, first : first + size, :] + piece
                )
        for function in range(2):
            for part in range(parts):
                some = pl.ds(part * share + done, at + 1 - done)
                copies.append(
                    pltpu.make_async_copy(
                        out.at[function, :, some, :],
                        out_hbm[function].at[:, some, :],
                        leaving.at[len(copies)],
                    )
                )
                copies[-1].start()

    dress(rows, sigma, left, right, copied, keep)
    for copy in copies:
        copy.wait()


def call(kernel, outs, scratch, flops, *operands, spaces=None, targets=None):
    shapes = [
        x if isinstance(x, jax.ShapeDtypeStruct) else jax.ShapeDtypeStruct(x, jnp.float32)
        for x in outs
    ]
    vmem = pl.BlockSpec(memory_space=pltpu.VMEM)
    moved = sum(x.size for x in operands) + sum(x.size for x in shapes)
    return pl.pallas_call(
        kernel,
        out_shape=shapes,
        in_specs=spaces or [vmem] * len(operands),
        out_specs=targets or [vmem] * len(shapes),
        scratch_shapes=scratch,
        compiler_params=PARAMS,
        cost_estimate=pl.CostEstimate(
            flops=flops, bytes_accessed=4 * moved, transcendentals=0
        ),
    )(*operands)


def beside(block):
    count = lax.axis_size("slab")
    if count == 2:
        return lax.ppermute(block, "slab", [(0, 1), (1, 0)])
    forward = [(i, i + 1) for i in range(count - 1)]
    backward = [(target, source) for source, target in forward]
    axis = block.ndim - 1
    atoms = block.shape[axis]
    low = lax.ppermute(lax.slice_in_dim(block, atoms - HW, atoms, axis=axis), "slab", forward)
    high = lax.ppermute(lax.slice_in_dim(block, 0, HW, axis=axis), "slab", backward)
    gap = jnp.zeros(block.shape[:-1] + (atoms - 2 * HW,), block.dtype)
    return jnp.concatenate([high, gap, low], axis=axis)


def body(
    lesser_free,
    greater_free,
    retarded,
    coupling,
    neighbour_offsets,
    phonon_shift,
    phonon_coupling,
    phonon_occupation,
):
    energies, pairs, atoms = lesser_free.shape
    rows = 2 * energies
    groups = NB * rows // ROWS
    parts = lax.axis_size("energy")
    share = -(-pairs // parts)
    total = energies * parts
    away = pl.BlockSpec(memory_space=pltpu.HBM)
    held = lambda *dims: pltpu.VMEM(dims, jnp.float32)
    wide = (pairs * ROWS, atoms)
    deep = (pairs, ROWS, atoms)
    thin = (pairs * rows, atoms)
    every = (parts * share, rows, atoms)
    flops = 4 * NORB * rows * pairs * atoms
    index = jax.ShapeDtypeStruct((groups, ROWS, atoms), jnp.int32)
    transfer = lambda count: pltpu.SemaphoreType.DMA((count,))

    free = (lesser_free, greater_free)
    halos = [beside(g) for g in free]
    phonons = (phonon_shift, phonon_coupling, phonon_occupation)
    constants = (retarded, *phonons, neighbour_offsets, coupling)
    own, left, right, mixing, links, lanes, is_near = call(
        prep_kernel,
        [wide, thin, wide, (2, total, total), (groups * wide[0], atoms), index, index],
        [held(2, *retarded.shape), held(*retarded.shape)]
        + [pltpu.SMEM(x.shape, x.dtype) for x in phonons]
        + [pltpu.VMEM(neighbour_offsets.shape, jnp.int32)]
        + [held(*coupling.shape), held(NB, atoms), transfer(7 + NB)],
        rows * coupling.size,
        *(pltpu.with_memory_space_constraint(x, pltpu.HBM) for x in (*free, *constants)),
        spaces=[away] * 8,
    )
    links = links.reshape(groups, pairs, ROWS, atoms)
    start = own
    left = left.reshape(pairs * rows // ROWS, ROWS, atoms)
    right = right.reshape(deep)

    for step in range(ITERS):
        if step > 0:
            own, compact = call(
                functools.partial(dress_between_kernel, rows),
                [wide, (pairs, rows, atoms)],
                [held(*deep)],
                flops,
                sigma,
                left,
                right,
                start,
            )
            halos = [beside(compact)]
        (coupled,) = call(
            functools.partial(couple_kernel, rows),
            [every],
            [held(*wide)] + [held(*deep)] * 3,
            NB * flops,
            own,
            *halos,
            lanes,
            is_near,
            links,
        )
        gathered = exchanged(coupled.reshape(parts, share, rows, atoms))
        (mixed,) = call(
            functools.partial(mix_kernel, 2),
            [gathered.shape],
            [held(total, share * atoms)] * 2,
            2 * total * gathered.size,
            mixing,
            gathered,
        )
        sigma = exchanged(mixed).reshape(every)
    stages = -(-thin[0] // (ROWS * 2 * NORB))
    return call(
        dress_last_kernel,
        [lesser_free.shape] * 2,
        [held(*deep), held(*thin), held(2, *lesser_free.shape)]
        + [transfer(stages * 2 * ROWS // rows)],
        flops,
        sigma,
        left,
        right,
        *free,
        targets=[away] * 2,
    )


def solution(mesh):
    placed = (
        P("energy", None, "slab"),
        P("energy", None, "slab"),
        P("energy", None, "slab"),
        P(None, None, "slab"),
        P(None, "slab"),
        P(),
        P(),
        P(),
    )
    return jax.shard_map(
        body,
        mesh=mesh,
        in_specs=placed,
        out_specs=(P("energy", None, "slab"), P("energy", None, "slab")),
        check_vma=False,
    )
```

```python
import functools
import math

import jax
import jax.numpy as jnp
from jax import lax
from jax.experimental import pallas as pl
from jax.experimental.pallas import tpu as pltpu
from jax.sharding import PartitionSpec as P

NORB = 12
NB = 12
HW = 32
ITERS = 2
ROWS = 8
LANES = 128
BLOCKED = 2

TOP_RANK = lax.Precision.HIGHEST
PARAMS = pltpu.CompilerParams(vmem_limit_bytes=24 * 1024 * 1024)


def each(count, step):
    lax.fori_loop(0, count, lambda at, _: step(at), None)


def eight(at):
    return pl.ds(pl.multiple_of(at * ROWS, ROWS), ROWS)


def spread_rows(target, base, row, source, first, count):
    for at in range(0, count, ROWS):
        size = min(ROWS, count - at)
        rows = pl.ds((base + at) * ROWS + row, size, stride=ROWS)
        target[rows, :] = source(first + at, size)


def standing(place, parts, odd):
    root = math.isqrt(parts)
    root = root if parts % root == 0 else 1
    place = place + odd * (parts - 1 - 2 * place)
    return place % root * (parts // root) + place // root


def exchanged(shares):
    parts, slabs = lax.axis_size("energy"), lax.axis_size("slab")
    groups = [
        [standing(place, parts, slab % 2) * slabs + slab for place in range(parts)]
        for slab in range(slabs)
    ]
    return lax.all_to_all(shares, ("energy", "slab"), 0, 0, axis_index_groups=groups)


def index_neighbours(rows, offsets, lanes, is_near, inside):
    atoms = offsets.shape[1]
    group = ROWS // rows
    slab, slabs = lax.axis_index("slab"), lax.axis_size("slab")
    targets = offsets[...] + lax.broadcasted_iota(jnp.int32, (NB, atoms), 1)
    placed = targets + slab * atoms
    inside[...] = ((placed >= 0) & (placed < slabs * atoms)).astype(jnp.float32)
    near = ((targets >= 0) & (targets < atoms)).astype(jnp.int32)
    lane = jnp.where(targets < 0, targets + atoms, targets)
    lane = jnp.where(lane >= atoms, lane - atoms, lane)
    for n in range(NB):
        some = slice(n % group * rows, (n % group + 1) * rows)
        lanes[n // group, some, :] = jnp.broadcast_to(lane[n : n + 1, :], (rows, atoms))
        is_near[n // group, some, :] = jnp.broadcast_to(near[n : n + 1, :], (rows, atoms))


def couple(own, other, lanes, is_near, links, gathered_a, gathered_b, total):
    groups, pairs = links.shape[:2]
    steps = NORB // BLOCKED
    chunk = pairs // steps

    def gather(target, g, step):
        lane, mine = lanes[g], is_near[g] != 0
        for at in range(chunk):
            pair = step * chunk + at
            inner = jnp.take_along_axis(own[eight(pair), :], lane, axis=1, mode="promise_in_bounds")
            outer = jnp.take_along_axis(other[eight(pair), :], lane, axis=1, mode="promise_in_bounds")
            target[pair] = jnp.where(mine, inner, outer)

    def group_sums(g, source, target):
        following = jnp.minimum(g + 1, groups - 1)

        def block_row(step):
            first = step * BLOCKED
            inner = [[None] * NORB for _ in range(BLOCKED)]
            for j in range(NORB):
                left = [links[g, (first + b) * NORB + j] for b in range(BLOCKED)]
                for l in range(NORB):
                    value = source[j * NORB + l]
                    for b in range(BLOCKED):
                        term = left[b] * value
                        inner[b][l] = term if j == 0 else inner[b][l] + term
            for k in range(NORB):
                at = [(first + b) * NORB + k for b in range(BLOCKED)]
                sums = [total[at[b]] for b in range(BLOCKED)]
                for l in range(NORB):
                    right = links[g, k * NORB + l]
                    for b in range(BLOCKED):
                        sums[b] = sums[b] + inner[b][l] * right
                for b in range(BLOCKED):
                    total[at[b]] = sums[b]
            gather(target, following, step)

        each(steps, block_row)

    def clear(step):
        for at in range(chunk):
            total[step * chunk + at] = jnp.zeros(total.shape[1:], jnp.float32)
        gather(gathered_a, 0, step)

    def two_groups(half):
        group_sums(half * 2, gathered_a, gathered_b)
        group_sums(half * 2 + 1, gathered_b, gathered_a)

    each(steps, clear)
    each(groups // 2, two_groups)
    if groups % 2:
        group_sums(groups - 1, gathered_a, gathered_b)


def mix_weights(mixing, energies, shifts, coupled, occupied):
    total = mixing.shape[1]
    parts, odd = total // energies, lax.axis_index("slab") % 2

    def energy_at(index):
        return standing(index // energies, parts, odd) * energies + index % energies

    lane = lax.broadcasted_iota(jnp.int32, (ROWS, LANES), 1)
    row = lax.broadcasted_iota(jnp.int32, (ROWS, LANES), 0)
    emitted = jnp.zeros((ROWS, LANES), jnp.float32)
    absorbed = jnp.zeros((ROWS, LANES), jnp.float32)
    for mode in range(shifts.shape[0]):
        hit = lane == shifts[mode]
        absorb = coupled[mode] * occupied[mode]
        emit = coupled[mode] * (occupied[mode] + 1.0)
        emitted = emitted + jnp.where(hit, emit, 0.0)
        absorbed = absorbed + jnp.where(hit, absorb, 0.0)
    for at in range(0, total, ROWS):
        for first in range(0, total, LANES):
            width = min(LANES, total - first)
            gap = energy_at(lane + first) - energy_at(row + at)
            far = jnp.minimum(jnp.abs(gap), LANES - 1)
            emit = jnp.take_along_axis(emitted, far, axis=1, mode="promise_in_bounds")
            absorb = jnp.take_along_axis(absorbed, far, axis=1, mode="promise_in_bounds")
            some = slice(first, first + width)
            mixing[0, at : at + ROWS, some] = jnp.where(gap > 0, emit, absorb)[:, :width]
            mixing[1, at : at + ROWS, some] = jnp.where(gap > 0, absorb, emit)[:, :width]


def prep_kernel(*refs):
    free_hbm, retarded_hbm, modes_hbm = refs[0:2], refs[2], refs[3:6]
    offsets_hbm, coupling_hbm = refs[6:8]
    start, left, right, mixing, links, lanes, is_near = refs[8:15]
    free, retarded, shifts, coupled, occupied, offsets, coupling, inside, sems = refs[15:]
    energies, pairs, _ = retarded.shape
    rows = 2 * energies
    group = ROWS // rows
    share = left.shape[0] // ROWS
    moves = [(free_hbm[f], free.at[f]) for f in range(2)] + [(retarded_hbm, retarded)]
    moves += list(zip(modes_hbm, (shifts, coupled, occupied))) + [(offsets_hbm, offsets)]
    moves += [(coupling_hbm.at[n], coupling.at[n]) for n in range(NB)]
    copies = [
        pltpu.make_async_copy(source, target, sems.at[at])
        for at, (source, target) in enumerate(moves)
    ]
    for copy in copies:
        copy.start()

    copies[0].wait()
    copies[1].wait()
    for row in range(ROWS):
        function, energy = row % rows // energies, row % energies
        read = lambda at, size: free[function, energy, at : at + size, :]
        spread_rows(start, 0, row, read, 0, pairs)
    copies[2].wait()
    for row in range(ROWS):
        skipped = row // rows * share
        read = lambda at, size: retarded[row % energies, at : at + size, :]
        spread_rows(left, 0, row, read, skipped, share)
        spread_rows(right, 0, row, read, 0, pairs)
    for copy in copies[3:7]:
        copy.wait()
    mix_weights(mixing, energies, shifts, coupled, occupied)
    index_neighbours(rows, offsets, lanes, is_near, inside)
    for n in range(NB):
        copies[7 + n].wait()
        valid = inside[n : n + 1, :]
        for row in range(rows):
            read = lambda at, size: coupling[n, at : at + size, :] * valid
            spread_rows(links, n // group * pairs, n % group * rows + row, read, 0, pairs)


def couple_kernel(rows, own, *refs):
    far, (lanes, is_near, links, out, other, *work) = refs[:-8], refs[-8:]
    pairs = links.shape[1]
    total = work[-1]
    if len(far) == 1:
        for pair in range(pairs):
            value = far[0][pair]
            for at in range(0, ROWS, rows):
                other[pair * ROWS + at : pair * ROWS + at + rows, :] = value
    else:
        energies = rows // len(far)
        for row in range(ROWS):
            source = far[row % rows // energies]
            read = lambda at, size: source[row % energies, at : at + size, :]
            spread_rows(other, 0, row, read, 0, pairs)
    couple(own, other, lanes, is_near, links, *work)
    for pair in range(pairs):
        value = total[pair]
        width = ROWS // 2
        while width >= rows:
            value = value + pltpu.roll(value, width, 0)
            width //= 2
        out[pair] = value[:rows]
    for at in range(pairs, out.shape[0]):
        out[at] = jnp.zeros(out.shape[1:], jnp.float32)


def mix_kernel(fused, mixing, blocks, out, before, after):
    parts, share, rows, atoms = blocks.shape
    energies = rows // fused
    for f in range(fused):
        some = slice(f * energies, (f + 1) * energies)
        for part in range(parts):
            for pair in range(share):
                before[part * energies : (part + 1) * energies, pair * atoms : (pair + 1) * atoms] = (
                    blocks[part, pair, some, :]
                )
        after[...] = jnp.dot(
            mixing[f], before[...], precision=TOP_RANK, preferred_element_type=jnp.float32
        )
        for part in range(parts):
            for pair in range(share):
                out[part, pair, some, :] = after[
                    part * energies : (part + 1) * energies, pair * atoms : (pair + 1) * atoms
                ]


def dress(rows, sigma, left, right, copied, keep):
    parts = ROWS // rows
    for pair in range(NORB * NORB):
        value = sigma[pair]
        for part in range(parts):
            copied[pair, part * rows : (part + 1) * rows, :] = value
    for i in range(NORB // parts):
        inner = [None] * NORB
        for j in range(NORB):
            factor = left[i * NORB + j]
            for l in range(NORB):
                term = factor * copied[j * NORB + l]
                inner[l] = term if j == 0 else inner[l] + term
        for k in range(NORB):
            value = inner[0] * right[k * NORB]
            for l in range(1, NORB):
                value = value + inner[l] * right[k * NORB + l]
            keep(i * NORB + k, value)


def dress_between_kernel(rows, sigma, left, right, free, own, compact, copied):
    atoms = sigma.shape[2]
    share = left.shape[0]
    row_at = lax.broadcasted_iota(jnp.int32, (ROWS, atoms), 0)

    def keep(at, value):
        for part in range(ROWS // rows):
            held = (row_at >= part * rows) & (row_at < (part + 1) * rows)
            piece = jnp.where(held, value, 0.0)
            width = ROWS // 2
            while width >= rows:
                piece = piece + pltpu.roll(piece, width, 0)
                width //= 2
            pair = part * share + at
            piece = piece + free[pair * ROWS : (pair + 1) * ROWS, :]
            own[pair * ROWS : (pair + 1) * ROWS, :] = piece
            compact[pair] = piece[:rows]

    dress(rows, sigma, left, right, copied, keep)


def dress_last_kernel(*refs):
    sigma, left, right = refs[:3]
    free, out_hbm = refs[3:5], refs[5:7]
    copied, dressed, out, leaving = refs[7:]
    energies, pairs, _ = free[0].shape
    rows = 2 * energies
    parts = ROWS // rows
    share = left.shape[0]
    stage = 2 * NORB
    copies = []

    def keep(at, value):
        dressed[at * ROWS : (at + 1) * ROWS, :] = value
        if (at + 1) % stage and at + 1 < share:
            return
        done = at // stage * stage
        for row in range(ROWS):
            function, energy, part = row % rows // energies, row % energies, row // rows
            for begin in range(done, at + 1, ROWS):
                size = min(ROWS, at + 1 - begin)
                first = part * share + begin
                piece = dressed[pl.ds(begin * ROWS + row, size, stride=ROWS), :]
                out[function, energy, first : first + size, :] = (
                    free[function][energy, first : first + size, :] + piece
                )
        for function in range(2):
            for part in range(parts):
                some = pl.ds(part * share + done, at + 1 - done)
                copies.append(
                    pltpu.make_async_copy(
                        out.at[function, :, some, :],
                        out_hbm[function].at[:, some, :],
                        leaving.at[len(copies)],
                    )
                )
                copies[-1].start()

    dress(rows, sigma, left, right, copied, keep)
    for copy in copies:
        copy.wait()


def call(kernel, outs, scratch, flops, *operands, spaces=None, targets=None):
    shapes = [
        x if isinstance(x, jax.ShapeDtypeStruct) else jax.ShapeDtypeStruct(x, jnp.float32)
        for x in outs
    ]
    vmem = pl.BlockSpec(memory_space=pltpu.VMEM)
    moved = sum(x.size for x in operands) + sum(x.size for x in shapes)
    return pl.pallas_call(
        kernel,
        out_shape=shapes,
        in_specs=spaces or [vmem] * len(operands),
        out_specs=targets or [vmem] * len(shapes),
        scratch_shapes=scratch,
        compiler_params=PARAMS,
        cost_estimate=pl.CostEstimate(
            flops=flops, bytes_accessed=4 * moved, transcendentals=0
        ),
    )(*operands)


def beside(block):
    count = lax.axis_size("slab")
    if count == 2:
        return lax.ppermute(block, "slab", [(0, 1), (1, 0)])
    forward = [(i, i + 1) for i in range(count - 1)]
    backward = [(target, source) for source, target in forward]
    axis = block.ndim - 1
    atoms = block.shape[axis]
    low = lax.ppermute(lax.slice_in_dim(block, atoms - HW, atoms, axis=axis), "slab", forward)
    high = lax.ppermute(lax.slice_in_dim(block, 0, HW, axis=axis), "slab", backward)
    gap = jnp.zeros(block.shape[:-1] + (atoms - 2 * HW,), block.dtype)
    return jnp.concatenate([high, gap, low], axis=axis)


def body(
    lesser_free,
    greater_free,
    retarded,
    coupling,
    neighbour_offsets,
    phonon_shift,
    phonon_coupling,
    phonon_occupation,
):
    energies, pairs, atoms = lesser_free.shape
    rows = 2 * energies
    groups = NB * rows // ROWS
    parts = lax.axis_size("energy")
    share = -(-pairs // parts)
    total = energies * parts
    away = pl.BlockSpec(memory_space=pltpu.HBM)
    held = lambda *dims: pltpu.VMEM(dims, jnp.float32)
    wide = (pairs * ROWS, atoms)
    deep = (pairs, ROWS, atoms)
    thin = (pairs * rows, atoms)
    every = (parts * share, rows, atoms)
    flops = 4 * NORB * rows * pairs * atoms
    index = jax.ShapeDtypeStruct((groups, ROWS, atoms), jnp.int32)
    transfer = lambda count: pltpu.SemaphoreType.DMA((count,))

    free = (lesser_free, greater_free)
    halos = [beside(g) for g in free]
    phonons = (phonon_shift, phonon_coupling, phonon_occupation)
    constants = (retarded, *phonons, neighbour_offsets, coupling)
    own, left, right, mixing, links, lanes, is_near = call(
        prep_kernel,
        [wide, thin, wide, (2, total, total), (groups * wide[0], atoms), index, index],
        [held(2, *retarded.shape), held(*retarded.shape)]
        + [pltpu.SMEM(x.shape, x.dtype) for x in phonons]
        + [pltpu.VMEM(neighbour_offsets.shape, jnp.int32)]
        + [held(*coupling.shape), held(NB, atoms), transfer(7 + NB)],
        rows * coupling.size,
        *(pltpu.with_memory_space_constraint(x, pltpu.HBM) for x in (*free, *constants)),
        spaces=[away] * 8,
    )
    links = links.reshape(groups, pairs, ROWS, atoms)
    start = own
    left = left.reshape(pairs * rows // ROWS, ROWS, atoms)
    right = right.reshape(deep)

    for step in range(ITERS):
        if step > 0:
            own, compact = call(
                functools.partial(dress_between_kernel, rows),
                [wide, (pairs, rows, atoms)],
                [held(*deep)],
                flops,
                sigma,
                left,
                right,
                start,
            )
            halos = [beside(compact)]
        (coupled,) = call(
            functools.partial(couple_kernel, rows),
            [every],
            [held(*wide)] + [held(*deep)] * 3,
            NB * flops,
            own,
            *halos,
            lanes,
            is_near,
            links,
        )
        gathered = exchanged(coupled.reshape(parts, share, rows, atoms))
        (mixed,) = call(
            functools.partial(mix_kernel, 2),
            [gathered.shape],
            [held(total, share * atoms)] * 2,
            2 * total * gathered.size,
            mixing,
            gathered,
        )
        sigma = exchanged(mixed).reshape(every)
    stages = -(-thin[0] // (ROWS * 2 * NORB))
    return call(
        dress_last_kernel,
        [lesser_free.shape] * 2,
        [held(*deep), held(*thin), held(2, *lesser_free.shape)]
        + [transfer(stages * 2 * ROWS // rows)],
        flops,
        sigma,
        left,
        right,
        *free,
        targets=[away] * 2,
    )


def solution(mesh):
    placed = (
        P("energy", None, "slab"),
        P("energy", None, "slab"),
        P("energy", None, "slab"),
        P(None, None, "slab"),
        P(None, "slab"),
        P(),
        P(),
        P(),
    )
    return jax.shard_map(
        body,
        mesh=mesh,
        in_specs=placed,
        out_specs=(P("energy", None, "slab"), P("energy", None, "slab")),
        check_vma=False,
    )
```

```python
import functools
import math

import jax
import jax.numpy as jnp
from jax import lax
from jax.experimental import pallas as pl
from jax.experimental.pallas import tpu as pltpu
from jax.sharding import PartitionSpec as P

NORB = 12
NB = 12
HW = 32
ITERS = 2
ROWS = 8
LANES = 128
TALL, BROAD = 4, 6

TOP_RANK = lax.Precision.HIGHEST
PARAMS = pltpu.CompilerParams(vmem_limit_bytes=24 * 1024 * 1024)


def each(count, step):
    lax.fori_loop(0, count, lambda at, _: step(at), None)


def eight(at):
    return pl.ds(pl.multiple_of(at * ROWS, ROWS), ROWS)


def spread_rows(target, base, row, source, first, count):
    for at in range(0, count, ROWS):
        size = min(ROWS, count - at)
        rows = pl.ds((base + at) * ROWS + row, size, stride=ROWS)
        target[rows, :] = source(first + at, size)


def standing(place, parts, odd):
    root = math.isqrt(parts)
    root = root if parts % root == 0 else 1
    place = place + odd * (parts - 1 - 2 * place)
    return place % root * (parts // root) + place // root


def exchanged(shares):
    parts, slabs = lax.axis_size("energy"), lax.axis_size("slab")
    groups = [
        [standing(place, parts, slab % 2) * slabs + slab for place in range(parts)]
        for slab in range(slabs)
    ]
    return lax.all_to_all(shares, ("energy", "slab"), 0, 0, axis_index_groups=groups)


def index_neighbours(rows, offsets, lanes, is_near, inside):
    atoms = offsets.shape[1]
    group = ROWS // rows
    slab, slabs = lax.axis_index("slab"), lax.axis_size("slab")
    targets = offsets[...] + lax.broadcasted_iota(jnp.int32, (NB, atoms), 1)
    placed = targets + slab * atoms
    inside[...] = ((placed >= 0) & (placed < slabs * atoms)).astype(jnp.float32)
    near = ((targets >= 0) & (targets < atoms)).astype(jnp.int32)
    lane = jnp.where(targets < 0, targets + atoms, targets)
    lane = jnp.where(lane >= atoms, lane - atoms, lane)
    for n in range(NB):
        some = slice(n % group * rows, (n % group + 1) * rows)
        lanes[n // group, some, :] = jnp.broadcast_to(lane[n : n + 1, :], (rows, atoms))
        is_near[n // group, some, :] = jnp.broadcast_to(near[n : n + 1, :], (rows, atoms))


def couple(own, other, lanes, is_near, links, gathered_a, gathered_b, inner_a, inner_b, total):
    groups, pairs = links.shape[:2]
    across = NORB // BROAD
    steps = NORB // TALL * across
    chunk = pairs // steps
    gathered, inner = (gathered_a, gathered_b), (inner_a, inner_b)

    def gather(target, g, step):
        lane, mine = lanes[g], is_near[g] != 0
        for at in range(chunk):
            pair = step * chunk + at
            near = jnp.take_along_axis(own[eight(pair), :], lane, axis=1, mode="promise_in_bounds")
            far = jnp.take_along_axis(other[eight(pair), :], lane, axis=1, mode="promise_in_bounds")
            target[pair] = jnp.where(mine, near, far)

    def corner(step):
        return step // across * TALL, step % across * BROAD

    def left_stage(g, source, target, step):
        top, side = corner(step)
        sums = [[None] * BROAD for _ in range(TALL)]
        for j in range(NORB):
            left = [links[g, (top + i) * NORB + j] for i in range(TALL)]
            right = [source[j * NORB + side + l] for l in range(BROAD)]
            for i in range(TALL):
                for l in range(BROAD):
                    term = left[i] * right[l]
                    sums[i][l] = term if j == 0 else sums[i][l] + term
        for i in range(TALL):
            for l in range(BROAD):
                target[(top + i) * NORB + side + l] = sums[i][l]

    def right_stage(g, source, step):
        top, side = corner(step)
        places = [[(top + i) * NORB + side + k for k in range(BROAD)] for i in range(TALL)]
        sums = [[total[place] for place in row] for row in places]
        for l in range(NORB):
            left = [source[(top + i) * NORB + l] for i in range(TALL)]
            right = [links[g, (side + k) * NORB + l] for k in range(BROAD)]
            for i in range(TALL):
                for k in range(BROAD):
                    sums[i][k] = sums[i][k] + left[i] * right[k]
        for i in range(TALL):
            for k in range(BROAD):
                total[places[i][k]] = sums[i][k]

    def clear(step):
        for at in range(chunk):
            total[step * chunk + at] = jnp.zeros(total.shape[1:], jnp.float32)
        gather(gathered_a, 0, step)

    def first_group(step):
        left_stage(0, gathered_a, inner_a, step)
        gather(gathered_b, min(1, groups - 1), step)

    def group_steps(g, odd):
        following = jnp.minimum(g + 1, groups - 1)

        def block(step):
            right_stage(g - 1, inner[1 - odd], step)
            left_stage(g, gathered[odd], inner[odd], step)
            gather(gathered[1 - odd], following, step)

        each(steps, block)

    def two_groups(half):
        group_steps(half * 2 + 1, 1)
        group_steps(half * 2 + 2, 0)

    each(steps, clear)
    each(steps, first_group)
    each((groups - 1) // 2, two_groups)
    if groups % 2 == 0:
        group_steps(groups - 1, 1)
    each(steps, lambda step: right_stage(groups - 1, inner[(groups - 1) % 2], step))


def mix_weights(mixing, energies, shifts, coupled, occupied):
    total = mixing.shape[1]
    parts, odd = total // energies, lax.axis_index("slab") % 2

    def energy_at(index):
        return standing(index // energies, parts, odd) * energies + index % energies

    lane = lax.broadcasted_iota(jnp.int32, (ROWS, LANES), 1)
    row = lax.broadcasted_iota(jnp.int32, (ROWS, LANES), 0)
    emitted = jnp.zeros((ROWS, LANES), jnp.float32)
    absorbed = jnp.zeros((ROWS, LANES), jnp.float32)
    for mode in range(shifts.shape[0]):
        hit = lane == shifts[mode]
        absorb = coupled[mode] * occupied[mode]
        emit = coupled[mode] * (occupied[mode] + 1.0)
        emitted = emitted + jnp.where(hit, emit, 0.0)
        absorbed = absorbed + jnp.where(hit, absorb, 0.0)
    for at in range(0, total, ROWS):
        for first in range(0, total, LANES):
            width = min(LANES, total - first)
            gap = energy_at(lane + first) - energy_at(row + at)
            far = jnp.minimum(jnp.abs(gap), LANES - 1)
            emit = jnp.take_along_axis(emitted, far, axis=1, mode="promise_in_bounds")
            absorb = jnp.take_along_axis(absorbed, far, axis=1, mode="promise_in_bounds")
            some = slice(first, first + width)
            mixing[0, at : at + ROWS, some] = jnp.where(gap > 0, emit, absorb)[:, :width]
            mixing[1, at : at + ROWS, some] = jnp.where(gap > 0, absorb, emit)[:, :width]


def prep_kernel(*refs):
    free_hbm, retarded_hbm, modes_hbm = refs[0:2], refs[2], refs[3:6]
    offsets_hbm, coupling_hbm = refs[6:8]
    start, left, right, mixing, links, lanes, is_near = refs[8:15]
    free, retarded, shifts, coupled, occupied, offsets, coupling, inside, sems = refs[15:]
    energies, pairs, _ = retarded.shape
    rows = 2 * energies
    group = ROWS // rows
    share = left.shape[0] // ROWS
    moves = list(zip(modes_hbm, (shifts, coupled, occupied))) + [(offsets_hbm, offsets)]
    moves += [(free_hbm[f], free.at[f]) for f in range(2)] + [(retarded_hbm, retarded)]
    moves += [(coupling_hbm.at[n], coupling.at[n]) for n in range(NB)]
    copies = [
        pltpu.make_async_copy(source, target, sems.at[at])
        for at, (source, target) in enumerate(moves)
    ]
    for copy in copies:
        copy.start()

    for copy in copies[:4]:
        copy.wait()
    mix_weights(mixing, energies, shifts, coupled, occupied)
    index_neighbours(rows, offsets, lanes, is_near, inside)
    copies[4].wait()
    copies[5].wait()
    for row in range(ROWS):
        function, energy = row % rows // energies, row % energies
        read = lambda at, size: free[function, energy, at : at + size, :]
        spread_rows(start, 0, row, read, 0, pairs)
    copies[6].wait()
    for row in range(ROWS):
        skipped = row // rows * share
        read = lambda at, size: retarded[row % energies, at : at + size, :]
        spread_rows(left, 0, row, read, skipped, share)
        spread_rows(right, 0, row, read, 0, pairs)
    for n in range(NB):
        copies[7 + n].wait()
        valid = inside[n : n + 1, :]
        for row in range(rows):
            read = lambda at, size: coupling[n, at : at + size, :] * valid
            spread_rows(links, n // group * pairs, n % group * rows + row, read, 0, pairs)


def couple_kernel(rows, own, *refs):
    far, (lanes, is_near, links, out, other, *work) = refs[:-10], refs[-10:]
    pairs = links.shape[1]
    total = work[-1]
    if len(far) == 1:
        for pair in range(pairs):
            value = far[0][pair]
            for at in range(0, ROWS, rows):
                other[pair * ROWS + at : pair * ROWS + at + rows, :] = value
    else:
        energies = rows // len(far)
        for row in range(ROWS):
            source = far[row % rows // energies]
            read = lambda at, size: source[row % energies, at : at + size, :]
            spread_rows(other, 0, row, read, 0, pairs)
    couple(own, other, lanes, is_near, links, *work)
    for pair in range(pairs):
        value = total[pair]
        width = ROWS // 2
        while width >= rows:
            value = value + pltpu.roll(value, width, 0)
            width //= 2
        out[pair] = value[:rows]
    for at in range(pairs, out.shape[0]):
        out[at] = jnp.zeros(out.shape[1:], jnp.float32)


def mix_kernel(fused, mixing, blocks, out, before, after):
    parts, share, rows, atoms = blocks.shape
    energies = rows // fused
    for f in range(fused):
        some = slice(f * energies, (f + 1) * energies)
        for part in range(parts):
            for pair in range(share):
                before[part * energies : (part + 1) * energies, pair * atoms : (pair + 1) * atoms] = (
                    blocks[part, pair, some, :]
                )
        after[...] = jnp.dot(
            mixing[f], before[...], precision=TOP_RANK, preferred_element_type=jnp.float32
        )
        for part in range(parts):
            for pair in range(share):
                out[part, pair, some, :] = after[
                    part * energies : (part + 1) * energies, pair * atoms : (pair + 1) * atoms
                ]


def dress(rows, sigma, left, right, copied, keep):
    parts = ROWS // rows
    for pair in range(NORB * NORB):
        value = sigma[pair]
        for part in range(parts):
            copied[pair, part * rows : (part + 1) * rows, :] = value
    for i in range(NORB // parts):
        inner = [None] * NORB
        for j in range(NORB):
            factor = left[i * NORB + j]
            for l in range(NORB):
                term = factor * copied[j * NORB + l]
                inner[l] = term if j == 0 else inner[l] + term
        for k in range(NORB):
            value = inner[0] * right[k * NORB]
            for l in range(1, NORB):
                value = value + inner[l] * right[k * NORB + l]
            keep(i * NORB + k, value)


def dress_between_kernel(rows, sigma, left, right, free, own, compact, copied):
    atoms = sigma.shape[2]
    share = left.shape[0]
    row_at = lax.broadcasted_iota(jnp.int32, (ROWS, atoms), 0)

    def keep(at, value):
        for part in range(ROWS // rows):
            held = (row_at >= part * rows) & (row_at < (part + 1) * rows)
            piece = jnp.where(held, value, 0.0)
            width = ROWS // 2
            while width >= rows:
                piece = piece + pltpu.roll(piece, width, 0)
                width //= 2
            pair = part * share + at
            piece = piece + free[pair * ROWS : (pair + 1) * ROWS, :]
            own[pair * ROWS : (pair + 1) * ROWS, :] = piece
            compact[pair] = piece[:rows]

    dress(rows, sigma, left, right, copied, keep)


def dress_last_kernel(*refs):
    sigma, left, right = refs[:3]
    free, out_hbm = refs[3:5], refs[5:7]
    copied, dressed, out, leaving = refs[7:]
    energies, pairs, _ = free[0].shape
    rows = 2 * energies
    parts = ROWS // rows
    share = left.shape[0]
    stage = 2 * NORB
    copies = []

    def keep(at, value):
        dressed[at * ROWS : (at + 1) * ROWS, :] = value
        if (at + 1) % stage and at + 1 < share:
            return
        done = at // stage * stage
        for row in range(ROWS):
            function, energy, part = row % rows // energies, row % energies, row // rows
            for begin in range(done, at + 1, ROWS):
                size = min(ROWS, at + 1 - begin)
                first = part * share + begin
                piece = dressed[pl.ds(begin * ROWS + row, size, stride=ROWS), :]
                out[function, energy, first : first + size, :] = (
                    free[function][energy, first : first + size, :] + piece
                )
        for function in range(2):
            for part in range(parts):
                some = pl.ds(part * share + done, at + 1 - done)
                copies.append(
                    pltpu.make_async_copy(
                        out.at[function, :, some, :],
                        out_hbm[function].at[:, some, :],
                        leaving.at[len(copies)],
                    )
                )
                copies[-1].start()

    dress(rows, sigma, left, right, copied, keep)
    for copy in copies:
        copy.wait()


def call(kernel, outs, scratch, flops, *operands, spaces=None, targets=None):
    shapes = [
        x if isinstance(x, jax.ShapeDtypeStruct) else jax.ShapeDtypeStruct(x, jnp.float32)
        for x in outs
    ]
    vmem = pl.BlockSpec(memory_space=pltpu.VMEM)
    moved = sum(x.size for x in operands) + sum(x.size for x in shapes)
    return pl.pallas_call(
        kernel,
        out_shape=shapes,
        in_specs=spaces or [vmem] * len(operands),
        out_specs=targets or [vmem] * len(shapes),
        scratch_shapes=scratch,
        compiler_params=PARAMS,
        cost_estimate=pl.CostEstimate(
            flops=flops, bytes_accessed=4 * moved, transcendentals=0
        ),
    )(*operands)


def beside(block):
    count = lax.axis_size("slab")
    if count == 2:
        return lax.ppermute(block, "slab", [(0, 1), (1, 0)])
    forward = [(i, i + 1) for i in range(count - 1)]
    backward = [(target, source) for source, target in forward]
    axis = block.ndim - 1
    atoms = block.shape[axis]
    low = lax.ppermute(lax.slice_in_dim(block, atoms - HW, atoms, axis=axis), "slab", forward)
    high = lax.ppermute(lax.slice_in_dim(block, 0, HW, axis=axis), "slab", backward)
    gap = jnp.zeros(block.shape[:-1] + (atoms - 2 * HW,), block.dtype)
    return jnp.concatenate([high, gap, low], axis=axis)


def body(
    lesser_free,
    greater_free,
    retarded,
    coupling,
    neighbour_offsets,
    phonon_shift,
    phonon_coupling,
    phonon_occupation,
):
    energies, pairs, atoms = lesser_free.shape
    rows = 2 * energies
    groups = NB * rows // ROWS
    parts = lax.axis_size("energy")
    share = -(-pairs // parts)
    total = energies * parts
    away = pl.BlockSpec(memory_space=pltpu.HBM)
    held = lambda *dims: pltpu.VMEM(dims, jnp.float32)
    wide = (pairs * ROWS, atoms)
    deep = (pairs, ROWS, atoms)
    thin = (pairs * rows, atoms)
    every = (parts * share, rows, atoms)
    flops = 4 * NORB * rows * pairs * atoms
    index = jax.ShapeDtypeStruct((groups, ROWS, atoms), jnp.int32)
    transfer = lambda count: pltpu.SemaphoreType.DMA((count,))

    free = (lesser_free, greater_free)
    halos = [beside(g) for g in free]
    phonons = (phonon_shift, phonon_coupling, phonon_occupation)
    constants = (retarded, *phonons, neighbour_offsets, coupling)
    own, left, right, mixing, links, lanes, is_near = call(
        prep_kernel,
        [wide, thin, wide, (2, total, total), (groups * wide[0], atoms), index, index],
        [held(2, *retarded.shape), held(*retarded.shape)]
        + [pltpu.SMEM(x.shape, x.dtype) for x in phonons]
        + [pltpu.VMEM(neighbour_offsets.shape, jnp.int32)]
        + [held(*coupling.shape), held(NB, atoms), transfer(7 + NB)],
        rows * coupling.size,
        *(pltpu.with_memory_space_constraint(x, pltpu.HBM) for x in (*free, *constants)),
        spaces=[away] * 8,
    )
    links = links.reshape(groups, pairs, ROWS, atoms)
    start = own
    left = left.reshape(pairs * rows // ROWS, ROWS, atoms)
    right = right.reshape(deep)

    for step in range(ITERS):
        if step > 0:
            own, compact = call(
                functools.partial(dress_between_kernel, rows),
                [wide, (pairs, rows, atoms)],
                [held(*deep)],
                flops,
                sigma,
                left,
                right,
                start,
            )
            halos = [beside(compact)]
        (coupled,) = call(
            functools.partial(couple_kernel, rows),
            [every],
            [held(*wide)] + [held(*deep)] * 5,
            NB * flops,
            own,
            *halos,
            lanes,
            is_near,
            links,
        )
        gathered = exchanged(coupled.reshape(parts, share, rows, atoms))
        (mixed,) = call(
            functools.partial(mix_kernel, 2),
            [gathered.shape],
            [held(total, share * atoms)] * 2,
            2 * total * gathered.size,
            mixing,
            gathered,
        )
        sigma = exchanged(mixed).reshape(every)
    stages = -(-thin[0] // (ROWS * 2 * NORB))
    return call(
        dress_last_kernel,
        [lesser_free.shape] * 2,
        [held(*deep), held(*thin), held(2, *lesser_free.shape)]
        + [transfer(stages * 2 * ROWS // rows)],
        flops,
        sigma,
        left,
        right,
        *free,
        targets=[away] * 2,
    )


def solution(mesh):
    placed = (
        P("energy", None, "slab"),
        P("energy", None, "slab"),
        P("energy", None, "slab"),
        P(None, None, "slab"),
        P(None, "slab"),
        P(),
        P(),
        P(),
    )
    return jax.shard_map(
        body,
        mesh=mesh,
        in_specs=placed,
        out_specs=(P("energy", None, "slab"), P("energy", None, "slab")),
        check_vma=False,
    )
```

```python
import functools
import math

import jax
import jax.numpy as jnp
from jax import lax
from jax.experimental import pallas as pl
from jax.experimental.pallas import tpu as pltpu
from jax.sharding import PartitionSpec as P

NORB = 12
NB = 12
HW = 32
ITERS = 2
ROWS = 8
LANES = 128
BLOCKED = 2
BROAD = 6

TOP_RANK = lax.Precision.HIGHEST
PARAMS = pltpu.CompilerParams(vmem_limit_bytes=24 * 1024 * 1024)


def each(count, step):
    lax.fori_loop(0, count, lambda at, _: step(at), None)


def eight(at):
    return pl.ds(pl.multiple_of(at * ROWS, ROWS), ROWS)


def spread_rows(target, base, row, source, first, count):
    for at in range(0, count, ROWS):
        size = min(ROWS, count - at)
        rows = pl.ds((base + at) * ROWS + row, size, stride=ROWS)
        target[rows, :] = source(first + at, size)


def standing(place, parts, odd):
    root = math.isqrt(parts)
    root = root if parts % root == 0 else 1
    place = place + odd * (parts - 1 - 2 * place)
    return place % root * (parts // root) + place // root


def exchanged(shares):
    parts, slabs = lax.axis_size("energy"), lax.axis_size("slab")
    groups = [
        [standing(place, parts, slab % 2) * slabs + slab for place in range(parts)]
        for slab in range(slabs)
    ]
    return lax.all_to_all(shares, ("energy", "slab"), 0, 0, axis_index_groups=groups)


def index_neighbours(rows, offsets, lanes, is_near, inside):
    atoms = offsets.shape[1]
    group = ROWS // rows
    slab, slabs = lax.axis_index("slab"), lax.axis_size("slab")
    targets = offsets[...] + lax.broadcasted_iota(jnp.int32, (NB, atoms), 1)
    placed = targets + slab * atoms
    inside[...] = ((placed >= 0) & (placed < slabs * atoms)).astype(jnp.float32)
    near = ((targets >= 0) & (targets < atoms)).astype(jnp.int32)
    lane = jnp.where(targets < 0, targets + atoms, targets)
    lane = jnp.where(lane >= atoms, lane - atoms, lane)
    for n in range(NB):
        some = slice(n % group * rows, (n % group + 1) * rows)
        lanes[n // group, some, :] = jnp.broadcast_to(lane[n : n + 1, :], (rows, atoms))
        is_near[n // group, some, :] = jnp.broadcast_to(near[n : n + 1, :], (rows, atoms))


def couple(own, other, lanes, is_near, links, gathered_a, gathered_b, total):
    groups, pairs = links.shape[:2]
    steps = NORB // BLOCKED
    chunk = pairs // steps

    def gather(target, g, step):
        lane, mine = lanes[g], is_near[g] != 0
        for at in range(chunk):
            pair = step * chunk + at
            inner = jnp.take_along_axis(own[eight(pair), :], lane, axis=1, mode="promise_in_bounds")
            outer = jnp.take_along_axis(other[eight(pair), :], lane, axis=1, mode="promise_in_bounds")
            target[pair] = jnp.where(mine, inner, outer)

    def group_sums(g, source, target):
        following = jnp.minimum(g + 1, groups - 1)

        def block_row(step):
            first = step * BLOCKED
            inner = [[None] * NORB for _ in range(BLOCKED)]
            for j in range(NORB):
                left = [links[g, (first + b) * NORB + j] for b in range(BLOCKED)]
                for l in range(NORB):
                    value = source[j * NORB + l]
                    for b in range(BLOCKED):
                        term = left[b] * value
                        inner[b][l] = term if j == 0 else inner[b][l] + term
            for side in range(0, NORB, BROAD):
                at = [
                    (b, (first + b) * NORB + k, k)
                    for k in range(side, side + BROAD)
                    for b in range(BLOCKED)
                ]
                sums = [total[place] for _, place, _ in at]
                for l in range(NORB):
                    right = {k: links[g, k * NORB + l] for k in range(side, side + BROAD)}
                    sums = [x + inner[b][l] * right[k] for x, (b, _, k) in zip(sums, at)]
                for x, (_, place, _) in zip(sums, at):
                    total[place] = x
            gather(target, following, step)

        each(steps, block_row)

    def clear(step):
        for at in range(chunk):
            total[step * chunk + at] = jnp.zeros(total.shape[1:], jnp.float32)
        gather(gathered_a, 0, step)

    def two_groups(half):
        group_sums(half * 2, gathered_a, gathered_b)
        group_sums(half * 2 + 1, gathered_b, gathered_a)

    each(steps, clear)
    each(groups // 2, two_groups)
    if groups % 2:
        group_sums(groups - 1, gathered_a, gathered_b)


def mix_weights(mixing, energies, shifts, coupled, occupied):
    total = mixing.shape[0]
    rows = 2 * energies
    parts, odd = total // rows, lax.axis_index("slab") % 2

    def energy_at(index):
        return standing(index // rows, parts, odd) * energies + index % energies

    lane = lax.broadcasted_iota(jnp.int32, (ROWS, LANES), 1)
    row = lax.broadcasted_iota(jnp.int32, (ROWS, LANES), 0)
    emitted = jnp.zeros((ROWS, LANES), jnp.float32)
    absorbed = jnp.zeros((ROWS, LANES), jnp.float32)
    for mode in range(shifts.shape[0]):
        hit = lane == shifts[mode]
        absorb = coupled[mode] * occupied[mode]
        emit = coupled[mode] * (occupied[mode] + 1.0)
        emitted = emitted + jnp.where(hit, emit, 0.0)
        absorbed = absorbed + jnp.where(hit, absorb, 0.0)
    for at in range(0, total, ROWS):
        for first in range(0, total, LANES):
            width = min(LANES, total - first)
            gap = energy_at(lane + first) - energy_at(row + at)
            far = jnp.minimum(jnp.abs(gap), LANES - 1)
            emit = jnp.take_along_axis(emitted, far, axis=1, mode="promise_in_bounds")
            absorb = jnp.take_along_axis(absorbed, far, axis=1, mode="promise_in_bounds")
            some = slice(first, first + width)
            function = (row + at) % rows // energies
            weight = jnp.where((gap > 0) == (function == 0), emit, absorb)
            weight = jnp.where((lane + first) % rows // energies == function, weight, 0.0)
            mixing[at : at + ROWS, some] = weight[:, :width]


def prep_kernel(*refs):
    free_hbm, retarded_hbm, modes_hbm = refs[0:2], refs[2], refs[3:6]
    offsets_hbm, coupling_hbm = refs[6:8]
    start, left, right, mixing, links, lanes, is_near = refs[8:15]
    free, retarded, shifts, coupled, occupied, offsets, coupling, inside, sems = refs[15:]
    energies, pairs, _ = retarded.shape
    rows = 2 * energies
    group = ROWS // rows
    share = left.shape[0] // ROWS
    moves = list(zip(modes_hbm, (shifts, coupled, occupied))) + [(offsets_hbm, offsets)]
    moves += [(free_hbm[f], free.at[f]) for f in range(2)] + [(retarded_hbm, retarded)]
    moves += [(coupling_hbm.at[n], coupling.at[n]) for n in range(NB)]
    copies = [
        pltpu.make_async_copy(source, target, sems.at[at])
        for at, (source, target) in enumerate(moves)
    ]
    for copy in copies:
        copy.start()

    for copy in copies[:4]:
        copy.wait()
    mix_weights(mixing, energies, shifts, coupled, occupied)
    index_neighbours(rows, offsets, lanes, is_near, inside)
    copies[4].wait()
    copies[5].wait()
    for row in range(ROWS):
        function, energy = row % rows // energies, row % energies
        read = lambda at, size: free[function, energy, at : at + size, :]
        spread_rows(start, 0, row, read, 0, pairs)
    copies[6].wait()
    for row in range(ROWS):
        skipped = row // rows * share
        read = lambda at, size: retarded[row % energies, at : at + size, :]
        spread_rows(left, 0, row, read, skipped, share)
        spread_rows(right, 0, row, read, 0, pairs)
    for n in range(NB):
        copies[7 + n].wait()
        valid = inside[n : n + 1, :]
        for row in range(rows):
            read = lambda at, size: coupling[n, at : at + size, :] * valid
            spread_rows(links, n // group * pairs, n % group * rows + row, read, 0, pairs)


def couple_kernel(rows, own, *refs):
    far, (lanes, is_near, links, out, other, *work) = refs[:-8], refs[-8:]
    pairs = links.shape[1]
    total = work[-1]
    if len(far) == 1:
        for pair in range(pairs):
            value = far[0][pair]
            for at in range(0, ROWS, rows):
                other[pair * ROWS + at : pair * ROWS + at + rows, :] = value
    else:
        energies = rows // len(far)
        for row in range(ROWS):
            source = far[row % rows // energies]
            read = lambda at, size: source[row % energies, at : at + size, :]
            spread_rows(other, 0, row, read, 0, pairs)
    couple(own, other, lanes, is_near, links, *work)
    for pair in range(pairs):
        value = total[pair]
        width = ROWS // 2
        while width >= rows:
            value = value + pltpu.roll(value, width, 0)
            width //= 2
        out[pair] = value[:rows]
    for at in range(pairs, out.shape[0]):
        out[at] = jnp.zeros(out.shape[1:], jnp.float32)


def mix_kernel(mixing, blocks, out, before, after):
    parts, share, rows, atoms = blocks.shape
    for part in range(parts):
        for pair in range(share):
            lanes = slice(pair * atoms, (pair + 1) * atoms)
            before[part * rows : (part + 1) * rows, lanes] = blocks[part, pair]
    after[...] = jnp.dot(
        mixing[...], before[...], precision=TOP_RANK, preferred_element_type=jnp.float32
    )
    for part in range(parts):
        for pair in range(share):
            lanes = slice(pair * atoms, (pair + 1) * atoms)
            out[part, pair] = after[part * rows : (part + 1) * rows, lanes]


def dress(rows, sigma, left, right, copied, keep):
    parts = ROWS // rows
    for pair in range(NORB * NORB):
        value = sigma[pair]
        for part in range(parts):
            copied[pair, part * rows : (part + 1) * rows, :] = value
    for i in range(NORB // parts):
        inner = [None] * NORB
        for j in range(NORB):
            factor = left[i * NORB + j]
            for l in range(NORB):
                term = factor * copied[j * NORB + l]
                inner[l] = term if j == 0 else inner[l] + term
        for k in range(NORB):
            value = inner[0] * right[k * NORB]
            for l in range(1, NORB):
                value = value + inner[l] * right[k * NORB + l]
            keep(i * NORB + k, value)


def dress_between_kernel(rows, sigma, left, right, free, own, compact, copied):
    atoms = sigma.shape[2]
    share = left.shape[0]
    row_at = lax.broadcasted_iota(jnp.int32, (ROWS, atoms), 0)

    def keep(at, value):
        for part in range(ROWS // rows):
            held = (row_at >= part * rows) & (row_at < (part + 1) * rows)
            piece = jnp.where(held, value, 0.0)
            width = ROWS // 2
            while width >= rows:
                piece = piece + pltpu.roll(piece, width, 0)
                width //= 2
            pair = part * share + at
            piece = piece + free[pair * ROWS : (pair + 1) * ROWS, :]
            own[pair * ROWS : (pair + 1) * ROWS, :] = piece
            compact[pair] = piece[:rows]

    dress(rows, sigma, left, right, copied, keep)


def dress_last_kernel(*refs):
    sigma, left, right = refs[:3]
    free, out_hbm = refs[3:5], refs[5:7]
    copied, dressed, out, leaving = refs[7:]
    energies, pairs, _ = free[0].shape
    rows = 2 * energies
    parts = ROWS // rows
    share = left.shape[0]
    stage = 2 * NORB
    copies = []

    def keep(at, value):
        dressed[at * ROWS : (at + 1) * ROWS, :] = value
        if (at + 1) % stage and at + 1 < share:
            return
        done = at // stage * stage
        for row in range(ROWS):
            function, energy, part = row % rows // energies, row % energies, row // rows
            for begin in range(done, at + 1, ROWS):
                size = min(ROWS, at + 1 - begin)
                first = part * share + begin
                piece = dressed[pl.ds(begin * ROWS + row, size, stride=ROWS), :]
                out[function, energy, first : first + size, :] = (
                    free[function][energy, first : first + size, :] + piece
                )
        for function in range(2):
            for part in range(parts):
                some = pl.ds(part * share + done, at + 1 - done)
                copies.append(
                    pltpu.make_async_copy(
                        out.at[function, :, some, :],
                        out_hbm[function].at[:, some, :],
                        leaving.at[len(copies)],
                    )
                )
                copies[-1].start()

    dress(rows, sigma, left, right, copied, keep)
    for copy in copies:
        copy.wait()


def call(kernel, outs, scratch, flops, *operands, spaces=None, targets=None):
    shapes = [
        x if isinstance(x, jax.ShapeDtypeStruct) else jax.ShapeDtypeStruct(x, jnp.float32)
        for x in outs
    ]
    vmem = pl.BlockSpec(memory_space=pltpu.VMEM)
    moved = sum(x.size for x in operands) + sum(x.size for x in shapes)
    return pl.pallas_call(
        kernel,
        out_shape=shapes,
        in_specs=spaces or [vmem] * len(operands),
        out_specs=targets or [vmem] * len(shapes),
        scratch_shapes=scratch,
        compiler_params=PARAMS,
        cost_estimate=pl.CostEstimate(
            flops=flops, bytes_accessed=4 * moved, transcendentals=0
        ),
    )(*operands)


def beside(block):
    count = lax.axis_size("slab")
    if count == 2:
        return lax.ppermute(block, "slab", [(0, 1), (1, 0)])
    forward = [(i, i + 1) for i in range(count - 1)]
    backward = [(target, source) for source, target in forward]
    axis = block.ndim - 1
    atoms = block.shape[axis]
    low = lax.ppermute(lax.slice_in_dim(block, atoms - HW, atoms, axis=axis), "slab", forward)
    high = lax.ppermute(lax.slice_in_dim(block, 0, HW, axis=axis), "slab", backward)
    gap = jnp.zeros(block.shape[:-1] + (atoms - 2 * HW,), block.dtype)
    return jnp.concatenate([high, gap, low], axis=axis)


def body(
    lesser_free,
    greater_free,
    retarded,
    coupling,
    neighbour_offsets,
    phonon_shift,
    phonon_coupling,
    phonon_occupation,
):
    energies, pairs, atoms = lesser_free.shape
    rows = 2 * energies
    groups = NB * rows // ROWS
    parts = lax.axis_size("energy")
    share = -(-pairs // parts)
    total = rows * parts
    away = pl.BlockSpec(memory_space=pltpu.HBM)
    held = lambda *dims: pltpu.VMEM(dims, jnp.float32)
    wide = (pairs * ROWS, atoms)
    deep = (pairs, ROWS, atoms)
    thin = (pairs * rows, atoms)
    every = (parts * share, rows, atoms)
    flops = 4 * NORB * rows * pairs * atoms
    index = jax.ShapeDtypeStruct((groups, ROWS, atoms), jnp.int32)
    transfer = lambda count: pltpu.SemaphoreType.DMA((count,))

    free = (lesser_free, greater_free)
    halos = [beside(g) for g in free]
    phonons = (phonon_shift, phonon_coupling, phonon_occupation)
    constants = (retarded, *phonons, neighbour_offsets, coupling)
    own, left, right, mixing, links, lanes, is_near = call(
        prep_kernel,
        [wide, thin, wide, (total, total), (groups * wide[0], atoms), index, index],
        [held(2, *retarded.shape), held(*retarded.shape)]
        + [pltpu.SMEM(x.shape, x.dtype) for x in phonons]
        + [pltpu.VMEM(neighbour_offsets.shape, jnp.int32)]
        + [held(*coupling.shape), held(NB, atoms), transfer(7 + NB)],
        rows * coupling.size,
        *(pltpu.with_memory_space_constraint(x, pltpu.HBM) for x in (*free, *constants)),
        spaces=[away] * 8,
    )
    links = links.reshape(groups, pairs, ROWS, atoms)
    start = own
    left = left.reshape(pairs * rows // ROWS, ROWS, atoms)
    right = right.reshape(deep)

    for step in range(ITERS):
        if step > 0:
            own, compact = call(
                functools.partial(dress_between_kernel, rows),
                [wide, (pairs, rows, atoms)],
                [held(*deep)],
                flops,
                sigma,
                left,
                right,
                start,
            )
            halos = [beside(compact)]
        (coupled,) = call(
            functools.partial(couple_kernel, rows),
            [every],
            [held(*wide)] + [held(*deep)] * 3,
            NB * flops,
            own,
            *halos,
            lanes,
            is_near,
            links,
        )
        gathered = exchanged(coupled.reshape(parts, share, rows, atoms))
        (mixed,) = call(
            mix_kernel,
            [gathered.shape],
            [held(total, share * atoms)] * 2,
            2 * total * gathered.size,
            mixing,
            gathered,
        )
        sigma = exchanged(mixed).reshape(every)
    stages = -(-thin[0] // (ROWS * 2 * NORB))
    return call(
        dress_last_kernel,
        [lesser_free.shape] * 2,
        [held(*deep), held(*thin), held(2, *lesser_free.shape)]
        + [transfer(stages * 2 * ROWS // rows)],
        flops,
        sigma,
        left,
        right,
        *free,
        targets=[away] * 2,
    )


def solution(mesh):
    placed = (
        P("energy", None, "slab"),
        P("energy", None, "slab"),
        P("energy", None, "slab"),
        P(None, None, "slab"),
        P(None, "slab"),
        P(),
        P(),
        P(),
    )
    return jax.shard_map(
        body,
        mesh=mesh,
        in_specs=placed,
        out_specs=(P("energy", None, "slab"), P("energy", None, "slab")),
        check_vma=False,
    )
```

```python
import functools
import math

import jax
import jax.numpy as jnp
from jax import lax
from jax.experimental import pallas as pl
from jax.experimental.pallas import tpu as pltpu
from jax.sharding import PartitionSpec as P

NORB = 12
NB = 12
HW = 32
ITERS = 2
ROWS = 8
LANES = 128
BLOCKED = 2
BROAD = 6

TOP_RANK = lax.Precision.HIGHEST
PARAMS = pltpu.CompilerParams(vmem_limit_bytes=24 * 1024 * 1024)


def each(count, step):
    lax.fori_loop(0, count, lambda at, _: step(at), None)


def eight(at):
    return pl.ds(pl.multiple_of(at * ROWS, ROWS), ROWS)


def spread_rows(target, base, row, source, first, count):
    for at in range(0, count, ROWS):
        size = min(ROWS, count - at)
        rows = pl.ds((base + at) * ROWS + row, size, stride=ROWS)
        target[rows, :] = source(first + at, size)


def standing(place, parts):
    root = math.isqrt(parts)
    root = root if parts % root == 0 else 1
    return place % root * (parts // root) + place // root


def exchanged(shares):
    parts, slabs = lax.axis_size("energy"), lax.axis_size("slab")
    groups = [
        [standing(place, parts) * slabs + slab for place in range(parts)]
        for slab in range(slabs)
    ]
    return lax.all_to_all(shares, ("energy", "slab"), 0, 0, axis_index_groups=groups)


def index_neighbours(rows, offsets, lanes, is_near, inside):
    atoms = offsets.shape[1]
    group = ROWS // rows
    slab, slabs = lax.axis_index("slab"), lax.axis_size("slab")
    targets = offsets[...] + lax.broadcasted_iota(jnp.int32, (NB, atoms), 1)
    placed = targets + slab * atoms
    inside[...] = ((placed >= 0) & (placed < slabs * atoms)).astype(jnp.float32)
    near = ((targets >= 0) & (targets < atoms)).astype(jnp.int32)
    lane = jnp.where(targets < 0, targets + atoms, targets)
    lane = jnp.where(lane >= atoms, lane - atoms, lane)
    for n in range(NB):
        some = slice(n % group * rows, (n % group + 1) * rows)
        lanes[n // group, some, :] = jnp.broadcast_to(lane[n : n + 1, :], (rows, atoms))
        is_near[n // group, some, :] = jnp.broadcast_to(near[n : n + 1, :], (rows, atoms))


def couple(own, other, lanes, is_near, links, gathered_a, gathered_b, total):
    groups, pairs = links.shape[:2]
    steps = NORB // BLOCKED
    chunk = pairs // steps

    def gather(target, g, step):
        lane, mine = lanes[g], is_near[g] != 0
        for at in range(chunk):
            pair = step * chunk + at
            inner = jnp.take_along_axis(own[eight(pair), :], lane, axis=1, mode="promise_in_bounds")
            outer = jnp.take_along_axis(other[eight(pair), :], lane, axis=1, mode="promise_in_bounds")
            target[pair] = jnp.where(mine, inner, outer)

    def group_sums(g, source, target):
        following = jnp.minimum(g + 1, groups - 1)

        def block_row(step):
            first = step * BLOCKED
            inner = [[None] * NORB for _ in range(BLOCKED)]
            for j in range(NORB):
                left = [links[g, (first + b) * NORB + j] for b in range(BLOCKED)]
                for l in range(NORB):
                    value = source[j * NORB + l]
                    for b in range(BLOCKED):
                        term = left[b] * value
                        inner[b][l] = term if j == 0 else inner[b][l] + term
            for side in range(0, NORB, BROAD):
                at = [
                    (b, (first + b) * NORB + k, k)
                    for k in range(side, side + BROAD)
                    for b in range(BLOCKED)
                ]
                sums = [total[place] for _, place, _ in at]
                for l in range(NORB):
                    right = {k: links[g, k * NORB + l] for k in range(side, side + BROAD)}
                    sums = [x + inner[b][l] * right[k] for x, (b, _, k) in zip(sums, at)]
                for x, (_, place, _) in zip(sums, at):
                    total[place] = x
            gather(target, following, step)

        each(steps, block_row)

    def clear(step):
        for at in range(chunk):
            total[step * chunk + at] = jnp.zeros(total.shape[1:], jnp.float32)
        gather(gathered_a, 0, step)

    def two_groups(half):
        group_sums(half * 2, gathered_a, gathered_b)
        group_sums(half * 2 + 1, gathered_b, gathered_a)

    each(steps, clear)
    each(groups // 2, two_groups)
    if groups % 2:
        group_sums(groups - 1, gathered_a, gathered_b)


def mix_weights(mixing, energies, shifts, coupled, occupied):
    total = mixing.shape[0]
    rows = 2 * energies
    parts = total // rows

    def energy_at(index):
        return standing(index // rows, parts) * energies + index % energies

    lane = lax.broadcasted_iota(jnp.int32, (ROWS, LANES), 1)
    row = lax.broadcasted_iota(jnp.int32, (ROWS, LANES), 0)
    emitted = jnp.zeros((ROWS, LANES), jnp.float32)
    absorbed = jnp.zeros((ROWS, LANES), jnp.float32)
    for mode in range(shifts.shape[0]):
        hit = lane == shifts[mode]
        absorb = coupled[mode] * occupied[mode]
        emit = coupled[mode] * (occupied[mode] + 1.0)
        emitted = emitted + jnp.where(hit, emit, 0.0)
        absorbed = absorbed + jnp.where(hit, absorb, 0.0)
    for at in range(0, total, ROWS):
        for first in range(0, total, LANES):
            width = min(LANES, total - first)
            gap = energy_at(lane + first) - energy_at(row + at)
            far = jnp.minimum(jnp.abs(gap), LANES - 1)
            emit = jnp.take_along_axis(emitted, far, axis=1, mode="promise_in_bounds")
            absorb = jnp.take_along_axis(absorbed, far, axis=1, mode="promise_in_bounds")
            some = slice(first, first + width)
            function = (row + at) % rows // energies
            weight = jnp.where((gap > 0) == (function == 0), emit, absorb)
            weight = jnp.where((lane + first) % rows // energies == function, weight, 0.0)
            mixing[at : at + ROWS, some] = weight[:, :width]


def prep_kernel(*refs):
    free_hbm, retarded_hbm, modes_hbm = refs[0:2], refs[2], refs[3:6]
    offsets_hbm, coupling_hbm = refs[6:8]
    start, left, right, mixing, links, lanes, is_near = refs[8:15]
    free, retarded, shifts, coupled, occupied, offsets, coupling, inside, sems = refs[15:]
    energies, pairs, _ = retarded.shape
    rows = 2 * energies
    group = ROWS // rows
    share = left.shape[0] // ROWS
    moves = list(zip(modes_hbm, (shifts, coupled, occupied))) + [(offsets_hbm, offsets)]
    moves += [(free_hbm[f], free.at[f]) for f in range(2)] + [(retarded_hbm, retarded)]
    moves += [(coupling_hbm.at[n], coupling.at[n]) for n in range(NB)]
    copies = [
        pltpu.make_async_copy(source, target, sems.at[at])
        for at, (source, target) in enumerate(moves)
    ]
    for copy in copies:
        copy.start()

    for copy in copies[:4]:
        copy.wait()
    mix_weights(mixing, energies, shifts, coupled, occupied)
    index_neighbours(rows, offsets, lanes, is_near, inside)
    copies[4].wait()
    copies[5].wait()
    for row in range(ROWS):
        function, energy = row % rows // energies, row % energies
        read = lambda at, size: free[function, energy, at : at + size, :]
        spread_rows(start, 0, row, read, 0, pairs)
    copies[6].wait()
    for row in range(ROWS):
        skipped = row // rows * share
        read = lambda at, size: retarded[row % energies, at : at + size, :]
        spread_rows(left, 0, row, read, skipped, share)
        spread_rows(right, 0, row, read, 0, pairs)
    for n in range(NB):
        copies[7 + n].wait()
        valid = inside[n : n + 1, :]
        for row in range(rows):
            read = lambda at, size: coupling[n, at : at + size, :] * valid
            spread_rows(links, n // group * pairs, n % group * rows + row, read, 0, pairs)


def couple_kernel(rows, own, *refs):
    far, (lanes, is_near, links, out, other, *work) = refs[:-8], refs[-8:]
    pairs = links.shape[1]
    total = work[-1]
    if len(far) == 1:
        for pair in range(pairs):
            value = far[0][pair]
            for at in range(0, ROWS, rows):
                other[pair * ROWS + at : pair * ROWS + at + rows, :] = value
    else:
        energies = rows // len(far)
        for row in range(ROWS):
            source = far[row % rows // energies]
            read = lambda at, size: source[row % energies, at : at + size, :]
            spread_rows(other, 0, row, read, 0, pairs)
    couple(own, other, lanes, is_near, links, *work)
    for pair in range(pairs):
        value = total[pair]
        width = ROWS // 2
        while width >= rows:
            value = value + pltpu.roll(value, width, 0)
            width //= 2
        out[pair] = value[:rows]
    for at in range(pairs, out.shape[0]):
        out[at] = jnp.zeros(out.shape[1:], jnp.float32)


def mix_kernel(mixing, blocks, out, before, after):
    parts, share, rows, atoms = blocks.shape
    for part in range(parts):
        for pair in range(share):
            lanes = slice(pair * atoms, (pair + 1) * atoms)
            before[part * rows : (part + 1) * rows, lanes] = blocks[part, pair]
    after[...] = jnp.dot(
        mixing[...], before[...], precision=TOP_RANK, preferred_element_type=jnp.float32
    )
    for part in range(parts):
        for pair in range(share):
            lanes = slice(pair * atoms, (pair + 1) * atoms)
            out[part, pair] = after[part * rows : (part + 1) * rows, lanes]


def dress(rows, sigma, left, right, copied, keep):
    parts = ROWS // rows
    for pair in range(NORB * NORB):
        value = sigma[pair]
        for part in range(parts):
            copied[pair, part * rows : (part + 1) * rows, :] = value
    for i in range(NORB // parts):
        inner = [None] * NORB
        for j in range(NORB):
            factor = left[i * NORB + j]
            for l in range(NORB):
                term = factor * copied[j * NORB + l]
                inner[l] = term if j == 0 else inner[l] + term
        for k in range(NORB):
            value = inner[0] * right[k * NORB]
            for l in range(1, NORB):
                value = value + inner[l] * right[k * NORB + l]
            keep(i * NORB + k, value)


def dress_between_kernel(rows, sigma, left, right, free, own, compact, copied):
    atoms = sigma.shape[2]
    share = left.shape[0]
    row_at = lax.broadcasted_iota(jnp.int32, (ROWS, atoms), 0)

    def keep(at, value):
        for part in range(ROWS // rows):
            held = (row_at >= part * rows) & (row_at < (part + 1) * rows)
            piece = jnp.where(held, value, 0.0)
            width = ROWS // 2
            while width >= rows:
                piece = piece + pltpu.roll(piece, width, 0)
                width //= 2
            pair = part * share + at
            piece = piece + free[pair * ROWS : (pair + 1) * ROWS, :]
            own[pair * ROWS : (pair + 1) * ROWS, :] = piece
            compact[pair] = piece[:rows]

    dress(rows, sigma, left, right, copied, keep)


def dress_last_kernel(*refs):
    sigma, left, right = refs[:3]
    free, out_hbm = refs[3:5], refs[5:7]
    copied, dressed, out, leaving = refs[7:]
    energies, pairs, _ = free[0].shape
    rows = 2 * energies
    parts = ROWS // rows
    share = left.shape[0]
    stage = 2 * NORB
    copies = []

    def keep(at, value):
        dressed[at * ROWS : (at + 1) * ROWS, :] = value
        if (at + 1) % stage and at + 1 < share:
            return
        done = at // stage * stage
        for row in range(ROWS):
            function, energy, part = row % rows // energies, row % energies, row // rows
            for begin in range(done, at + 1, ROWS):
                size = min(ROWS, at + 1 - begin)
                first = part * share + begin
                piece = dressed[pl.ds(begin * ROWS + row, size, stride=ROWS), :]
                out[function, energy, first : first + size, :] = (
                    free[function][energy, first : first + size, :] + piece
                )
        for function in range(2):
            for part in range(parts):
                some = pl.ds(part * share + done, at + 1 - done)
                copies.append(
                    pltpu.make_async_copy(
                        out.at[function, :, some, :],
                        out_hbm[function].at[:, some, :],
                        leaving.at[len(copies)],
                    )
                )
                copies[-1].start()

    dress(rows, sigma, left, right, copied, keep)
    for copy in copies:
        copy.wait()


def call(kernel, outs, scratch, flops, *operands, spaces=None, targets=None):
    shapes = [
        x if isinstance(x, jax.ShapeDtypeStruct) else jax.ShapeDtypeStruct(x, jnp.float32)
        for x in outs
    ]
    vmem = pl.BlockSpec(memory_space=pltpu.VMEM)
    moved = sum(x.size for x in operands) + sum(x.size for x in shapes)
    return pl.pallas_call(
        kernel,
        out_shape=shapes,
        in_specs=spaces or [vmem] * len(operands),
        out_specs=targets or [vmem] * len(shapes),
        scratch_shapes=scratch,
        compiler_params=PARAMS,
        cost_estimate=pl.CostEstimate(
            flops=flops, bytes_accessed=4 * moved, transcendentals=0
        ),
    )(*operands)


def beside(block):
    count = lax.axis_size("slab")
    if count == 2:
        return lax.ppermute(block, "slab", [(0, 1), (1, 0)])
    forward = [(i, i + 1) for i in range(count - 1)]
    backward = [(target, source) for source, target in forward]
    axis = block.ndim - 1
    atoms = block.shape[axis]
    low = lax.ppermute(lax.slice_in_dim(block, atoms - HW, atoms, axis=axis), "slab", forward)
    high = lax.ppermute(lax.slice_in_dim(block, 0, HW, axis=axis), "slab", backward)
    gap = jnp.zeros(block.shape[:-1] + (atoms - 2 * HW,), block.dtype)
    return jnp.concatenate([high, gap, low], axis=axis)


def body(
    lesser_free,
    greater_free,
    retarded,
    coupling,
    neighbour_offsets,
    phonon_shift,
    phonon_coupling,
    phonon_occupation,
):
    energies, pairs, atoms = lesser_free.shape
    rows = 2 * energies
    groups = NB * rows // ROWS
    parts = lax.axis_size("energy")
    share = -(-pairs // parts)
    total = rows * parts
    away = pl.BlockSpec(memory_space=pltpu.HBM)
    held = lambda *dims: pltpu.VMEM(dims, jnp.float32)
    wide = (pairs * ROWS, atoms)
    deep = (pairs, ROWS, atoms)
    thin = (pairs * rows, atoms)
    every = (parts * share, rows, atoms)
    flops = 4 * NORB * rows * pairs * atoms
    index = jax.ShapeDtypeStruct((groups, ROWS, atoms), jnp.int32)
    transfer = lambda count: pltpu.SemaphoreType.DMA((count,))

    free = (lesser_free, greater_free)
    halos = [beside(g) for g in free]
    phonons = (phonon_shift, phonon_coupling, phonon_occupation)
    constants = (retarded, *phonons, neighbour_offsets, coupling)
    own, left, right, mixing, links, lanes, is_near = call(
        prep_kernel,
        [wide, thin, wide, (total, total), (groups * wide[0], atoms), index, index],
        [held(2, *retarded.shape), held(*retarded.shape)]
        + [pltpu.SMEM(x.shape, x.dtype) for x in phonons]
        + [pltpu.VMEM(neighbour_offsets.shape, jnp.int32)]
        + [held(*coupling.shape), held(NB, atoms), transfer(7 + NB)],
        rows * coupling.size,
        *(pltpu.with_memory_space_constraint(x, pltpu.HBM) for x in (*free, *constants)),
        spaces=[away] * 8,
    )
    links = links.reshape(groups, pairs, ROWS, atoms)
    start = own
    left = left.reshape(pairs * rows // ROWS, ROWS, atoms)
    right = right.reshape(deep)

    for step in range(ITERS):
        if step > 0:
            own, compact = call(
                functools.partial(dress_between_kernel, rows),
                [wide, (pairs, rows, atoms)],
                [held(*deep)],
                flops,
                sigma,
                left,
                right,
                start,
            )
            halos = [beside(compact)]
        (coupled,) = call(
            functools.partial(couple_kernel, rows),
            [every],
            [held(*wide)] + [held(*deep)] * 3,
            NB * flops,
            own,
            *halos,
            lanes,
            is_near,
            links,
        )
        gathered = exchanged(coupled.reshape(parts, share, rows, atoms))
        (mixed,) = call(
            mix_kernel,
            [gathered.shape],
            [held(total, share * atoms)] * 2,
            2 * total * gathered.size,
            mixing,
            gathered,
        )
        sigma = exchanged(mixed).reshape(every)
    stages = -(-thin[0] // (ROWS * 2 * NORB))
    return call(
        dress_last_kernel,
        [lesser_free.shape] * 2,
        [held(*deep), held(*thin), held(2, *lesser_free.shape)]
        + [transfer(stages * 2 * ROWS // rows)],
        flops,
        sigma,
        left,
        right,
        *free,
        targets=[away] * 2,
    )


def solution(mesh):
    placed = (
        P("energy", None, "slab"),
        P("energy", None, "slab"),
        P("energy", None, "slab"),
        P(None, None, "slab"),
        P(None, "slab"),
        P(),
        P(),
        P(),
    )
    return jax.shard_map(
        body,
        mesh=mesh,
        in_specs=placed,
        out_specs=(P("energy", None, "slab"), P("energy", None, "slab")),
        check_vma=False,
    )
```

```python
import functools
import math

import jax
import jax.numpy as jnp
from jax import lax
from jax.experimental import pallas as pl
from jax.experimental.pallas import tpu as pltpu
from jax.sharding import PartitionSpec as P

NORB = 12
NB = 12
HW = 32
ITERS = 2
ROWS = 8
LANES = 128
BLOCKED = 2
BROAD = 6

TOP_RANK = lax.Precision.HIGHEST
PARAMS = pltpu.CompilerParams(vmem_limit_bytes=24 * 1024 * 1024)


def each(count, step):
    lax.fori_loop(0, count, lambda at, _: step(at), None)


def eight(at):
    return pl.ds(pl.multiple_of(at * ROWS, ROWS), ROWS)


def spread_rows(target, base, row, source, first, count):
    for at in range(0, count, ROWS):
        size = min(ROWS, count - at)
        rows = pl.ds((base + at) * ROWS + row, size, stride=ROWS)
        target[rows, :] = source(first + at, size)


def standing(place, parts, even):
    root = math.isqrt(parts)
    root = root if parts % root == 0 else 1
    place = place + even * (parts - 1 - 2 * place)
    return place % root * (parts // root) + place // root


def exchanged(shares):
    parts, slabs = lax.axis_size("energy"), lax.axis_size("slab")
    groups = [
        [standing(place, parts, 1 - slab % 2) * slabs + slab for place in range(parts)]
        for slab in range(slabs)
    ]
    return lax.all_to_all(shares, ("energy", "slab"), 0, 0, axis_index_groups=groups)


def index_neighbours(rows, offsets, lanes, is_near, inside):
    atoms = offsets.shape[1]
    group = ROWS // rows
    slab, slabs = lax.axis_index("slab"), lax.axis_size("slab")
    targets = offsets[...] + lax.broadcasted_iota(jnp.int32, (NB, atoms), 1)
    placed = targets + slab * atoms
    inside[...] = ((placed >= 0) & (placed < slabs * atoms)).astype(jnp.float32)
    near = ((targets >= 0) & (targets < atoms)).astype(jnp.int32)
    lane = jnp.where(targets < 0, targets + atoms, targets)
    lane = jnp.where(lane >= atoms, lane - atoms, lane)
    for n in range(NB):
        some = slice(n % group * rows, (n % group + 1) * rows)
        lanes[n // group, some, :] = jnp.broadcast_to(lane[n : n + 1, :], (rows, atoms))
        is_near[n // group, some, :] = jnp.broadcast_to(near[n : n + 1, :], (rows, atoms))


def couple(own, other, lanes, is_near, links, gathered_a, gathered_b, total):
    groups, pairs = links.shape[:2]
    steps = NORB // BLOCKED
    chunk = pairs // steps

    def gather(target, g, step):
        lane, mine = lanes[g], is_near[g] != 0
        for at in range(chunk):
            pair = step * chunk + at
            inner = jnp.take_along_axis(own[eight(pair), :], lane, axis=1, mode="promise_in_bounds")
            outer = jnp.take_along_axis(other[eight(pair), :], lane, axis=1, mode="promise_in_bounds")
            target[pair] = jnp.where(mine, inner, outer)

    def group_sums(g, source, target):
        following = jnp.minimum(g + 1, groups - 1)

        def block_row(step):
            first = step * BLOCKED
            inner = [[None] * NORB for _ in range(BLOCKED)]
            for j in range(NORB):
                left = [links[g, (first + b) * NORB + j] for b in range(BLOCKED)]
                for l in range(NORB):
                    value = source[j * NORB + l]
                    for b in range(BLOCKED):
                        term = left[b] * value
                        inner[b][l] = term if j == 0 else inner[b][l] + term
            for side in range(0, NORB, BROAD):
                at = [
                    (b, (first + b) * NORB + k, k)
                    for k in range(side, side + BROAD)
                    for b in range(BLOCKED)
                ]
                sums = [total[place] for _, place, _ in at]
                for l in range(NORB):
                    right = {k: links[g, k * NORB + l] for k in range(side, side + BROAD)}
                    sums = [x + inner[b][l] * right[k] for x, (b, _, k) in zip(sums, at)]
                for x, (_, place, _) in zip(sums, at):
                    total[place] = x
            gather(target, following, step)

        each(steps, block_row)

    def clear(step):
        for at in range(chunk):
            total[step * chunk + at] = jnp.zeros(total.shape[1:], jnp.float32)
        gather(gathered_a, 0, step)

    def two_groups(half):
        group_sums(half * 2, gathered_a, gathered_b)
        group_sums(half * 2 + 1, gathered_b, gathered_a)

    each(steps, clear)
    each(groups // 2, two_groups)
    if groups % 2:
        group_sums(groups - 1, gathered_a, gathered_b)


def mix_weights(mixing, energies, shifts, coupled, occupied):
    total = mixing.shape[0]
    rows = 2 * energies
    parts, even = total // rows, 1 - lax.axis_index("slab") % 2

    def energy_at(index):
        return standing(index // rows, parts, even) * energies + index % energies

    lane = lax.broadcasted_iota(jnp.int32, (ROWS, LANES), 1)
    row = lax.broadcasted_iota(jnp.int32, (ROWS, LANES), 0)
    emitted = jnp.zeros((ROWS, LANES), jnp.float32)
    absorbed = jnp.zeros((ROWS, LANES), jnp.float32)
    for mode in range(shifts.shape[0]):
        hit = lane == shifts[mode]
        absorb = coupled[mode] * occupied[mode]
        emit = coupled[mode] * (occupied[mode] + 1.0)
        emitted = emitted + jnp.where(hit, emit, 0.0)
        absorbed = absorbed + jnp.where(hit, absorb, 0.0)
    for at in range(0, total, ROWS):
        for first in range(0, total, LANES):
            width = min(LANES, total - first)
            gap = energy_at(lane + first) - energy_at(row + at)
            far = jnp.minimum(jnp.abs(gap), LANES - 1)
            emit = jnp.take_along_axis(emitted, far, axis=1, mode="promise_in_bounds")
            absorb = jnp.take_along_axis(absorbed, far, axis=1, mode="promise_in_bounds")
            some = slice(first, first + width)
            function = (row + at) % rows // energies
            weight = jnp.where((gap > 0) == (function == 0), emit, absorb)
            weight = jnp.where((lane + first) % rows // energies == function, weight, 0.0)
            mixing[at : at + ROWS, some] = weight[:, :width]


def prep_kernel(*refs):
    free_hbm, retarded_hbm, modes_hbm = refs[0:2], refs[2], refs[3:6]
    offsets_hbm, coupling_hbm = refs[6:8]
    start, left, right, mixing, links, lanes, is_near = refs[8:15]
    free, retarded, shifts, coupled, occupied, offsets, coupling, inside, sems = refs[15:]
    energies, pairs, _ = retarded.shape
    rows = 2 * energies
    group = ROWS // rows
    share = left.shape[0] // ROWS
    moves = list(zip(modes_hbm, (shifts, coupled, occupied))) + [(offsets_hbm, offsets)]
    moves += [(free_hbm[f], free.at[f]) for f in range(2)] + [(retarded_hbm, retarded)]
    moves += [(coupling_hbm.at[n], coupling.at[n]) for n in range(NB)]
    copies = [
        pltpu.make_async_copy(source, target, sems.at[at])
        for at, (source, target) in enumerate(moves)
    ]
    for copy in copies:
        copy.start()

    for copy in copies[:4]:
        copy.wait()
    mix_weights(mixing, energies, shifts, coupled, occupied)
    index_neighbours(rows, offsets, lanes, is_near, inside)
    copies[4].wait()
    copies[5].wait()
    for row in range(ROWS):
        function, energy = row % rows // energies, row % energies
        read = lambda at, size: free[function, energy, at : at + size, :]
        spread_rows(start, 0, row, read, 0, pairs)
    copies[6].wait()
    for row in range(ROWS):
        skipped = row // rows * share
        read = lambda at, size: retarded[row % energies, at : at + size, :]
        spread_rows(left, 0, row, read, skipped, share)
        spread_rows(right, 0, row, read, 0, pairs)
    for n in range(NB):
        copies[7 + n].wait()
        valid = inside[n : n + 1, :]
        for row in range(rows):
            read = lambda at, size: coupling[n, at : at + size, :] * valid
            spread_rows(links, n // group * pairs, n % group * rows + row, read, 0, pairs)


def couple_kernel(rows, own, *refs):
    far, (lanes, is_near, links, out, other, *work) = refs[:-8], refs[-8:]
    pairs = links.shape[1]
    total = work[-1]
    if len(far) == 1:
        for pair in range(pairs):
            value = far[0][pair]
            for at in range(0, ROWS, rows):
                other[pair * ROWS + at : pair * ROWS + at + rows, :] = value
    else:
        energies = rows // len(far)
        for row in range(ROWS):
            source = far[row % rows // energies]
            read = lambda at, size: source[row % energies, at : at + size, :]
            spread_rows(other, 0, row, read, 0, pairs)
    couple(own, other, lanes, is_near, links, *work)
    for pair in range(pairs):
        value = total[pair]
        width = ROWS // 2
        while width >= rows:
            value = value + pltpu.roll(value, width, 0)
            width //= 2
        out[pair] = value[:rows]
    for at in range(pairs, out.shape[0]):
        out[at] = jnp.zeros(out.shape[1:], jnp.float32)


def mix_kernel(mixing, blocks, out, before, after):
    parts, share, rows, atoms = blocks.shape
    for part in range(parts):
        for pair in range(share):
            lanes = slice(pair * atoms, (pair + 1) * atoms)
            before[part * rows : (part + 1) * rows, lanes] = blocks[part, pair]
    after[...] = jnp.dot(
        mixing[...], before[...], precision=TOP_RANK, preferred_element_type=jnp.float32
    )
    for part in range(parts):
        for pair in range(share):
            lanes = slice(pair * atoms, (pair + 1) * atoms)
            out[part, pair] = after[part * rows : (part + 1) * rows, lanes]


def dress(rows, sigma, left, right, copied, keep):
    parts = ROWS // rows
    for pair in range(NORB * NORB):
        value = sigma[pair]
        for part in range(parts):
            copied[pair, part * rows : (part + 1) * rows, :] = value
    for i in range(NORB // parts):
        inner = [None] * NORB
        for j in range(NORB):
            factor = left[i * NORB + j]
            for l in range(NORB):
                term = factor * copied[j * NORB + l]
                inner[l] = term if j == 0 else inner[l] + term
        for k in range(NORB):
            value = inner[0] * right[k * NORB]
            for l in range(1, NORB):
                value = value + inner[l] * right[k * NORB + l]
            keep(i * NORB + k, value)


def dress_between_kernel(rows, sigma, left, right, free, own, compact, copied):
    atoms = sigma.shape[2]
    share = left.shape[0]
    row_at = lax.broadcasted_iota(jnp.int32, (ROWS, atoms), 0)

    def keep(at, value):
        for part in range(ROWS // rows):
            held = (row_at >= part * rows) & (row_at < (part + 1) * rows)
            piece = jnp.where(held, value, 0.0)
            width = ROWS // 2
            while width >= rows:
                piece = piece + pltpu.roll(piece, width, 0)
                width //= 2
            pair = part * share + at
            piece = piece + free[pair * ROWS : (pair + 1) * ROWS, :]
            own[pair * ROWS : (pair + 1) * ROWS, :] = piece
            compact[pair] = piece[:rows]

    dress(rows, sigma, left, right, copied, keep)


def dress_last_kernel(*refs):
    sigma, left, right = refs[:3]
    free, out_hbm = refs[3:5], refs[5:7]
    copied, dressed, out, leaving = refs[7:]
    energies, pairs, _ = free[0].shape
    rows = 2 * energies
    parts = ROWS // rows
    share = left.shape[0]
    stage = 2 * NORB
    copies = []

    def keep(at, value):
        dressed[at * ROWS : (at + 1) * ROWS, :] = value
        if (at + 1) % stage and at + 1 < share:
            return
        done = at // stage * stage
        for row in range(ROWS):
            function, energy, part = row % rows // energies, row % energies, row // rows
            for begin in range(done, at + 1, ROWS):
                size = min(ROWS, at + 1 - begin)
                first = part * share + begin
                piece = dressed[pl.ds(begin * ROWS + row, size, stride=ROWS), :]
                out[function, energy, first : first + size, :] = (
                    free[function][energy, first : first + size, :] + piece
                )
        for function in range(2):
            for part in range(parts):
                some = pl.ds(part * share + done, at + 1 - done)
                copies.append(
                    pltpu.make_async_copy(
                        out.at[function, :, some, :],
                        out_hbm[function].at[:, some, :],
                        leaving.at[len(copies)],
                    )
                )
                copies[-1].start()

    dress(rows, sigma, left, right, copied, keep)
    for copy in copies:
        copy.wait()


def call(kernel, outs, scratch, flops, *operands, spaces=None, targets=None):
    shapes = [
        x if isinstance(x, jax.ShapeDtypeStruct) else jax.ShapeDtypeStruct(x, jnp.float32)
        for x in outs
    ]
    vmem = pl.BlockSpec(memory_space=pltpu.VMEM)
    moved = sum(x.size for x in operands) + sum(x.size for x in shapes)
    return pl.pallas_call(
        kernel,
        out_shape=shapes,
        in_specs=spaces or [vmem] * len(operands),
        out_specs=targets or [vmem] * len(shapes),
        scratch_shapes=scratch,
        compiler_params=PARAMS,
        cost_estimate=pl.CostEstimate(
            flops=flops, bytes_accessed=4 * moved, transcendentals=0
        ),
    )(*operands)


def beside(block):
    count = lax.axis_size("slab")
    if count == 2:
        return lax.ppermute(block, "slab", [(0, 1), (1, 0)])
    forward = [(i, i + 1) for i in range(count - 1)]
    backward = [(target, source) for source, target in forward]
    axis = block.ndim - 1
    atoms = block.shape[axis]
    low = lax.ppermute(lax.slice_in_dim(block, atoms - HW, atoms, axis=axis), "slab", forward)
    high = lax.ppermute(lax.slice_in_dim(block, 0, HW, axis=axis), "slab", backward)
    gap = jnp.zeros(block.shape[:-1] + (atoms - 2 * HW,), block.dtype)
    return jnp.concatenate([high, gap, low], axis=axis)


def body(
    lesser_free,
    greater_free,
    retarded,
    coupling,
    neighbour_offsets,
    phonon_shift,
    phonon_coupling,
    phonon_occupation,
):
    energies, pairs, atoms = lesser_free.shape
    rows = 2 * energies
    groups = NB * rows // ROWS
    parts = lax.axis_size("energy")
    share = -(-pairs // parts)
    total = rows * parts
    away = pl.BlockSpec(memory_space=pltpu.HBM)
    held = lambda *dims: pltpu.VMEM(dims, jnp.float32)
    wide = (pairs * ROWS, atoms)
    deep = (pairs, ROWS, atoms)
    thin = (pairs * rows, atoms)
    every = (parts * share, rows, atoms)
    flops = 4 * NORB * rows * pairs * atoms
    index = jax.ShapeDtypeStruct((groups, ROWS, atoms), jnp.int32)
    transfer = lambda count: pltpu.SemaphoreType.DMA((count,))

    free = (lesser_free, greater_free)
    halos = [beside(g) for g in free]
    phonons = (phonon_shift, phonon_coupling, phonon_occupation)
    constants = (retarded, *phonons, neighbour_offsets, coupling)
    own, left, right, mixing, links, lanes, is_near = call(
        prep_kernel,
        [wide, thin, wide, (total, total), (groups * wide[0], atoms), index, index],
        [held(2, *retarded.shape), held(*retarded.shape)]
        + [pltpu.SMEM(x.shape, x.dtype) for x in phonons]
        + [pltpu.VMEM(neighbour_offsets.shape, jnp.int32)]
        + [held(*coupling.shape), held(NB, atoms), transfer(7 + NB)],
        rows * coupling.size,
        *(pltpu.with_memory_space_constraint(x, pltpu.HBM) for x in (*free, *constants)),
        spaces=[away] * 8,
    )
    links = links.reshape(groups, pairs, ROWS, atoms)
    start = own
    left = left.reshape(pairs * rows // ROWS, ROWS, atoms)
    right = right.reshape(deep)

    for step in range(ITERS):
        if step > 0:
            own, compact = call(
                functools.partial(dress_between_kernel, rows),
                [wide, (pairs, rows, atoms)],
                [held(*deep)],
                flops,
                sigma,
                left,
                right,
                start,
            )
            halos = [beside(compact)]
        (coupled,) = call(
            functools.partial(couple_kernel, rows),
            [every],
            [held(*wide)] + [held(*deep)] * 3,
            NB * flops,
            own,
            *halos,
            lanes,
            is_near,
            links,
        )
        gathered = exchanged(coupled.reshape(parts, share, rows, atoms))
        (mixed,) = call(
            mix_kernel,
            [gathered.shape],
            [held(total, share * atoms)] * 2,
            2 * total * gathered.size,
            mixing,
            gathered,
        )
        sigma = exchanged(mixed).reshape(every)
    stages = -(-thin[0] // (ROWS * 2 * NORB))
    return call(
        dress_last_kernel,
        [lesser_free.shape] * 2,
        [held(*deep), held(*thin), held(2, *lesser_free.shape)]
        + [transfer(stages * 2 * ROWS // rows)],
        flops,
        sigma,
        left,
        right,
        *free,
        targets=[away] * 2,
    )


def solution(mesh):
    placed = (
        P("energy", None, "slab"),
        P("energy", None, "slab"),
        P("energy", None, "slab"),
        P(None, None, "slab"),
        P(None, "slab"),
        P(),
        P(),
        P(),
    )
    return jax.shard_map(
        body,
        mesh=mesh,
        in_specs=placed,
        out_specs=(P("energy", None, "slab"), P("energy", None, "slab")),
        check_vma=False,
    )
```
